32 devices in a mesh: clu: 16 (over z, y, x), grp: 2 (over core).
Axes of the slice: x: 2, y: 2, z: 4, core: 2. Of those that a mesh axis runs over, the one named last changes fastest.
Arguments:
- embeddings: bfloat16 [4096, 512], P(('clu', 'grp')), may hold values from -60 to 60
- cluster_id: int32 [4096], P(('clu', 'grp')), may hold values from 0 to 63, as said below
- cluster_group: int32 [64], replicated, may hold values from 0 to 15, as said below
Outputs:
- best_similarity: float32 [4096], P(('clu', 'grp'))
The draws below stay inside these ranges and needn't reach their ends.
Inputs may be any that keep to these rules, and one draw needn't show every extreme that they name: `cluster_id`: on every device's rows, at most 32 rows belong to clusters of one group, and exactly 32 for some group. `cluster_group`: every group is named by exactly 4 clusters.
All inputs are finite; a program needn't handle non-finite values.
Results may differ from the reference program's by a relative error of at most 0.0015.
Values may be sent and summed in bfloat16 or wider, within the bound.
No kernel may reach another device: no remote copies, remote signals or barrier semaphores. Data moves between devices by JAX's collectives and lax.ppermute only.
A program may use at most 64 MiB of HBM per device.

```python
import jax
import jax.numpy as jnp
from jax import lax

D = 512
ROWS_DEV = 128
K_G = 4
GROUP_ROW_LIMIT = 32
CLUSTERS = 64
ROWS = 4096
N_CLU = 16
N_GRP = 2


def routing(key):
    group_table = CLUSTERS // K_G
    device_list = ROWS // ROWS_DEV
    slot_total = group_table * GROUP_ROW_LIMIT
    perm = jax.random.permutation(jax.random.fold_in(key, 11), CLUSTERS).astype(jnp.int32)
    group_of = perm // K_G
    inverse = jnp.zeros((CLUSTERS,), jnp.int32).at[perm].set(jnp.arange(CLUSTERS, dtype=jnp.int32))
    load_pressure = jax.random.randint(jax.random.fold_in(key, 12), (group_table,), 0, 2 ** 14)
    random_jitter = jax.random.randint(jax.random.fold_in(key, 13), (device_list, slot_total), 0, 2 ** 14)
    pinned_choice = jax.random.randint(jax.random.fold_in(key, 14), (device_list,), 0, group_table)
    slot_owner_group = jnp.arange(slot_total, dtype=jnp.int32) // GROUP_ROW_LIMIT
    reward_term = jnp.where(slot_owner_group[None, :] == pinned_choice[:, None], 2 ** 17, 0)
    fitness_value = (random_jitter + load_pressure[slot_owner_group][None, :] + reward_term) * slot_total + jnp.arange(slot_total, dtype=jnp.int32)[None, :]
    _, chosen = lax.top_k(fitness_value, ROWS_DEV)
    shuffle = jax.random.permutation(jax.random.fold_in(key, 15), ROWS_DEV).astype(jnp.int32)
    chosen = chosen[:, shuffle]
    dest = chosen // GROUP_ROW_LIMIT
    first = jax.random.randint(jax.random.fold_in(key, 16), (device_list, ROWS_DEV), 0, K_G)
    second = jax.random.randint(jax.random.fold_in(key, 17), (device_list, ROWS_DEV), 0, K_G)
    sub = jnp.minimum(first, second)
    cluster = inverse[dest * K_G + sub]
    return (group_of.astype(jnp.int32), cluster.reshape(ROWS).astype(jnp.int32))


def draw_cluster_id(key, part):
    return routing(key)[1]


def draw_cluster_group(key, part):
    return routing(key)[0]


def draw_embeddings(key, part):
    entries = jnp.clip(jax.random.normal(jax.random.fold_in(key, 24), (ROWS, D), jnp.float32), -6.0, 6.0)
    scales = jnp.exp(jax.random.uniform(jax.random.fold_in(key, 25), (ROWS, 1), jnp.float32, 0.0, 2.3))
    values = entries * scales
    return values.astype(jnp.bfloat16)


def setup_inputs(seed: int = 0) -> dict:
    streams_of = jax.random.split(jax.random.key(seed), 4)
    embeddings = draw_embeddings(jax.random.fold_in(streams_of[3], 71), 0)
    cluster_id = draw_cluster_id(jax.random.fold_in(streams_of[3], 71), 0)
    cluster_group = draw_cluster_group(jax.random.fold_in(streams_of[3], 71), 0)
    return dict(embeddings=embeddings, cluster_id=cluster_id, cluster_group=cluster_group)


def normalize(embeddings):
    values = embeddings.astype(jnp.float32)
    scale = lax.rsqrt(lax.optimization_barrier(jnp.sum(values * values, axis=-1, keepdims=True)) + 1e-06)
    return (values * scale).astype(jnp.bfloat16)

def reference(embeddings, cluster_id, cluster_group):
    unit = normalize(embeddings)
    dest = cluster_group[cluster_id].astype(jnp.int32)
    index = jnp.arange(ROWS, dtype=jnp.int32)
    device = index // ROWS_DEV
    local = index % ROWS_DEV
    rank = device % N_GRP * (N_CLU * ROWS_DEV) + device // N_GRP * ROWS_DEV + local
    order = jnp.argsort(dest * ROWS + rank).astype(jnp.int32)
    window = N_GRP * N_CLU * GROUP_ROW_LIMIT
    sorted_units = jnp.concatenate([jnp.zeros((window, D), jnp.float32), unit[order].astype(jnp.float32)], axis=0)
    sorted_clusters = jnp.concatenate([jnp.full((window,), -1, jnp.int32), cluster_id[order].astype(jnp.int32)], axis=0)
    sorted_groups = jnp.concatenate([jnp.full((window,), -1, jnp.int32), dest[order].astype(jnp.int32)], axis=0)
    width_q = 512

    def one_block(start):
        queries = lax.dynamic_slice_in_dim(sorted_units, start + window, width_q, 0)
        query_cl = lax.dynamic_slice_in_dim(sorted_clusters, start + window, width_q, 0)
        query_gr = lax.dynamic_slice_in_dim(sorted_groups, start + window, width_q, 0)
        keys = lax.dynamic_slice_in_dim(sorted_units, start, window + width_q, 0)
        key_cl = lax.dynamic_slice_in_dim(sorted_clusters, start, window + width_q, 0)
        key_gr = lax.dynamic_slice_in_dim(sorted_groups, start, window + width_q, 0)
        sims = jnp.dot(queries, keys.T, precision=lax.Precision.HIGHEST)
        score = jnp.where(query_cl[:, None] == key_cl[None, :], sims, 0.5 * sims)
        query_pos = jnp.arange(width_q, dtype=jnp.int32) + window
        key_pos = jnp.arange(window + width_q, dtype=jnp.int32)
        mask = (query_gr[:, None] == key_gr[None, :]) & (key_pos[None, :] < query_pos[:, None])
        return lax.optimization_barrier(jnp.max(jnp.where(mask, score, -1.0), axis=1))
    starts = jnp.arange(ROWS // width_q, dtype=jnp.int32) * width_q
    best = lax.map(one_block, starts).reshape(ROWS)
    return jnp.zeros((ROWS,), best.dtype).at[order].set(best)
```

```python
import functools

import jax
import jax.numpy as jnp
from jax import lax
from jax.experimental import pallas as pl
from jax.experimental.pallas import tpu as pltpu
from jax.sharding import PartitionSpec as P

AUX = 16
CHUNK = 4
DIGIT = 256


def pack_kernel(emb_ref, id_ref, out_ref):
    rows, width = emb_ref.shape
    values = emb_ref[...].astype(jnp.float32)
    scale = lax.rsqrt(jnp.sum(values * values, axis=-1, keepdims=True) + 1e-06)
    out_ref[:rows, :] = (values * scale).astype(jnp.bfloat16)
    ids = jnp.broadcast_to(id_ref[...], (AUX, rows))
    row = lax.broadcasted_iota(jnp.int32, (AUX, rows), 0)
    digits = jnp.where(row == 0, ids % DIGIT, ids // DIGIT)
    if width > rows:
        digits = jnp.concatenate([digits, jnp.zeros((AUX, width - rows), jnp.int32)], axis=1)
    out_ref[rows:, :] = digits.astype(jnp.float32).astype(jnp.bfloat16)


def pack(embeddings, cluster_id):
    rows, width = embeddings.shape
    return pl.pallas_call(
        pack_kernel,
        out_shape=jax.ShapeDtypeStruct((rows + AUX, width), jnp.bfloat16),
    )(embeddings, cluster_id.reshape(1, rows))


def one_hot(digits, clusters):
    number = digits[0:1].astype(jnp.int32) + DIGIT * digits[1:2].astype(jnp.int32)
    index = lax.broadcasted_iota(jnp.int32, (clusters, digits.shape[1]), 0)
    return jnp.where(index == number, 1.0, 0.0).astype(jnp.bfloat16)


def weights_table(group_ref, groups):
    clusters = group_ref.shape[1]
    index = lax.broadcasted_iota(jnp.int32, (groups, clusters), 0)
    member = jnp.where(index == group_ref[...], 1.0, 0.0).astype(jnp.bfloat16)
    same = lax.dot_general(member, member, (((0,), (0,)), ((), ())), preferred_element_type=jnp.float32)
    a = lax.broadcasted_iota(jnp.int32, (clusters, clusters), 0)
    b = lax.broadcasted_iota(jnp.int32, (clusters, clusters), 1)
    return jnp.where(a == b, 1.0, 0.5 * same).astype(jnp.bfloat16)


def best_kernel(n_grp, rows, groups, place_ref, all_ref, own_ref, group_ref, out_ref):
    blocks = all_ref.shape[0]
    clusters = group_ref.shape[1]
    n_clu = blocks // n_grp
    base = place_ref[0]
    table = weights_table(group_ref, groups)
    queries = own_ref[:rows, :]
    own_hot = one_hot(own_ref[rows:, :rows].astype(jnp.float32), clusters)
    mixed = jnp.dot(table, own_hot, preferred_element_type=jnp.float32).astype(jnp.bfloat16)
    chunk = min(CHUNK, blocks)
    best = jnp.full((1, rows), -1.0, jnp.float32)
    for first in range(0, blocks, chunk):
        keys = all_ref[first : first + chunk, :rows, :].reshape(chunk * rows, -1)
        hot = jnp.concatenate(
            [one_hot(all_ref[d, rows:, :rows].astype(jnp.float32), clusters) for d in range(first, first + chunk)],
            axis=1,
        )
        weight = lax.dot_general(hot, mixed, (((0,), (0,)), ((), ())), preferred_element_type=jnp.float32)
        sims = lax.dot_general(keys, queries, (((1,), (1,)), ((), ())), preferred_element_type=jnp.float32)
        local = lax.broadcasted_iota(jnp.int32, (rows, rows), 0)
        mine = lax.broadcasted_iota(jnp.int32, (rows, rows), 1) + base
        order = jnp.concatenate(
            [local + ((d % n_grp) * n_clu + d // n_grp) * rows - mine for d in range(first, first + chunk)], axis=0
        )
        score = jnp.where((weight > 0) & (order < 0), weight * sims, -1.0)
        best = jnp.maximum(best, jnp.max(score, axis=0, keepdims=True))
    out_ref[...] = best


def gathered(n_grp, embeddings, cluster_id, cluster_group):
    rows, width = embeddings.shape
    n_clu = lax.axis_size("clu")
    own = pack(embeddings, cluster_id)
    every = lax.all_gather(own, ("clu", "grp"), axis=0)
    base = (lax.axis_index("grp") * n_clu + lax.axis_index("clu")) * rows
    vmem = pl.BlockSpec(memory_space=pltpu.VMEM)
    best = pl.pallas_call(
        functools.partial(best_kernel, n_grp, rows, n_clu),
        out_shape=jax.ShapeDtypeStruct((1, rows), jnp.float32),
        in_specs=[pl.BlockSpec(memory_space=pltpu.SMEM), vmem, vmem, vmem],
        out_specs=vmem,
        compiler_params=pltpu.CompilerParams(vmem_limit_bytes=40 * 2**20),
    )(base.reshape(1).astype(jnp.int32), every, own, cluster_group.reshape(1, -1))
    return best.reshape(rows)


def normalize(embeddings):
    values = embeddings.astype(jnp.float32)
    scale = lax.rsqrt(jnp.sum(values * values, axis=-1, keepdims=True) + 1e-06)
    return (values * scale).astype(jnp.bfloat16)


def tile_max(best, queries, query_cl, query_pos, keys, key_cl, key_pos):
    sims = lax.dot_general(
        queries, keys, (((1,), (1,)), ((), ())), preferred_element_type=jnp.float32
    )
    score = jnp.where(query_cl[:, None] == key_cl[None, :], sims, 0.5 * sims)
    mask = (key_cl[None, :] >= 0) & (key_pos[None, :] < query_pos[:, None])
    return jnp.maximum(best, jnp.max(jnp.where(mask, score, -1.0), axis=1))


def routed(embeddings, cluster_id, cluster_group):
    rows, width = embeddings.shape
    n_clu = lax.axis_size("clu")
    slots = 4 * rows // n_clu
    block = slots * n_clu
    clusters = cluster_group.shape[0]
    unit = normalize(embeddings)
    table = cluster_id[:, None] == jnp.arange(clusters, dtype=jnp.int32)[None, :]
    dest = jnp.sum(jnp.where(table, cluster_group[None, :], 0), axis=1)
    dest_hot = (dest[:, None] == jnp.arange(n_clu, dtype=jnp.int32)[None, :]).astype(jnp.int32)
    position = jnp.sum(jnp.cumsum(dest_hot, axis=0) * dest_hot, axis=1) - 1
    send_units = jnp.zeros((n_clu, slots, width), jnp.bfloat16).at[dest, position].set(unit)
    send_clusters = jnp.full((n_clu, slots), -1, jnp.int32).at[dest, position].set(cluster_id)
    recv_units, recv_clusters = (
        lax.all_to_all(send_units, "clu", split_axis=0, concat_axis=0, tiled=True),
        lax.all_to_all(send_clusters, "clu", split_axis=0, concat_axis=0, tiled=True),
    )
    queries = recv_units.reshape(block, width)
    query_cl = recv_clusters.reshape(block)
    mine = lax.axis_index("grp")
    query_pos = mine * block + jnp.arange(block, dtype=jnp.int32)
    initial = jnp.full((block,), -1.0, jnp.float32)
    keys = lax.all_gather(queries, "grp", axis=0, tiled=True)
    key_cl = lax.all_gather(query_cl, "grp", axis=0, tiled=True)
    key_pos = jnp.arange(keys.shape[0], dtype=jnp.int32)
    best = tile_max(initial, queries, query_cl, query_pos, keys, key_cl, key_pos)
    returned = lax.all_to_all(
        best.reshape(n_clu, slots), "clu", split_axis=0, concat_axis=0, tiled=True
    )
    return returned[dest, position]


def solution(mesh):
    n_grp = mesh.shape["grp"]
    devices = n_grp * mesh.shape["clu"]

    def shards(embeddings, cluster_id, cluster_group):
        rows, width = embeddings.shape
        if devices * (rows + AUX) * width * 2 > 16 * 2**20:
            return routed(embeddings, cluster_id, cluster_group)
        return gathered(n_grp, embeddings, cluster_id, cluster_group)

    placed = (P(("clu", "grp"), None), P(("clu", "grp")), P())
    return jax.shard_map(
        shards, mesh=mesh, in_specs=placed, out_specs=P(("clu", "grp")), check_vma=False
    )
```

```python
import functools
import math

import jax
import jax.numpy as jnp
from jax import lax
from jax.experimental import pallas as pl
from jax.experimental.pallas import tpu as pltpu
from jax.sharding import PartitionSpec as P

AUX = 16
DIGIT = 256


def pack_kernel(emb_ref, id_ref, out_ref):
    rows, width = emb_ref.shape
    values = emb_ref[...].astype(jnp.float32)
    scale = lax.rsqrt(jnp.sum(values * values, axis=-1, keepdims=True) + 1e-06)
    out_ref[:rows, :] = (values * scale).astype(jnp.bfloat16)
    ids = jnp.broadcast_to(id_ref[...], (AUX, rows))
    row = lax.broadcasted_iota(jnp.int32, (AUX, rows), 0)
    digits = jnp.where(row == 0, ids % DIGIT, jnp.where(row == 1, ids // DIGIT, 1))
    if width > rows:
        digits = jnp.concatenate([digits, jnp.zeros((AUX, width - rows), jnp.int32)], axis=1)
    out_ref[rows:, :] = digits.astype(jnp.float32).astype(jnp.bfloat16)


def pack(embeddings, cluster_id):
    rows, width = embeddings.shape
    return pl.pallas_call(
        pack_kernel,
        out_shape=jax.ShapeDtypeStruct((rows + AUX, width), jnp.bfloat16),
    )(embeddings, cluster_id.reshape(1, rows))


def one_hot(digits, clusters):
    number = digits[0:1].astype(jnp.int32) + DIGIT * digits[1:2].astype(jnp.int32)
    index = lax.broadcasted_iota(jnp.int32, (clusters, digits.shape[1]), 0)
    return jnp.where((index == number) & (digits[2:3] > 0), 1.0, 0.0).astype(jnp.bfloat16)


def weights_table(group_ref, groups):
    clusters = group_ref.shape[1]
    index = lax.broadcasted_iota(jnp.int32, (groups, clusters), 0)
    member = jnp.where(index == group_ref[...], 1.0, 0.0).astype(jnp.bfloat16)
    same = lax.dot_general(member, member, (((0,), (0,)), ((), ())), preferred_element_type=jnp.float32)
    a = lax.broadcasted_iota(jnp.int32, (clusters, clusters), 0)
    b = lax.broadcasted_iota(jnp.int32, (clusters, clusters), 1)
    return jnp.where(a == b, 1.0, 0.5 * same).astype(jnp.bfloat16)


def dot_t(a, b):
    return lax.dot_general(a, b, (((1,), (1,)), ((), ())), preferred_element_type=jnp.float32)


def dot_0(a, b):
    return lax.dot_general(a, b, (((0,), (0,)), ((), ())), preferred_element_type=jnp.float32)


def best_kernel(n_plane, n_line, groups, order_ref, group_ref, *refs):
    blocks = refs[: n_plane + n_line]
    outs = refs[n_plane + n_line :]
    rows = blocks[0].shape[0] - AUX
    clusters = group_ref.shape[1]
    table = weights_table(group_ref, groups)
    hots = [one_hot(b[rows:, :rows].astype(jnp.float32), clusters) for b in blocks]
    plane_hot = jnp.concatenate(hots[:n_plane], axis=1)
    plane = jnp.concatenate([b[:rows, :] for b in blocks[:n_plane]], axis=0)
    plane_mix = jnp.dot(table, plane_hot, preferred_element_type=jnp.float32).astype(jnp.bfloat16)

    def scored(weight, sims):
        return jnp.where(weight > 0, weight * sims, -1.0)

    def column_max(score):
        return jnp.max(score, axis=0, keepdims=True)

    def part(score, i):
        return score[i * rows : (i + 1) * rows, :]

    own = blocks[0][:rows, :]
    score = scored(dot_0(plane_hot, plane_mix[:, :rows]), dot_t(plane, own))
    k = lax.broadcasted_iota(jnp.int32, (rows, rows), 0)
    q = lax.broadcasted_iota(jnp.int32, (rows, rows), 1)
    best = column_max(jnp.where(k < q, part(score, 0), -1.0))
    for i in range(1, n_plane):
        best = jnp.maximum(best, jnp.where(order_ref[i] < order_ref[0], column_max(part(score, i)), -1.0))
    outs[0][...] = best
    back = [jnp.full((1, rows), -1.0, jnp.float32) for _ in range(n_plane)]
    for j in range(n_line):
        line = blocks[n_plane + j][:rows, :]
        line_hot = hots[n_plane + j]
        line_order = order_ref[n_plane + j]
        score = scored(dot_0(plane_hot, jnp.dot(table, line_hot, preferred_element_type=jnp.float32).astype(jnp.bfloat16)), dot_t(plane, line))
        best = jnp.full((1, rows), -1.0, jnp.float32)
        for i in range(n_plane):
            best = jnp.maximum(best, jnp.where(order_ref[i] < line_order, column_max(part(score, i)), -1.0))
        outs[n_plane + j][...] = best
        score = column_max(scored(dot_0(line_hot, plane_mix), dot_t(line, plane)))
        for i in range(n_plane):
            mine = score[:, i * rows : (i + 1) * rows]
            back[i] = jnp.maximum(back[i], jnp.where(line_order < order_ref[i], mine, -1.0))
    outs[0][...] = jnp.maximum(outs[0][...], back[0])
    for i in range(1, n_plane):
        outs[i][...] = back[i]


def shifted(i, s, n):
    return i ^ s if n & (n - 1) == 0 else (i + s) % n


class Plan:
    def __init__(self, n_clu, n_grp):
        self.n_clu, self.n_grp = n_clu, n_grp
        target = math.sqrt(n_clu * n_grp)
        wide = min(a for a in range(1, n_clu + 1) if n_clu % a == 0 and (a * n_grp >= target or a == n_clu))
        length = n_clu // wide
        self.plane, self.line = [], []
        for s in range(wide):
            for t in range(n_grp):
                if s or t:
                    self.plane.append({
                        (z * wide + a) * n_grp + g: (z * wide + shifted(a, s, wide)) * n_grp + shifted(g, t, n_grp)
                        for z in range(length) for a in range(wide) for g in range(n_grp)
                    })
        for s in range(1, length // 2 + 1):
            pairs = [((z + s) % length, z) for z in range(length)]
            if 2 * s == length:
                pairs = [(z + s, z) if z % 2 == 0 else (z, z + s) for z in range(s)]
            self.line.append({
                (to * wide + a) * n_grp + g: (at * wide + a) * n_grp + g
                for to, at in pairs for a in range(wide) for g in range(n_grp)
            })

    def table(self):
        n = self.n_clu * self.n_grp
        rank = [(d % self.n_grp) * self.n_clu + d // self.n_grp for d in range(n)]
        rows = [[rank[d]] + [rank[m[d]] if d in m else -1 for m in self.plane + self.line] for d in range(n)]
        return jnp.array(rows, jnp.int32)


def send(x, mapping):
    return lax.ppermute(x, ("clu", "grp"), [(at, to) for to, at in mapping.items()])


def send_back(x, mapping):
    return lax.ppermute(x, ("clu", "grp"), list(mapping.items()))


def solution(mesh):
    n_clu, n_grp = mesh.shape["clu"], mesh.shape["grp"]
    plan = Plan(n_clu, n_grp)
    n_plane, n_line = 1 + len(plan.plane), len(plan.line)

    def shards(embeddings, cluster_id, cluster_group):
        rows = embeddings.shape[0]
        own = pack(embeddings, cluster_id)
        line = [send(own, m) for m in plan.line]
        plane = [own] + [send(own, m) for m in plan.plane]
        device = lax.axis_index("clu") * n_grp + lax.axis_index("grp")
        order = lax.dynamic_index_in_dim(plan.table(), device, 0, keepdims=False)
        vmem = pl.BlockSpec(memory_space=pltpu.VMEM)
        count = n_plane + n_line
        best = pl.pallas_call(
            functools.partial(best_kernel, n_plane, n_line, n_clu),
            out_shape=[jax.ShapeDtypeStruct((1, rows), jnp.float32)] * count,
            in_specs=[pl.BlockSpec(memory_space=pltpu.SMEM)] + [vmem] * (1 + count),
            out_specs=[vmem] * count,
            compiler_params=pltpu.CompilerParams(vmem_limit_bytes=48 * 2**20),
        )(order, cluster_group.reshape(1, -1), *plane, *line)
        found = [best[0]]
        for x, m in zip(best[1:], plan.plane + plan.line):
            back = send_back(x, m)
            if len(m) < n_clu * n_grp:
                got = jnp.isin(device, jnp.array(sorted(m.values()), jnp.int32))
                back = jnp.where(got, back, -1.0)
            found.append(back)
        return functools.reduce(jnp.maximum, found).reshape(rows)

    placed = (P(("clu", "grp"), None), P(("clu", "grp")), P())
    return jax.shard_map(
        shards, mesh=mesh, in_specs=placed, out_specs=P(("clu", "grp")), check_vma=False
    )
```

```python
import functools
import math

import jax
import jax.numpy as jnp
from jax import lax
from jax.experimental import pallas as pl
from jax.experimental.pallas import tpu as pltpu
from jax.sharding import PartitionSpec as P

AUX = 16
DIGIT = 256


def pack_kernel(emb_ref, id_ref, out_ref):
    rows, width = emb_ref.shape
    values = emb_ref[...].astype(jnp.float32)
    scale = lax.rsqrt(jnp.sum(values * values, axis=-1, keepdims=True) + 1e-06)
    out_ref[:rows, :] = (values * scale).astype(jnp.bfloat16)
    ids = jnp.broadcast_to(id_ref[...], (AUX, rows))
    row = lax.broadcasted_iota(jnp.int32, (AUX, rows), 0)
    digits = jnp.where(row == 0, ids % DIGIT, jnp.where(row == 1, ids // DIGIT, 1))
    if width > rows:
        digits = jnp.concatenate([digits, jnp.zeros((AUX, width - rows), jnp.int32)], axis=1)
    out_ref[rows:, :] = digits.astype(jnp.float32).astype(jnp.bfloat16)


def pack(embeddings, cluster_id):
    rows, width = embeddings.shape
    return pl.pallas_call(
        pack_kernel,
        out_shape=jax.ShapeDtypeStruct((rows + AUX, width), jnp.bfloat16),
    )(embeddings, cluster_id.reshape(1, rows))


def one_hot(digits, clusters):
    number = digits[0:1].astype(jnp.int32) + DIGIT * digits[1:2].astype(jnp.int32)
    index = lax.broadcasted_iota(jnp.int32, (clusters, digits.shape[1]), 0)
    return jnp.where((index == number) & (digits[2:3] > 0), 1.0, 0.0).astype(jnp.bfloat16)


def weights_table(group_ref, groups):
    clusters = group_ref.shape[1]
    index = lax.broadcasted_iota(jnp.int32, (groups, clusters), 0)
    member = jnp.where(index == group_ref[...], 1.0, 0.0).astype(jnp.bfloat16)
    same = lax.dot_general(member, member, (((0,), (0,)), ((), ())), preferred_element_type=jnp.float32)
    a = lax.broadcasted_iota(jnp.int32, (clusters, clusters), 0)
    b = lax.broadcasted_iota(jnp.int32, (clusters, clusters), 1)
    return jnp.where(a == b, 1.0, 0.5 * same).astype(jnp.bfloat16)


def best_kernel(n_keys, groups, order_ref, group_ref, *refs):
    n_in = (len(refs) + n_keys - 1) // 2
    blocks, outs = refs[:n_in], refs[n_in:]
    rows = blocks[0].shape[0] - AUX
    clusters = group_ref.shape[1]
    table = weights_table(group_ref, groups)
    hots = [one_hot(b[rows:, :rows].astype(jnp.float32), clusters) for b in blocks]
    key_hot = jnp.concatenate(hots[:n_keys], axis=1)
    keys = jnp.concatenate([b[:rows, :] for b in blocks[:n_keys]], axis=0)
    for out, j in zip(outs, [0, *range(n_keys, n_in)]):
        mixed = jnp.dot(table, hots[j], preferred_element_type=jnp.float32).astype(jnp.bfloat16)
        weight = lax.dot_general(key_hot, mixed, (((0,), (0,)), ((), ())), preferred_element_type=jnp.float32)
        sims = lax.dot_general(
            keys, blocks[j][:rows, :], (((1,), (1,)), ((), ())), preferred_element_type=jnp.float32
        )
        score = jnp.where(weight > 0, weight * sims, -1.0)
        best = jnp.full((1, rows), -1.0, jnp.float32)
        for i in range(n_keys):
            part = score[i * rows : (i + 1) * rows, :]
            if i == j:
                k = lax.broadcasted_iota(jnp.int32, (rows, rows), 0)
                q = lax.broadcasted_iota(jnp.int32, (rows, rows), 1)
                part = jnp.where(k < q, part, -1.0)
            found = jnp.max(part, axis=0, keepdims=True)
            if i != j:
                found = jnp.where(order_ref[i] < order_ref[j], found, -1.0)
            best = jnp.maximum(best, found)
        out[...] = best


def solution(mesh):
    n_clu, n_grp = mesh.shape["clu"], mesh.shape["grp"]
    target = math.sqrt(n_clu * n_grp)
    wide = min(a for a in range(1, n_clu + 1) if n_clu % a == 0 and (a * n_grp >= target or a == n_clu))
    length = n_clu // wide

    def permute(x, move):
        pairs = []
        for z in range(length):
            for a in range(wide):
                for g in range(n_grp):
                    at = move(z, a, g)
                    if at is not None:
                        pairs.append((((at[0] * wide) + at[1]) * n_grp + at[2], (z * wide + a) * n_grp + g))
        return pairs, lax.ppermute(x, ("clu", "grp"), pairs)

    def turned(a, s):
        return a ^ s if wide & (wide - 1) == 0 else (a + s) % wide

    def shards(embeddings, cluster_id, cluster_group):
        rows = embeddings.shape[0]
        own = pack(embeddings, cluster_id)
        clu, grp = lax.axis_index("clu"), lax.axis_index("grp")
        line, place = clu // wide, clu % wide

        def rank(z, a, g):
            return jnp.where(g < 0, n_clu * n_grp, g * n_clu + z * wide + a)

        visitors, ways, visitor_rank = [], [], []
        for s in range(1, length):
            def visit(z, a, g, s=s):
                at = (z + s) % length
                return (at, a, g) if g > 0 or at > z else None

            pairs, block = permute(own, visit)
            visitors.append(block)
            ways.append(pairs)
            visitor_rank.append(rank((line + s) % length, place, grp))
        keys, key_rank = [own], [rank(line, place, grp)]
        for s in range(1, wide):
            keys.append(permute(own, lambda z, a, g: (z, turned(a, s), g))[1])
            key_rank.append(rank(line, turned(place, s), grp))
        for i in range(wide):
            for t in range(1, n_grp):
                keys.append(permute(keys[i], lambda z, a, g: (z, a, g - t) if g >= t else None)[1])
                key_rank.append(rank(line, turned(place, i), grp - t))
        vmem = pl.BlockSpec(memory_space=pltpu.VMEM)
        best = pl.pallas_call(
            functools.partial(best_kernel, len(keys), n_clu),
            out_shape=[jax.ShapeDtypeStruct((1, rows), jnp.float32)] * length,
            in_specs=[pl.BlockSpec(memory_space=pltpu.SMEM)] + [vmem] * (1 + len(keys) + len(visitors)),
            out_specs=[vmem] * length,
            compiler_params=pltpu.CompilerParams(vmem_limit_bytes=48 * 2**20),
        )(jnp.stack(key_rank + visitor_rank).astype(jnp.int32), cluster_group.reshape(1, -1), *keys, *visitors)
        found = [best[0]]
        for s, pairs in zip(range(1, length), ways):
            back = lax.ppermute(best[s], ("clu", "grp"), [(to, at) for at, to in pairs])
            found.append(jnp.where((grp > 0) | (line >= s), back, -1.0))
        return functools.reduce(jnp.maximum, found).reshape(rows)

    placed = (P(("clu", "grp"), None), P(("clu", "grp")), P())
    return jax.shard_map(
        shards, mesh=mesh, in_specs=placed, out_specs=P(("clu", "grp")), check_vma=False
    )
```

```python
import functools
import math

import jax
import jax.numpy as jnp
from jax import lax
from jax.experimental import pallas as pl
from jax.experimental.pallas import tpu as pltpu
from jax.sharding import PartitionSpec as P

AUX = 16
DIGIT = 256


def pack_kernel(emb_ref, id_ref, out_ref):
    rows, width = emb_ref.shape
    values = emb_ref[...].astype(jnp.float32)
    scale = lax.rsqrt(jnp.sum(values * values, axis=-1, keepdims=True) + 1e-06)
    unit = (values * scale).astype(jnp.bfloat16)
    ids = jnp.broadcast_to(id_ref[...], (AUX, rows))
    row = lax.broadcasted_iota(jnp.int32, (AUX, rows), 0)
    digits = jnp.where(row == 0, ids % DIGIT, ids // DIGIT)
    if width > rows:
        digits = jnp.concatenate([digits, jnp.zeros((AUX, width - rows), jnp.int32)], axis=1)
    digits = digits.astype(jnp.float32).astype(jnp.bfloat16)
    for i in range(out_ref.shape[0]):
        out_ref[i, :rows, :] = unit
        out_ref[i, rows:, :] = digits


def pack(embeddings, cluster_id, copies):
    rows, width = embeddings.shape
    return pl.pallas_call(
        pack_kernel,
        out_shape=jax.ShapeDtypeStruct((copies, rows + AUX, width), jnp.bfloat16),
    )(embeddings, cluster_id.reshape(1, rows))


def one_hot(digits, clusters):
    number = digits[0:1].astype(jnp.int32) + DIGIT * digits[1:2].astype(jnp.int32)
    index = lax.broadcasted_iota(jnp.int32, (clusters, digits.shape[1]), 0)
    return jnp.where(index == number, 1.0, 0.0).astype(jnp.bfloat16)


def weights_table(group_ref, groups):
    clusters = group_ref.shape[1]
    index = lax.broadcasted_iota(jnp.int32, (groups, clusters), 0)
    member = jnp.where(index == group_ref[...], 1.0, 0.0).astype(jnp.bfloat16)
    same = lax.dot_general(member, member, (((0,), (0,)), ((), ())), preferred_element_type=jnp.float32)
    a = lax.broadcasted_iota(jnp.int32, (clusters, clusters), 0)
    b = lax.broadcasted_iota(jnp.int32, (clusters, clusters), 1)
    return jnp.where(a == b, 1.0, 0.5 * same).astype(jnp.bfloat16)


def best_kernel(groups, rank_ref, group_ref, visit_ref, *refs):
    key_refs, out_ref = refs[:-1], refs[-1]
    count, rows = visit_ref.shape[0], visit_ref.shape[1] - AUX
    clusters = group_ref.shape[1]
    table = weights_table(group_ref, groups)

    def hot(ref, i):
        return one_hot(ref[i, rows:, :rows].astype(jnp.float32), clusters)

    slots = [(ref, i) for ref in key_refs for i in range(ref.shape[0])]
    key_hot = jnp.concatenate([hot(ref, i) for ref, i in slots], axis=1)
    keys = jnp.concatenate([ref[i, :rows, :] for ref, i in slots], axis=0)
    k = lax.broadcasted_iota(jnp.int32, (rows, rows), 0)
    q = lax.broadcasted_iota(jnp.int32, (rows, rows), 1)
    for j in range(count):
        mixed = jnp.dot(table, hot(visit_ref, j), preferred_element_type=jnp.float32).astype(jnp.bfloat16)
        weight = lax.dot_general(key_hot, mixed, (((0,), (0,)), ((), ())), preferred_element_type=jnp.float32)
        sims = lax.dot_general(
            keys, visit_ref[j, :rows, :], (((1,), (1,)), ((), ())), preferred_element_type=jnp.float32
        )
        best = jnp.full((rows, rows), -1.0, jnp.float32)
        for i in range(len(slots)):
            at = slice(i * rows, (i + 1) * rows)
            earlier = k - q < (rank_ref[j] - rank_ref[count + i]) * rows
            best = jnp.maximum(best, jnp.where((weight[at] > 0) & earlier, weight[at] * sims[at], -1.0))
        out_ref[j : j + 1, :] = jnp.max(best, axis=0, keepdims=True)


def solution(mesh):
    n_clu, n_grp = mesh.shape["clu"], mesh.shape["grp"]
    target = math.sqrt(n_clu * n_grp)
    wide = min(a for a in range(1, n_clu + 1) if n_clu % a == 0 and (a * n_grp >= target or a == n_clu))
    length = n_clu // wide
    planes = [[z * wide + a for a in range(wide)] for z in range(length)]
    lines = [[z * wide + a for z in range(length)] for a in range(wide)]

    def exchange(x, groups):
        return lax.all_to_all(x, "clu", 0, 0, axis_index_groups=groups, tiled=True)

    def shards(embeddings, cluster_id, cluster_group):
        rows = embeddings.shape[0]
        own = pack(embeddings, cluster_id, max(wide, length))
        clu, grp = lax.axis_index("clu"), lax.axis_index("grp")
        line, place = clu // wide, clu % wide
        visitors = exchange(own[:length], lines)
        keys = [exchange(own[:wide], planes)]
        visit_rank = grp * n_clu + jnp.arange(length) * wide + place
        key_rank = [grp * n_clu + line * wide + jnp.arange(wide)]
        for t in range(1, n_grp):
            keys.append(lax.ppermute(keys[0], "grp", [(g, (g + t) % n_grp) for g in range(n_grp)]))
            key_rank.append((grp - t) % n_grp * n_clu + line * wide + jnp.arange(wide))
        vmem = pl.BlockSpec(memory_space=pltpu.VMEM)
        best = pl.pallas_call(
            functools.partial(best_kernel, n_clu),
            out_shape=jax.ShapeDtypeStruct((length, rows), jnp.float32),
            in_specs=[pl.BlockSpec(memory_space=pltpu.SMEM)] + [vmem] * (2 + len(keys)),
            out_specs=vmem,
            compiler_params=pltpu.CompilerParams(vmem_limit_bytes=48 * 2**20),
        )(jnp.concatenate([visit_rank] + key_rank).astype(jnp.int32), cluster_group.reshape(1, -1), visitors, *keys)
        return jnp.max(exchange(best, lines), axis=0)

    placed = (P(("clu", "grp"), None), P(("clu", "grp")), P())
    return jax.shard_map(
        shards, mesh=mesh, in_specs=placed, out_specs=P(("clu", "grp")), check_vma=False
    )
```

```python
import functools
import math

import jax
import jax.numpy as jnp
from jax import lax
from jax.experimental import pallas as pl
from jax.experimental.pallas import tpu as pltpu
from jax.sharding import PartitionSpec as P

AUX = 16
DIGIT = 256


def pack_kernel(emb_ref, id_ref, out_ref):
    rows, width = emb_ref.shape
    values = emb_ref[...].astype(jnp.float32)
    scale = lax.rsqrt(jnp.sum(values * values, axis=-1, keepdims=True) + 1e-06)
    out_ref[:rows, :] = (values * scale).astype(jnp.bfloat16)
    ids = jnp.broadcast_to(id_ref[...], (AUX, rows))
    row = lax.broadcasted_iota(jnp.int32, (AUX, rows), 0)
    digits = jnp.where(row == 0, ids % DIGIT, jnp.where(row == 1, ids // DIGIT, 1))
    if width > rows:
        digits = jnp.concatenate([digits, jnp.zeros((AUX, width - rows), jnp.int32)], axis=1)
    out_ref[rows:, :] = digits.astype(jnp.float32).astype(jnp.bfloat16)


def pack(embeddings, cluster_id):
    rows, width = embeddings.shape
    return pl.pallas_call(
        pack_kernel,
        out_shape=jax.ShapeDtypeStruct((rows + AUX, width), jnp.bfloat16),
    )(embeddings, cluster_id.reshape(1, rows))


def one_hot(digits, clusters):
    number = digits[0:1].astype(jnp.int32) + DIGIT * digits[1:2].astype(jnp.int32)
    index = lax.broadcasted_iota(jnp.int32, (clusters, digits.shape[1]), 0)
    return jnp.where((index == number) & (digits[2:3] > 0), 1.0, 0.0).astype(jnp.bfloat16)


def weights_table(group_ref, groups):
    clusters = group_ref.shape[1]
    index = lax.broadcasted_iota(jnp.int32, (groups, clusters), 0)
    member = jnp.where(index == group_ref[...], 1.0, 0.0).astype(jnp.bfloat16)
    same = lax.dot_general(member, member, (((0,), (0,)), ((), ())), preferred_element_type=jnp.float32)
    a = lax.broadcasted_iota(jnp.int32, (clusters, clusters), 0)
    b = lax.broadcasted_iota(jnp.int32, (clusters, clusters), 1)
    return jnp.where(a == b, 1.0, 0.5 * same).astype(jnp.bfloat16)


def best_kernel(n_keys, groups, order_ref, group_ref, *refs):
    n_in = (len(refs) + n_keys - 1) // 2
    blocks, outs = refs[:n_in], refs[n_in:]
    rows = blocks[0].shape[0] - AUX
    clusters = group_ref.shape[1]
    table = weights_table(group_ref, groups)
    hots = [one_hot(b[rows:, :rows].astype(jnp.float32), clusters) for b in blocks]
    key_hot = jnp.concatenate(hots[:n_keys], axis=1)
    keys = jnp.concatenate([b[:rows, :] for b in blocks[:n_keys]], axis=0)
    for out, j in zip(outs, [0, *range(n_keys, n_in)]):
        mixed = jnp.dot(table, hots[j], preferred_element_type=jnp.float32).astype(jnp.bfloat16)
        weight = lax.dot_general(key_hot, mixed, (((0,), (0,)), ((), ())), preferred_element_type=jnp.float32)
        sims = lax.dot_general(
            keys, blocks[j][:rows, :], (((1,), (1,)), ((), ())), preferred_element_type=jnp.float32
        )
        score = jnp.where(weight > 0, weight * sims, -1.0)
        best = jnp.full((1, rows), -1.0, jnp.float32)
        for i in range(n_keys):
            part = score[i * rows : (i + 1) * rows, :]
            if i == j:
                k = lax.broadcasted_iota(jnp.int32, (rows, rows), 0)
                q = lax.broadcasted_iota(jnp.int32, (rows, rows), 1)
                part = jnp.where(k < q, part, -1.0)
            found = jnp.max(part, axis=0, keepdims=True)
            if i != j:
                found = jnp.where(order_ref[i] < order_ref[j], found, -1.0)
            best = jnp.maximum(best, found)
        out[...] = best


def solution(mesh):
    n_clu, n_grp = mesh.shape["clu"], mesh.shape["grp"]
    target = math.sqrt(n_clu * n_grp)
    wide = min(a for a in range(1, n_clu + 1) if n_clu % a == 0 and (a * n_grp >= target or a == n_clu))
    length = n_clu // wide

    def permute(x, move):
        pairs = []
        for z in range(length):
            for a in range(wide):
                for g in range(n_grp):
                    at = move(z, a, g)
                    if at is not None:
                        pairs.append((((at[0] * wide) + at[1]) * n_grp + at[2], (z * wide + a) * n_grp + g))
        return pairs, lax.ppermute(x, ("clu", "grp"), pairs)

    def turned(a, s, n):
        return a ^ s if n & (n - 1) == 0 else (a + s) % n

    def shards(embeddings, cluster_id, cluster_group):
        rows = embeddings.shape[0]
        own = pack(embeddings, cluster_id)
        clu, grp = lax.axis_index("clu"), lax.axis_index("grp")
        line, place = clu // wide, clu % wide

        def rank(z, a, g):
            return jnp.where(g < 0, n_clu * n_grp, g * n_clu + z * wide + a)

        visitors, ways, visitor_rank = [], [], []
        for s in range(1, length):
            def visit(z, a, g, s=s):
                at = turned(z, s, length)
                return (at, a, g) if g > 0 or at > z else None

            pairs, block = permute(own, visit)
            visitors.append(block)
            ways.append(pairs)
            visitor_rank.append(rank(turned(line, s, length), place, grp))
        keys, key_rank = [own], [rank(line, place, grp)]
        for t in reversed(range(n_grp)):
            for s in range(wide):
                if s or t:
                    keys.append(permute(own, lambda z, a, g: (z, turned(a, s, wide), g - t) if g >= t else None)[1])
                    key_rank.append(rank(line, turned(place, s, wide), grp - t))
        vmem = pl.BlockSpec(memory_space=pltpu.VMEM)
        best = pl.pallas_call(
            functools.partial(best_kernel, len(keys), n_clu),
            out_shape=[jax.ShapeDtypeStruct((1, rows), jnp.float32)] * length,
            in_specs=[pl.BlockSpec(memory_space=pltpu.SMEM)] + [vmem] * (1 + len(keys) + len(visitors)),
            out_specs=[vmem] * length,
            compiler_params=pltpu.CompilerParams(vmem_limit_bytes=48 * 2**20),
        )(jnp.stack(key_rank + visitor_rank).astype(jnp.int32), cluster_group.reshape(1, -1), *keys, *visitors)
        found = [best[0]]
        for s, pairs in zip(range(1, length), ways):
            back = lax.ppermute(best[s], ("clu", "grp"), [(to, at) for at, to in pairs])
            at = line ^ s if length & (length - 1) == 0 else (line - s) % length
            found.append(jnp.where((grp > 0) | (at < line), back, -1.0))
        return functools.reduce(jnp.maximum, found).reshape(rows)

    placed = (P(("clu", "grp"), None), P(("clu", "grp")), P())
    return jax.shard_map(
        shards, mesh=mesh, in_specs=placed, out_specs=P(("clu", "grp")), check_vma=False
    )
```

```python
import functools
import math

import jax
import jax.numpy as jnp
from jax import lax
from jax.experimental import pallas as pl
from jax.experimental.pallas import tpu as pltpu
from jax.sharding import PartitionSpec as P

AUX = 16
DIGIT = 256


def pack_kernel(emb_ref, id_ref, out_ref):
    rows, width = emb_ref.shape
    values = emb_ref[...].astype(jnp.float32)
    scale = lax.rsqrt(jnp.sum(values * values, axis=-1, keepdims=True) + 1e-06)
    out_ref[:rows, :] = (values * scale).astype(jnp.bfloat16)
    ids = jnp.broadcast_to(id_ref[...], (AUX, rows))
    row = lax.broadcasted_iota(jnp.int32, (AUX, rows), 0)
    digits = jnp.where(row == 0, ids % DIGIT, jnp.where(row == 1, ids // DIGIT, 1))
    if width > rows:
        digits = jnp.concatenate([digits, jnp.zeros((AUX, width - rows), jnp.int32)], axis=1)
    out_ref[rows:, :] = digits.astype(jnp.float32).astype(jnp.bfloat16)


def pack(embeddings, cluster_id):
    rows, width = embeddings.shape
    return pl.pallas_call(
        pack_kernel,
        out_shape=jax.ShapeDtypeStruct((rows + AUX, width), jnp.bfloat16),
    )(embeddings, cluster_id.reshape(1, rows))


def one_hot(digits, clusters):
    number = digits[0:1].astype(jnp.int32) + DIGIT * digits[1:2].astype(jnp.int32)
    index = lax.broadcasted_iota(jnp.int32, (clusters, digits.shape[1]), 0)
    return jnp.where((index == number) & (digits[2:3] > 0), 1.0, 0.0).astype(jnp.bfloat16)


def weights_table(group_ref, groups):
    clusters = group_ref.shape[1]
    index = lax.broadcasted_iota(jnp.int32, (groups, clusters), 0)
    member = jnp.where(index == group_ref[...], 1.0, 0.0).astype(jnp.bfloat16)
    same = lax.dot_general(member, member, (((0,), (0,)), ((), ())), preferred_element_type=jnp.float32)
    a = lax.broadcasted_iota(jnp.int32, (clusters, clusters), 0)
    b = lax.broadcasted_iota(jnp.int32, (clusters, clusters), 1)
    return jnp.where(a == b, 1.0, 0.5 * same).astype(jnp.bfloat16)


def best_kernel(n_keys, groups, rank_ref, group_ref, *refs):
    key_refs = refs[:n_keys]
    count = (len(refs) - n_keys - 1) // 2
    visitors, outs = refs[n_keys : n_keys + count], refs[n_keys + count :]
    blocks = [ref.at[i] for ref in key_refs for i in range(ref.shape[0])]
    n_blocks = len(blocks)
    rows = blocks[0].shape[0] - AUX
    clusters = group_ref.shape[1]
    table = weights_table(group_ref, groups)

    def hot(block):
        return one_hot(block[rows:, :rows].astype(jnp.float32), clusters)

    key_hot = jnp.concatenate([hot(b) for b in blocks], axis=1)
    keys = jnp.concatenate([b[:rows, :] for b in blocks], axis=0)
    for j, (out, query) in enumerate(zip(outs, [blocks[0], *visitors])):
        mixed = jnp.dot(table, hot(query), preferred_element_type=jnp.float32).astype(jnp.bfloat16)
        weight = lax.dot_general(key_hot, mixed, (((0,), (0,)), ((), ())), preferred_element_type=jnp.float32)
        sims = lax.dot_general(
            keys, query[:rows, :], (((1,), (1,)), ((), ())), preferred_element_type=jnp.float32
        )
        score = jnp.where(weight > 0, weight * sims, -1.0)
        best = jnp.full((1, rows), -1.0, jnp.float32)
        rank = rank_ref[n_blocks + j - 1] if j else rank_ref[0]
        for i in range(n_blocks):
            part = score[i * rows : (i + 1) * rows, :]
            if i + j == 0:
                k = lax.broadcasted_iota(jnp.int32, (rows, rows), 0)
                q = lax.broadcasted_iota(jnp.int32, (rows, rows), 1)
                part = jnp.where(k < q, part, -1.0)
            found = jnp.max(part, axis=0, keepdims=True)
            if i + j:
                found = jnp.where(rank_ref[i] < rank, found, -1.0)
            best = jnp.maximum(best, found)
        out[...] = best


def solution(mesh):
    n_clu, n_grp = mesh.shape["clu"], mesh.shape["grp"]
    target = math.sqrt(n_clu * n_grp)
    wide = min(a for a in range(1, n_clu + 1) if n_clu % a == 0 and (a * n_grp >= target or a == n_clu))
    length = n_clu // wide

    def pairs_of(move):
        pairs = []
        for z in range(length):
            for a in range(wide):
                for g in range(n_grp):
                    at = move(z, a, g)
                    if at is not None:
                        pairs.append((((at[0] * wide) + at[1]) * n_grp + at[2], (z * wide + a) * n_grp + g))
        return pairs

    def permute(x, move):
        pairs = pairs_of(move)
        return pairs, lax.ppermute(x, ("clu", "grp"), pairs)

    def turned(a, s, n):
        return a ^ s if n & (n - 1) == 0 else (a + s) % n

    def shards(embeddings, cluster_id, cluster_group):
        rows = embeddings.shape[0]
        own = pack(embeddings, cluster_id)
        clu, grp = lax.axis_index("clu"), lax.axis_index("grp")
        line, place = clu // wide, clu % wide

        def rank(z, a, g):
            return jnp.where(g < 0, n_clu * n_grp, g * n_clu + z * wide + a)

        half = length // 2 if length & (length - 1) == 0 else length
        visitors, ways, visitor_rank = [], [], []
        for s in range(1, length):
            hop = s % half if s > half else s

            def visit(z, a, g, by):
                home = turned(z, s, length)
                return (turned(z, by, length), a, g) if g > 0 or home > z else None

            block = visitors[half - 1] if s > half else own
            visitors.append(permute(block, lambda z, a, g: visit(z, a, g, hop))[1])
            ways.append(pairs_of(lambda z, a, g: visit(z, a, g, s)))
            visitor_rank.append(rank(turned(line, s, length), place, grp))
        near = [permute(own, lambda z, a, g: (z, turned(a, s, wide), g))[1] for s in range(1, wide)]
        near = jnp.stack([own] + near)
        near_rank = [rank(line, turned(place, s, wide), grp) for s in range(wide)]
        keys, key_rank = [near], near_rank
        for t in range(1, n_grp):
            keys.append(permute(near, lambda z, a, g: (z, a, g - t) if g >= t else None)[1])
            key_rank = key_rank + [rank(line, turned(place, s, wide), grp - t) for s in range(wide)]
        vmem = pl.BlockSpec(memory_space=pltpu.VMEM)
        best = pl.pallas_call(
            functools.partial(best_kernel, len(keys), n_clu),
            out_shape=[jax.ShapeDtypeStruct((1, rows), jnp.float32)] * length,
            in_specs=[pl.BlockSpec(memory_space=pltpu.SMEM)] + [vmem] * (1 + len(keys) + len(visitors)),
            out_specs=[vmem] * length,
            compiler_params=pltpu.CompilerParams(vmem_limit_bytes=48 * 2**20),
        )(jnp.stack(key_rank + visitor_rank).astype(jnp.int32), cluster_group.reshape(1, -1), *keys, *visitors)
        found = [best[0]]
        for s, pairs in zip(range(1, length), ways):
            back = lax.ppermute(best[s], ("clu", "grp"), [(to, at) for at, to in pairs])
            at = line ^ s if length & (length - 1) == 0 else (line - s) % length
            found.append(jnp.where((grp > 0) | (at < line), back, -1.0))
        return functools.reduce(jnp.maximum, found).reshape(rows)

    placed = (P(("clu", "grp"), None), P(("clu", "grp")), P())
    return jax.shard_map(
        shards, mesh=mesh, in_specs=placed, out_specs=P(("clu", "grp")), check_vma=False
    )
```

```python
import functools
import math

import jax
import jax.numpy as jnp
from jax import lax
from jax.experimental import pallas as pl
from jax.experimental.pallas import tpu as pltpu
from jax.sharding import PartitionSpec as P

AUX = 16
DIGIT = 256


def pack_kernel(emb_ref, id_ref, out_ref):
    rows, width = emb_ref.shape
    values = emb_ref[...].astype(jnp.float32)
    scale = lax.rsqrt(jnp.sum(values * values, axis=-1, keepdims=True) + 1e-06)
    out_ref[:rows, :] = (values * scale).astype(jnp.bfloat16)
    ids = jnp.broadcast_to(id_ref[...], (AUX, rows))
    row = lax.broadcasted_iota(jnp.int32, (AUX, rows), 0)
    digits = jnp.where(row == 0, ids % DIGIT, ids // DIGIT)
    if width > rows:
        digits = jnp.concatenate([digits, jnp.zeros((AUX, width - rows), jnp.int32)], axis=1)
    out_ref[rows:, :] = digits.astype(jnp.float32).astype(jnp.bfloat16)


def pack(embeddings, cluster_id):
    rows, width = embeddings.shape
    return pl.pallas_call(
        pack_kernel,
        out_shape=jax.ShapeDtypeStruct((rows + AUX, width), jnp.bfloat16),
    )(embeddings, cluster_id.reshape(1, rows))


def one_hot(digits, clusters):
    number = digits[0:1].astype(jnp.int32) + DIGIT * digits[1:2].astype(jnp.int32)
    index = lax.broadcasted_iota(jnp.int32, (clusters, digits.shape[1]), 0)
    return jnp.where(index == number, 1.0, 0.0).astype(jnp.bfloat16)


def weights_table(group_ref, groups):
    clusters = group_ref.shape[1]
    index = lax.broadcasted_iota(jnp.int32, (groups, clusters), 0)
    member = jnp.where(index == group_ref[...], 1.0, 0.0).astype(jnp.bfloat16)
    same = lax.dot_general(member, member, (((0,), (0,)), ((), ())), preferred_element_type=jnp.float32)
    a = lax.broadcasted_iota(jnp.int32, (clusters, clusters), 0)
    b = lax.broadcasted_iota(jnp.int32, (clusters, clusters), 1)
    return jnp.where(a == b, 1.0, 0.5 * same).astype(jnp.bfloat16)


def best_kernel(n_keys, groups, rank_ref, group_ref, *refs):
    key_refs = refs[:n_keys]
    count = (len(refs) - n_keys - 1) // 2
    visitors, outs = refs[n_keys : n_keys + count], refs[n_keys + count :]
    blocks = [ref.at[i] for ref in key_refs for i in range(ref.shape[0])]
    n_blocks = len(blocks)
    rows = blocks[0].shape[0] - AUX
    clusters = group_ref.shape[1]
    table = weights_table(group_ref, groups)

    def hot(block):
        return one_hot(block[rows:, :rows].astype(jnp.float32), clusters)

    key_hot = jnp.concatenate([hot(b) for b in blocks], axis=1)
    keys = jnp.concatenate([b[:rows, :] for b in blocks], axis=0)
    for j, (out, query) in enumerate(zip(outs, [blocks[0], *visitors])):
        mixed = jnp.dot(table, hot(query), preferred_element_type=jnp.float32).astype(jnp.bfloat16)
        weight = lax.dot_general(key_hot, mixed, (((0,), (0,)), ((), ())), preferred_element_type=jnp.float32)
        sims = lax.dot_general(
            keys, query[:rows, :], (((1,), (1,)), ((), ())), preferred_element_type=jnp.float32
        )
        score = jnp.where(weight > 0, weight * sims, -1.0)
        best = jnp.full((1, rows), -1.0, jnp.float32)
        rank = rank_ref[n_blocks + j - 1] if j else rank_ref[0]
        for i in range(n_blocks):
            part = score[i * rows : (i + 1) * rows, :]
            if i + j == 0:
                k = lax.broadcasted_iota(jnp.int32, (rows, rows), 0)
                q = lax.broadcasted_iota(jnp.int32, (rows, rows), 1)
                part = jnp.where(k < q, part, -1.0)
            found = jnp.max(part, axis=0, keepdims=True)
            if i + j:
                found = jnp.where(rank_ref[i] < rank, found, -1.0)
            best = jnp.maximum(best, found)
        out[...] = best


def solution(mesh):
    n_clu, n_grp = mesh.shape["clu"], mesh.shape["grp"]
    target = math.sqrt(n_clu * n_grp)
    wide = min(a for a in range(1, n_clu + 1) if n_clu % a == 0 and (a * n_grp >= target or a == n_clu))
    length = n_clu // wide

    def permute(x, move):
        pairs = []
        for z in range(length):
            for a in range(wide):
                for g in range(n_grp):
                    at = move(z, a, g)
                    pairs.append(((at[0] * wide + at[1]) * n_grp + at[2], (z * wide + a) * n_grp + g))
        return lax.ppermute(x, ("clu", "grp"), pairs)

    def turned(a, s, n):
        return a ^ abs(s) if n & (n - 1) == 0 else (a + s) % n

    def shards(embeddings, cluster_id, cluster_group):
        rows = embeddings.shape[0]
        own = pack(embeddings, cluster_id)
        clu, grp = lax.axis_index("clu"), lax.axis_index("grp")
        line, place = clu // wide, clu % wide

        def rank(z, a, g):
            return g * n_clu + z * wide + a

        half = length // 2 if length & (length - 1) == 0 else length
        first = [permute(own, lambda z, a, g: (turned(z, s, length), a, g)) for s in range(1, min(half + 1, length))]
        near = [permute(own, lambda z, a, g: (z, turned(a, s, wide), g)) for s in range(1, wide)]
        first, near = lax.optimization_barrier((first, near))
        visitors = first + [
            permute(first[half - 1], lambda z, a, g: (turned(z, s, length), a, g)) for s in range(1, length - half)
        ]
        visitor_rank = [rank(turned(line, s, length), place, grp) for s in range(1, length)]
        near = jnp.stack([own] + near)
        keys = [near]
        key_rank = [rank(line, turned(place, s, wide), grp) for s in range(wide)]
        for t in range(1, n_grp):
            keys.append(permute(near, lambda z, a, g: (z, a, turned(g, t, n_grp))))
            key_rank += [rank(line, turned(place, s, wide), turned(grp, t, n_grp)) for s in range(wide)]
        vmem = pl.BlockSpec(memory_space=pltpu.VMEM)
        best = pl.pallas_call(
            functools.partial(best_kernel, len(keys), n_clu),
            out_shape=[jax.ShapeDtypeStruct((1, rows), jnp.float32)] * length,
            in_specs=[pl.BlockSpec(memory_space=pltpu.SMEM)] + [vmem] * (1 + len(keys) + len(visitors)),
            out_specs=[vmem] * length,
            compiler_params=pltpu.CompilerParams(vmem_limit_bytes=48 * 2**20),
        )(jnp.stack(key_rank + visitor_rank).astype(jnp.int32), cluster_group.reshape(1, -1), *keys, *visitors)
        found = [best[0]]
        for s in range(1, length):
            found.append(permute(best[s], lambda z, a, g: (turned(z, -s, length), a, g)))
        return functools.reduce(jnp.maximum, found).reshape(rows)

    placed = (P(("clu", "grp"), None), P(("clu", "grp")), P())
    return jax.shard_map(
        shards, mesh=mesh, in_specs=placed, out_specs=P(("clu", "grp")), check_vma=False
    )
```

```python
import functools
import math

import jax
import jax.numpy as jnp
from jax import lax
from jax.experimental import pallas as pl
from jax.experimental.pallas import tpu as pltpu
from jax.sharding import PartitionSpec as P

AUX = 16
DIGIT = 256


def pack_kernel(emb_ref, id_ref, out_ref):
    rows, width = emb_ref.shape
    values = emb_ref[...].astype(jnp.float32)
    scale = lax.rsqrt(jnp.sum(values * values, axis=-1, keepdims=True) + 1e-06)
    out_ref[:rows, :] = (values * scale).astype(jnp.bfloat16)
    ids = jnp.broadcast_to(id_ref[...], (AUX, rows))
    row = lax.broadcasted_iota(jnp.int32, (AUX, rows), 0)
    digits = jnp.where(row == 0, ids % DIGIT, ids // DIGIT)
    if width > rows:
        digits = jnp.concatenate([digits, jnp.zeros((AUX, width - rows), jnp.int32)], axis=1)
    out_ref[rows:, :] = digits.astype(jnp.float32).astype(jnp.bfloat16)


def pack(embeddings, cluster_id):
    rows, width = embeddings.shape
    return pl.pallas_call(
        pack_kernel,
        out_shape=jax.ShapeDtypeStruct((rows + AUX, width), jnp.bfloat16),
    )(embeddings, cluster_id.reshape(1, rows))


def one_hot(digits, clusters):
    number = digits[0:1].astype(jnp.int32) + DIGIT * digits[1:2].astype(jnp.int32)
    index = lax.broadcasted_iota(jnp.int32, (clusters, digits.shape[1]), 0)
    return jnp.where(index == number, 1.0, 0.0).astype(jnp.bfloat16)


def weights_table(group_ref, groups):
    clusters = group_ref.shape[1]
    index = lax.broadcasted_iota(jnp.int32, (groups, clusters), 0)
    member = jnp.where(index == group_ref[...], 1.0, 0.0).astype(jnp.bfloat16)
    same = lax.dot_general(member, member, (((0,), (0,)), ((), ())), preferred_element_type=jnp.float32)
    a = lax.broadcasted_iota(jnp.int32, (clusters, clusters), 0)
    b = lax.broadcasted_iota(jnp.int32, (clusters, clusters), 1)
    return jnp.where(a == b, 1.0, 0.5 * same).astype(jnp.bfloat16)


def best_kernel(n_keys, groups, rank_ref, group_ref, *refs):
    blocks = refs[:n_keys]
    count = (len(refs) - n_keys - 1) // 2
    visitors, outs = refs[n_keys : n_keys + count], refs[n_keys + count :]
    rows = blocks[0].shape[0] - AUX
    clusters = group_ref.shape[1]
    table = weights_table(group_ref, groups)

    def hot(block):
        return one_hot(block[rows:, :rows].astype(jnp.float32), clusters)

    key_hot = jnp.concatenate([hot(b) for b in blocks], axis=1)
    keys = jnp.concatenate([b[:rows, :] for b in blocks], axis=0)
    for j, (out, query) in enumerate(zip(outs, [blocks[0], *visitors])):
        mixed = jnp.dot(table, hot(query), preferred_element_type=jnp.float32).astype(jnp.bfloat16)
        weight = lax.dot_general(key_hot, mixed, (((0,), (0,)), ((), ())), preferred_element_type=jnp.float32)
        sims = lax.dot_general(
            keys, query[:rows, :], (((1,), (1,)), ((), ())), preferred_element_type=jnp.float32
        )
        score = jnp.where(weight > 0, weight * sims, -1.0)
        best = jnp.full((1, rows), -1.0, jnp.float32)
        rank = rank_ref[n_keys + j - 1] if j else rank_ref[0]
        for i in range(n_keys):
            part = score[i * rows : (i + 1) * rows, :]
            if i + j == 0:
                k = lax.broadcasted_iota(jnp.int32, (rows, rows), 0)
                q = lax.broadcasted_iota(jnp.int32, (rows, rows), 1)
                part = jnp.where(k < q, part, -1.0)
            found = jnp.max(part, axis=0, keepdims=True)
            if i + j:
                found = jnp.where(rank_ref[i] < rank, found, -1.0)
            best = jnp.maximum(best, found)
        out[...] = best


def solution(mesh):
    n_clu, n_grp = mesh.shape["clu"], mesh.shape["grp"]
    target = math.sqrt(n_clu * n_grp)
    wide = min(a for a in range(1, n_clu + 1) if n_clu % a == 0 and (a * n_grp >= target or a == n_clu))
    length = n_clu // wide

    def permute(x, move):
        pairs = []
        for z in range(length):
            for a in range(wide):
                for g in range(n_grp):
                    at = move(z, a, g)
                    pairs.append(((at[0] * wide + at[1]) * n_grp + at[2], (z * wide + a) * n_grp + g))
        return lax.ppermute(x, ("clu", "grp"), pairs)

    def turned(a, s, n):
        return a ^ abs(s) if n & (n - 1) == 0 else (a + s) % n

    def shards(embeddings, cluster_id, cluster_group):
        rows = embeddings.shape[0]
        own = pack(embeddings, cluster_id)
        clu, grp = lax.axis_index("clu"), lax.axis_index("grp")
        line, place = clu // wide, clu % wide

        def rank(z, a, g):
            return g * n_clu + z * wide + a

        half = length // 2 if length & (length - 1) == 0 else length
        near = [permute(own, lambda z, a, g: (z, turned(a, s, wide), g)) for s in range(1, wide)]
        first = [permute(own, lambda z, a, g: (turned(z, s, length), a, g)) for s in range(1, min(half + 1, length))]
        near, first = lax.optimization_barrier((near, first))
        visitors = first + [
            permute(first[half - 1], lambda z, a, g: (turned(z, s, length), a, g)) for s in range(1, length - half)
        ]
        visitor_rank = [rank(turned(line, s, length), place, grp) for s in range(1, length)]
        keys = [own] + near
        key_rank = [rank(line, turned(place, s, wide), grp) for s in range(wide)]
        for t in range(1, n_grp):
            for s in range(wide):
                keys.append(permute(keys[s], lambda z, a, g: (z, a, turned(g, t, n_grp))))
                key_rank.append(rank(line, turned(place, s, wide), turned(grp, t, n_grp)))
        vmem = pl.BlockSpec(memory_space=pltpu.VMEM)
        best = pl.pallas_call(
            functools.partial(best_kernel, len(keys), n_clu),
            out_shape=[jax.ShapeDtypeStruct((1, rows), jnp.float32)] * length,
            in_specs=[pl.BlockSpec(memory_space=pltpu.SMEM)] + [vmem] * (1 + len(keys) + len(visitors)),
            out_specs=[vmem] * length,
            compiler_params=pltpu.CompilerParams(vmem_limit_bytes=48 * 2**20),
        )(jnp.stack(key_rank + visitor_rank).astype(jnp.int32), cluster_group.reshape(1, -1), *keys, *visitors)
        found = [best[0]]
        for s in range(1, length):
            found.append(permute(best[s], lambda z, a, g: (turned(z, -s, length), a, g)))
        return functools.reduce(jnp.maximum, found).reshape(rows)

    placed = (P(("clu", "grp"), None), P(("clu", "grp")), P())
    return jax.shard_map(
        shards, mesh=mesh, in_specs=placed, out_specs=P(("clu", "grp")), check_vma=False
    )
```

```python
import functools
import math

import jax
import jax.numpy as jnp
from jax import lax
from jax.experimental import pallas as pl
from jax.experimental.pallas import tpu as pltpu
from jax.sharding import PartitionSpec as P

AUX = 16
DIGIT = 256


def pack_kernel(emb_ref, id_ref, *out_refs):
    rows, width = emb_ref.shape
    values = emb_ref[...].astype(jnp.float32)
    scale = lax.rsqrt(jnp.sum(values * values, axis=-1, keepdims=True) + 1e-06)
    unit = (values * scale).astype(jnp.bfloat16)
    ids = jnp.broadcast_to(id_ref[...], (AUX, rows))
    row = lax.broadcasted_iota(jnp.int32, (AUX, rows), 0)
    digits = jnp.where(row == 0, ids % DIGIT, ids // DIGIT)
    if width > rows:
        digits = jnp.concatenate([digits, jnp.zeros((AUX, width - rows), jnp.int32)], axis=1)
    digits = digits.astype(jnp.float32).astype(jnp.bfloat16)
    for ref in out_refs:
        ref[:rows, :] = unit
        ref[rows:, :] = digits


def pack(embeddings, cluster_id):
    rows, width = embeddings.shape
    return pl.pallas_call(
        pack_kernel,
        out_shape=[jax.ShapeDtypeStruct((rows + AUX, width), jnp.bfloat16)] * 2,
    )(embeddings, cluster_id.reshape(1, rows))


def one_hot(digits, clusters):
    number = digits[0:1].astype(jnp.int32) + DIGIT * digits[1:2].astype(jnp.int32)
    index = lax.broadcasted_iota(jnp.int32, (clusters, digits.shape[1]), 0)
    return jnp.where(index == number, 1.0, 0.0).astype(jnp.bfloat16)


def weights_table(group_ref, groups):
    clusters = group_ref.shape[1]
    index = lax.broadcasted_iota(jnp.int32, (groups, clusters), 0)
    member = jnp.where(index == group_ref[...], 1.0, 0.0).astype(jnp.bfloat16)
    same = lax.dot_general(member, member, (((0,), (0,)), ((), ())), preferred_element_type=jnp.float32)
    a = lax.broadcasted_iota(jnp.int32, (clusters, clusters), 0)
    b = lax.broadcasted_iota(jnp.int32, (clusters, clusters), 1)
    return jnp.where(a == b, 1.0, 0.5 * same).astype(jnp.bfloat16)


def best_kernel(jobs, n_blocks, groups, rank_ref, group_ref, *refs):
    blocks, outs = refs[:n_blocks], refs[len(refs) - len(jobs) :]
    before = iter(refs[n_blocks : len(refs) - len(jobs)])
    rows = blocks[0].shape[0] - AUX
    clusters = group_ref.shape[1]
    table = weights_table(group_ref, groups)
    hots = [one_hot(b[rows:, :rows].astype(jnp.float32), clusters) for b in blocks]
    spans = {}
    for _, lo, hi, _ in jobs:
        if (lo, hi) not in spans:
            spans[lo, hi] = (
                jnp.concatenate(hots[lo:hi], axis=1),
                jnp.concatenate([b[:rows, :] for b in blocks[lo:hi]], axis=0),
            )
    for (query, lo, hi, continues), out in zip(jobs, outs):
        key_hot, keys = spans[lo, hi]
        mixed = jnp.dot(table, hots[query], preferred_element_type=jnp.float32).astype(jnp.bfloat16)
        weight = lax.dot_general(key_hot, mixed, (((0,), (0,)), ((), ())), preferred_element_type=jnp.float32)
        sims = lax.dot_general(
            keys, blocks[query][:rows, :], (((1,), (1,)), ((), ())), preferred_element_type=jnp.float32
        )
        score = jnp.where(weight > 0, weight * sims, -1.0)
        best = next(before)[...] if continues else jnp.full((1, rows), -1.0, jnp.float32)
        for i in range(lo, hi):
            part = score[(i - lo) * rows : (i - lo + 1) * rows, :]
            if i == query:
                k = lax.broadcasted_iota(jnp.int32, (rows, rows), 0)
                q = lax.broadcasted_iota(jnp.int32, (rows, rows), 1)
                found = jnp.max(jnp.where(k < q, part, -1.0), axis=0, keepdims=True)
            else:
                found = jnp.max(part, axis=0, keepdims=True)
                found = jnp.where(rank_ref[i] < rank_ref[query], found, -1.0)
            best = jnp.maximum(best, found)
        out[...] = best


def best_of(jobs, blocks, before, cluster_group, groups):
    rows, width = blocks[0][0].shape[0] - AUX, blocks[0][0].shape[1]
    vmem = pl.BlockSpec(memory_space=pltpu.VMEM)
    ranks = jnp.stack([r for _, r in blocks]).astype(jnp.int32)
    pairs = sum(hi - lo for _, lo, hi, _ in jobs) * rows * rows
    return pl.pallas_call(
        functools.partial(best_kernel, jobs, len(blocks), groups),
        out_shape=[jax.ShapeDtypeStruct((1, rows), jnp.float32)] * len(jobs),
        in_specs=[pl.BlockSpec(memory_space=pltpu.SMEM)] + [vmem] * (1 + len(blocks) + len(before)),
        out_specs=[vmem] * len(jobs),
        compiler_params=pltpu.CompilerParams(vmem_limit_bytes=40 * 2**20),
        cost_estimate=pl.CostEstimate(
            flops=2 * pairs * width, bytes_accessed=2 * len(blocks) * rows * width, transcendentals=0
        ),
    )(ranks, cluster_group.reshape(1, -1), *[b for b, _ in blocks], *before)


def solution(mesh):
    n_clu, n_grp = mesh.shape["clu"], mesh.shape["grp"]
    target = math.sqrt(n_clu * n_grp)
    wide = min(a for a in range(1, n_clu + 1) if n_clu % a == 0 and (a * n_grp >= target or a == n_clu))
    length = n_clu // wide

    def permute(x, move):
        pairs = []
        for z in range(length):
            for a in range(wide):
                for g in range(n_grp):
                    at = move(z, a, g)
                    pairs.append(((at[0] * wide + at[1]) * n_grp + at[2], (z * wide + a) * n_grp + g))
        return lax.ppermute(x, ("clu", "grp"), pairs)

    def turned(a, s, n):
        return a ^ abs(s) if n & (n - 1) == 0 else (a + s) % n

    def shards(embeddings, cluster_id, cluster_group):
        rows = embeddings.shape[0]
        own, local = pack(embeddings, cluster_id)
        clu, grp = lax.axis_index("clu"), lax.axis_index("grp")
        line, place = clu // wide, clu % wide

        def rank(z, a, g):
            return g * n_clu + z * wide + a

        def along(x, s):
            return permute(x, lambda z, a, g: (turned(z, s, length), a, g))

        half = length // 2 if length & (length - 1) == 0 else length
        near = [permute(own, lambda z, a, g: (z, turned(a, s, wide), g)) for s in range(1, wide)]
        first = [along(own, s) for s in range(1, min(half + 1, length))]
        near, first = lax.optimization_barrier((near, first))
        last = [along(first[half - 1], s) for s in range(1, length - half)]
        far, far_rank = [], []
        for t in range(1, n_grp):
            for s in range(wide):
                block = near[s - 1] if s else own
                far.append(permute(block, lambda z, a, g: (z, a, turned(g, t, n_grp))))
                far_rank.append(rank(line, turned(place, s, wide), turned(grp, t, n_grp)))
        near = list(zip([local] + near, [rank(line, turned(place, s, wide), grp) for s in range(wide)]))
        far = list(zip(far, far_rank))
        visit_rank = [rank(turned(line, s, length), place, grp) for s in range(1, length)]
        first = list(zip(first, visit_rank))
        last = list(zip(last, visit_rank[len(first) :]))
        jobs = [(0, 0, wide, False)] + [(wide + j, 0, wide, False) for j in range(len(first))]
        best = best_of(jobs, near + first, [], cluster_group, n_clu)
        at, end = len(last), len(last) + wide + len(far)
        jobs = [(at, at + wide, end, True)] + [(end + j, at + wide, end, True) for j in range(len(first))]
        jobs += [(j, at, end, False) for j in range(at)]
        best = best_of(jobs, last + near + far + first, best, cluster_group, n_clu)
        found = [best[0]] + [along(best[s], -s) for s in range(1, length)]
        return functools.reduce(jnp.maximum, found).reshape(rows)

    placed = (P(("clu", "grp"), None), P(("clu", "grp")), P())
    return jax.shard_map(
        shards, mesh=mesh, in_specs=placed, out_specs=P(("clu", "grp")), check_vma=False
    )
```

```python
import functools
import math

import jax
import jax.numpy as jnp
from jax import lax
from jax.experimental import pallas as pl
from jax.experimental.pallas import tpu as pltpu
from jax.sharding import PartitionSpec as P

AUX = 16
DIGIT = 256


def pack_kernel(groups, emb_ref, id_ref, group_ref, out_ref, table_ref):
    rows, width = emb_ref.shape
    values = emb_ref[...].astype(jnp.float32)
    scale = lax.rsqrt(jnp.sum(values * values, axis=-1, keepdims=True) + 1e-06)
    out_ref[:rows, :] = (values * scale).astype(jnp.bfloat16)
    ids = jnp.broadcast_to(id_ref[...], (AUX, rows))
    row = lax.broadcasted_iota(jnp.int32, (AUX, rows), 0)
    digits = jnp.where(row == 0, ids % DIGIT, ids // DIGIT)
    if width > rows:
        digits = jnp.concatenate([digits, jnp.zeros((AUX, width - rows), jnp.int32)], axis=1)
    out_ref[rows:, :] = digits.astype(jnp.float32).astype(jnp.bfloat16)
    clusters = group_ref.shape[1]
    index = lax.broadcasted_iota(jnp.int32, (groups, clusters), 0)
    member = jnp.where(index == group_ref[...], 1.0, 0.0).astype(jnp.bfloat16)
    same = lax.dot_general(member, member, (((0,), (0,)), ((), ())), preferred_element_type=jnp.float32)
    one = lax.broadcasted_iota(jnp.int32, (clusters, clusters), 0)
    other = lax.broadcasted_iota(jnp.int32, (clusters, clusters), 1)
    table_ref[...] = jnp.where(one == other, 1.0, 0.5 * same).astype(jnp.bfloat16)


def pack(embeddings, cluster_id, cluster_group, groups):
    rows, width = embeddings.shape
    clusters = cluster_group.shape[0]
    return pl.pallas_call(
        functools.partial(pack_kernel, groups),
        out_shape=[pltpu.VMEM((rows + AUX, width), jnp.bfloat16), pltpu.VMEM((clusters, clusters), jnp.bfloat16)],
    )(embeddings, cluster_id.reshape(1, rows), cluster_group.reshape(1, clusters))


def one_hot(digits, clusters):
    number = digits[0:1].astype(jnp.int32) + DIGIT * digits[1:2].astype(jnp.int32)
    index = lax.broadcasted_iota(jnp.int32, (clusters, digits.shape[1]), 0)
    return jnp.where(index == number, 1.0, 0.0).astype(jnp.bfloat16)


def best_kernel(n_keys, own, rank_ref, table_ref, *refs):
    n_queries = (len(refs) - n_keys) // 2
    keys, queries, outs = refs[:n_keys], refs[n_keys : n_keys + n_queries], refs[n_keys + n_queries :]
    rows = keys[0].shape[0] - AUX
    clusters = table_ref.shape[0]

    def hot(block):
        return one_hot(block[rows:, :rows].astype(jnp.float32), clusters)

    key_hot = jnp.concatenate([hot(b) for b in keys], axis=1)
    key_rows = jnp.concatenate([b[:rows, :] for b in keys], axis=0)
    for j in range(n_queries):
        mixed = jnp.dot(table_ref[...], hot(queries[j]), preferred_element_type=jnp.float32).astype(jnp.bfloat16)
        weight = lax.dot_general(key_hot, mixed, (((0,), (0,)), ((), ())), preferred_element_type=jnp.float32)
        sims = lax.dot_general(
            key_rows, queries[j][:rows, :], (((1,), (1,)), ((), ())), preferred_element_type=jnp.float32
        )
        score = jnp.where(weight > 0, weight * sims, -1.0)
        best = jnp.full((1, rows), -1.0, jnp.float32)
        for i in range(n_keys):
            part = score[i * rows : (i + 1) * rows, :]
            if own and i + j == 0:
                k = lax.broadcasted_iota(jnp.int32, (rows, rows), 0)
                q = lax.broadcasted_iota(jnp.int32, (rows, rows), 1)
                found = jnp.max(jnp.where(k < q, part, -1.0), axis=0, keepdims=True)
            else:
                found = jnp.max(part, axis=0, keepdims=True)
                found = jnp.where(rank_ref[i] < rank_ref[n_keys + j], found, -1.0)
            best = jnp.maximum(best, found)
        outs[j][...] = best


def best_of(keys, queries, table, own):
    rows, width = keys[0][0].shape[0] - AUX, keys[0][0].shape[1]
    vmem = pl.BlockSpec(memory_space=pltpu.VMEM)
    ranks = jnp.stack([r for _, r in keys + queries]).astype(jnp.int32)
    pairs = len(keys) * len(queries) * rows * rows
    return pl.pallas_call(
        functools.partial(best_kernel, len(keys), own),
        out_shape=[jax.ShapeDtypeStruct((1, rows), jnp.float32)] * len(queries),
        in_specs=[pl.BlockSpec(memory_space=pltpu.SMEM)] + [vmem] * (1 + len(keys) + len(queries)),
        out_specs=[vmem] * len(queries),
        compiler_params=pltpu.CompilerParams(vmem_limit_bytes=40 * 2**20),
        cost_estimate=pl.CostEstimate(
            flops=2 * pairs * width, bytes_accessed=2 * (len(keys) + len(queries)) * rows * width, transcendentals=0
        ),
    )(ranks, table, *[b for b, _ in keys + queries])


def solution(mesh):
    n_clu, n_grp = mesh.shape["clu"], mesh.shape["grp"]
    target = math.sqrt(n_clu * n_grp)
    wide = min(a for a in range(1, n_clu + 1) if n_clu % a == 0 and (a * n_grp >= target or a == n_clu))
    length = n_clu // wide

    def permute(x, move):
        pairs = []
        for z in range(length):
            for a in range(wide):
                for g in range(n_grp):
                    at = move(z, a, g)
                    pairs.append(((at[0] * wide + at[1]) * n_grp + at[2], (z * wide + a) * n_grp + g))
        return lax.ppermute(x, ("clu", "grp"), pairs)

    def turned(a, s, n):
        return a ^ abs(s) if n & (n - 1) == 0 else (a + s) % n

    def shards(embeddings, cluster_id, cluster_group):
        rows = embeddings.shape[0]
        own, table = pack(embeddings, cluster_id, cluster_group, n_clu)
        clu, grp = lax.axis_index("clu"), lax.axis_index("grp")
        line, place = clu // wide, clu % wide

        def rank(z, a, g):
            return g * n_clu + z * wide + a

        def along(x, s):
            return permute(x, lambda z, a, g: (turned(z, s, length), a, g))

        half = length // 2 if length & (length - 1) == 0 else length
        first = [along(own, s) for s in reversed(range(1, min(half + 1, length)))]
        near = [permute(own, lambda z, a, g: (z, turned(a, s, wide), g)) for s in reversed(range(1, wide))]
        first, near = lax.optimization_barrier((first, near))
        first, near = first[::-1], near[::-1]
        last = [along(first[half - 1], s) for s in range(1, length - half)]
        far, far_rank = [], []
        for t in range(1, n_grp):
            for s in range(wide):
                block = near[s - 1] if s else own
                far.append(permute(block, lambda z, a, g: (z, a, turned(g, t, n_grp))))
                far_rank.append(rank(line, turned(place, s, wide), turned(grp, t, n_grp)))
        near = list(zip([own] + near, [rank(line, turned(place, s, wide), grp) for s in range(wide)]))
        far = list(zip(far, far_rank))
        visit_rank = [rank(turned(line, s, length), place, grp) for s in range(1, length)]
        first = list(zip(first, visit_rank))
        last = list(zip(last, visit_rank[len(first) :]))
        best = best_of(near + far, near[:1] + first, table, True)
        if last:
            best = best + best_of(near + far, last, table, False)
        found = [best[0]] + [along(best[s], -s) for s in range(1, length)]
        return functools.reduce(jnp.maximum, found).reshape(rows)

    placed = (P(("clu", "grp"), None), P(("clu", "grp")), P())
    return jax.shard_map(
        shards, mesh=mesh, in_specs=placed, out_specs=P(("clu", "grp")), check_vma=False
    )
```

```python
import functools
import math

import jax
import jax.numpy as jnp
from jax import lax
from jax.experimental import pallas as pl
from jax.experimental.pallas import tpu as pltpu
from jax.sharding import PartitionSpec as P

AUX = 16
DIGIT = 256


def pack_kernel(groups, emb_ref, id_ref, group_ref, out_ref, table_ref):
    rows, width = emb_ref.shape
    values = emb_ref[...].astype(jnp.float32)
    scale = lax.rsqrt(jnp.sum(values * values, axis=-1, keepdims=True) + 1e-06)
    out_ref[:rows, :] = (values * scale).astype(jnp.bfloat16)
    ids = jnp.broadcast_to(id_ref[...], (AUX, rows))
    row = lax.broadcasted_iota(jnp.int32, (AUX, rows), 0)
    digits = jnp.where(row == 0, ids % DIGIT, ids // DIGIT)
    if width > rows:
        digits = jnp.concatenate([digits, jnp.zeros((AUX, width - rows), jnp.int32)], axis=1)
    out_ref[rows:, :] = digits.astype(jnp.float32).astype(jnp.bfloat16)
    clusters = group_ref.shape[1]
    index = lax.broadcasted_iota(jnp.int32, (groups, clusters), 0)
    member = jnp.where(index == group_ref[...], 1.0, 0.0).astype(jnp.bfloat16)
    same = lax.dot_general(member, member, (((0,), (0,)), ((), ())), preferred_element_type=jnp.float32)
    one = lax.broadcasted_iota(jnp.int32, (clusters, clusters), 0)
    other = lax.broadcasted_iota(jnp.int32, (clusters, clusters), 1)
    table_ref[...] = jnp.where(one == other, 1.0, 0.5 * same).astype(jnp.bfloat16)


def pack(embeddings, cluster_id, cluster_group, groups):
    rows, width = embeddings.shape
    clusters = cluster_group.shape[0]
    return pl.pallas_call(
        functools.partial(pack_kernel, groups),
        out_shape=[pltpu.VMEM((rows + AUX, width), jnp.bfloat16), pltpu.VMEM((clusters, clusters), jnp.bfloat16)],
    )(embeddings, cluster_id.reshape(1, rows), cluster_group.reshape(1, clusters))


def one_hot(digits, clusters):
    number = digits[0:1].astype(jnp.int32) + DIGIT * digits[1:2].astype(jnp.int32)
    index = lax.broadcasted_iota(jnp.int32, (clusters, digits.shape[1]), 0)
    return jnp.where(index == number, 1.0, 0.0).astype(jnp.bfloat16)


def best_kernel(n_keys, own, ranks, table_ref, *refs):
    n_queries = (len(refs) - n_keys) // 2
    keys, queries, outs = refs[:n_keys], refs[n_keys : n_keys + n_queries], refs[n_keys + n_queries :]
    rows = keys[0].shape[0] - AUX
    clusters = table_ref.shape[0]
    clu, grp = lax.axis_index("clu"), lax.axis_index("grp")
    ranks = [rank(clu, grp) for rank in ranks]

    def hot(block):
        return one_hot(block[rows:, :rows].astype(jnp.float32), clusters)

    key_hot = jnp.concatenate([hot(b) for b in keys], axis=1)
    key_rows = jnp.concatenate([b[:rows, :] for b in keys], axis=0)
    for j in range(n_queries):
        mixed = jnp.dot(table_ref[...], hot(queries[j]), preferred_element_type=jnp.float32).astype(jnp.bfloat16)
        weight = lax.dot_general(key_hot, mixed, (((0,), (0,)), ((), ())), preferred_element_type=jnp.float32)
        sims = lax.dot_general(
            key_rows, queries[j][:rows, :], (((1,), (1,)), ((), ())), preferred_element_type=jnp.float32
        )
        score = jnp.where(weight > 0, weight * sims, -1.0)
        best = jnp.full((1, rows), -1.0, jnp.float32)
        for i in range(n_keys):
            part = score[i * rows : (i + 1) * rows, :]
            if own and i + j == 0:
                k = lax.broadcasted_iota(jnp.int32, (rows, rows), 0)
                q = lax.broadcasted_iota(jnp.int32, (rows, rows), 1)
                found = jnp.max(jnp.where(k < q, part, -1.0), axis=0, keepdims=True)
            else:
                found = jnp.max(part, axis=0, keepdims=True)
                found = jnp.where(ranks[i] < ranks[n_keys + j], found, -1.0)
            best = jnp.maximum(best, found)
        outs[j][...] = best


def best_of(keys, queries, table, own):
    rows, width = keys[0][0].shape[0] - AUX, keys[0][0].shape[1]
    vmem = pl.BlockSpec(memory_space=pltpu.VMEM)
    ranks = [r for _, r in keys + queries]
    pairs = len(keys) * len(queries) * rows * rows
    return pl.pallas_call(
        functools.partial(best_kernel, len(keys), own, ranks),
        out_shape=[jax.ShapeDtypeStruct((1, rows), jnp.float32)] * len(queries),
        in_specs=[vmem] * (1 + len(keys) + len(queries)),
        out_specs=[vmem] * len(queries),
        compiler_params=pltpu.CompilerParams(vmem_limit_bytes=40 * 2**20),
        cost_estimate=pl.CostEstimate(
            flops=2 * pairs * width, bytes_accessed=2 * (len(keys) + len(queries)) * rows * width, transcendentals=0
        ),
    )(table, *[b for b, _ in keys + queries])


def solution(mesh):
    n_clu, n_grp = mesh.shape["clu"], mesh.shape["grp"]
    target = math.sqrt(n_clu * n_grp)
    wide = min(a for a in range(1, n_clu + 1) if n_clu % a == 0 and (a * n_grp >= target or a == n_clu))
    length = n_clu // wide

    def permute(x, move):
        pairs = []
        for z in range(length):
            for a in range(wide):
                for g in range(n_grp):
                    at = move(z, a, g)
                    pairs.append(((at[0] * wide + at[1]) * n_grp + at[2], (z * wide + a) * n_grp + g))
        return lax.ppermute(x, ("clu", "grp"), pairs)

    def turned(a, s, n):
        return a ^ abs(s) if n & (n - 1) == 0 else (a + s) % n

    def shards(embeddings, cluster_id, cluster_group):
        rows = embeddings.shape[0]
        own, table = pack(embeddings, cluster_id, cluster_group, n_clu)

        def rank(z=0, a=0, g=0):
            def of(clu, grp):
                line, place = turned(clu // wide, z, length), turned(clu % wide, a, wide)
                return turned(grp, g, n_grp) * n_clu + line * wide + place

            return of

        def along(x, s):
            return permute(x, lambda z, a, g: (turned(z, s, length), a, g))

        half = length // 2 if length & (length - 1) == 0 else length
        first = [along(own, s) for s in reversed(range(1, min(half + 1, length)))]
        near = [permute(own, lambda z, a, g: (z, turned(a, s, wide), g)) for s in reversed(range(1, wide))]
        first, near = lax.optimization_barrier((first, near))
        first, near = first[::-1], near[::-1]
        last = [along(first[half - 1], s) for s in range(1, length - half)]
        far, far_rank = [], []
        for t in range(1, n_grp):
            for s in range(wide):
                block = near[s - 1] if s else own
                far.append(permute(block, lambda z, a, g: (z, a, turned(g, t, n_grp))))
                far_rank.append(rank(a=s, g=t))
        near = list(zip([own] + near, [rank(a=s) for s in range(wide)]))
        far = list(zip(far, far_rank))
        visit_rank = [rank(z=s) for s in range(1, length)]
        first = list(zip(first, visit_rank))
        last = list(zip(last, visit_rank[len(first) :]))
        best = best_of(near + far, near[:1] + first, table, True)
        if last:
            best = best + best_of(near + far, last, table, False)
        found = [best[0]] + [along(best[s], -s) for s in range(1, length)]
        return functools.reduce(jnp.maximum, found).reshape(rows)

    placed = (P(("clu", "grp"), None), P(("clu", "grp")), P())
    return jax.shard_map(
        shards, mesh=mesh, in_specs=placed, out_specs=P(("clu", "grp")), check_vma=False
    )
```

```python
import functools
import math

import jax
import jax.numpy as jnp
from jax import lax
from jax.experimental import pallas as pl
from jax.experimental.pallas import tpu as pltpu
from jax.sharding import PartitionSpec as P

AUX = 16
DIGIT = 256


def pack_kernel(groups, emb_ref, id_ref, group_ref, out_ref, table_ref):
    rows, width = emb_ref.shape
    values = emb_ref[...].astype(jnp.float32)
    scale = lax.rsqrt(jnp.sum(values * values, axis=-1, keepdims=True) + 1e-06)
    out_ref[:rows, :] = (values * scale).astype(jnp.bfloat16)
    ids = jnp.broadcast_to(id_ref[...], (AUX, rows))
    row = lax.broadcasted_iota(jnp.int32, (AUX, rows), 0)
    digits = jnp.where(row == 0, ids % DIGIT, ids // DIGIT)
    if width > rows:
        digits = jnp.concatenate([digits, jnp.zeros((AUX, width - rows), jnp.int32)], axis=1)
    out_ref[rows:, :] = digits.astype(jnp.float32).astype(jnp.bfloat16)
    clusters = group_ref.shape[1]
    index = lax.broadcasted_iota(jnp.int32, (groups, clusters), 0)
    member = jnp.where(index == group_ref[...], 1.0, 0.0).astype(jnp.bfloat16)
    same = lax.dot_general(member, member, (((0,), (0,)), ((), ())), preferred_element_type=jnp.float32)
    one = lax.broadcasted_iota(jnp.int32, (clusters, clusters), 0)
    other = lax.broadcasted_iota(jnp.int32, (clusters, clusters), 1)
    table_ref[...] = jnp.where(one == other, 1.0, 0.5 * same).astype(jnp.bfloat16)


def pack(embeddings, cluster_id, cluster_group, groups):
    rows, width = embeddings.shape
    clusters = cluster_group.shape[0]
    return pl.pallas_call(
        functools.partial(pack_kernel, groups),
        out_shape=[pltpu.VMEM((rows + AUX, width), jnp.bfloat16), pltpu.VMEM((clusters, clusters), jnp.bfloat16)],
    )(embeddings, cluster_id.reshape(1, rows), cluster_group.reshape(1, clusters))


def one_hot(digits, clusters):
    number = digits[0:1].astype(jnp.int32) + DIGIT * digits[1:2].astype(jnp.int32)
    index = lax.broadcasted_iota(jnp.int32, (clusters, digits.shape[1]), 0)
    return jnp.where(index == number, 1.0, 0.0).astype(jnp.bfloat16)


def best_kernel(n_keys, own, ranks, table_ref, *refs):
    n_queries = (len(refs) - n_keys) // 2
    keys, queries, outs = refs[:n_keys], refs[n_keys : n_keys + n_queries], refs[n_keys + n_queries :]
    rows = keys[0].shape[0] - AUX
    clusters = table_ref.shape[0]
    clu, grp = lax.axis_index("clu"), lax.axis_index("grp")
    ranks = [rank(clu, grp) for rank in ranks]

    def hot(block):
        return one_hot(block[rows:, :rows].astype(jnp.float32), clusters)

    key_hot = jnp.concatenate([hot(b) for b in keys], axis=1)
    key_rows = jnp.concatenate([b[:rows, :] for b in keys], axis=0)
    for j in range(n_queries):
        mixed = jnp.dot(table_ref[...], hot(queries[j]), preferred_element_type=jnp.float32).astype(jnp.bfloat16)
        weight = lax.dot_general(key_hot, mixed, (((0,), (0,)), ((), ())), preferred_element_type=jnp.float32)
        sims = lax.dot_general(
            key_rows, queries[j][:rows, :], (((1,), (1,)), ((), ())), preferred_element_type=jnp.float32
        )
        score = jnp.where(weight > 0, weight * sims, -1.0)
        best = jnp.full((1, rows), -1.0, jnp.float32)
        for i in range(n_keys):
            part = score[i * rows : (i + 1) * rows, :]
            if own and i + j == 0:
                k = lax.broadcasted_iota(jnp.int32, (rows, rows), 0)
                q = lax.broadcasted_iota(jnp.int32, (rows, rows), 1)
                found = jnp.max(jnp.where(k < q, part, -1.0), axis=0, keepdims=True)
            else:
                found = jnp.max(part, axis=0, keepdims=True)
                found = jnp.where(ranks[i] < ranks[n_keys + j], found, -1.0)
            best = jnp.maximum(best, found)
        outs[j][...] = best


def best_of(keys, queries, table, own):
    rows, width = keys[0][0].shape[0] - AUX, keys[0][0].shape[1]
    vmem = pl.BlockSpec(memory_space=pltpu.VMEM)
    ranks = [r for _, r in keys + queries]
    pairs = len(keys) * len(queries) * rows * rows
    return pl.pallas_call(
        functools.partial(best_kernel, len(keys), own, ranks),
        out_shape=[jax.ShapeDtypeStruct((1, rows), jnp.float32)] * len(queries),
        in_specs=[vmem] * (1 + len(keys) + len(queries)),
        out_specs=[vmem] * len(queries),
        compiler_params=pltpu.CompilerParams(vmem_limit_bytes=40 * 2**20),
        cost_estimate=pl.CostEstimate(
            flops=2 * pairs * width, bytes_accessed=2 * (len(keys) + len(queries)) * rows * width, transcendentals=0
        ),
    )(table, *[b for b, _ in keys + queries])


def solution(mesh):
    n_clu, n_grp = mesh.shape["clu"], mesh.shape["grp"]
    target = math.sqrt(n_clu * n_grp)
    wide = min(a for a in range(1, n_clu + 1) if n_clu % a == 0 and (a * n_grp >= target or a == n_clu))
    length = n_clu // wide

    def permute(x, move):
        pairs = []
        for z in range(length):
            for a in range(wide):
                for g in range(n_grp):
                    at = move(z, a, g)
                    pairs.append(((at[0] * wide + at[1]) * n_grp + at[2], (z * wide + a) * n_grp + g))
        return lax.ppermute(x, ("clu", "grp"), pairs)

    def turned(a, s, n):
        return a ^ abs(s) if n & (n - 1) == 0 else (a + s) % n

    def shards(embeddings, cluster_id, cluster_group):
        rows = embeddings.shape[0]
        own, table = pack(embeddings, cluster_id, cluster_group, n_clu)

        def rank(z=0, a=0, g=0):
            def of(clu, grp):
                line, place = turned(clu // wide, z, length), turned(clu % wide, a, wide)
                return turned(grp, g, n_grp) * n_clu + line * wide + place

            return of

        def along(x, s):
            return permute(x, lambda z, a, g: (turned(z, s, length), a, g))

        half = length // 2 if length & (length - 1) == 0 else length
        middle = along(own, half) if half < length else None
        near = [permute(own, lambda z, a, g: (z, turned(a, s, wide), g)) for s in reversed(range(1, wide))]
        first = [along(own, s) for s in range(1, half)]
        middle, near, first = lax.optimization_barrier((middle, near, first))
        near = near[::-1]
        first = first if middle is None else first + [middle]
        last = [along(first[half - 1], s) for s in range(1, length - half)]
        far, far_rank = [], []
        for t in range(1, n_grp):
            for s in range(wide):
                block = near[s - 1] if s else own
                far.append(permute(block, lambda z, a, g: (z, a, turned(g, t, n_grp))))
                far_rank.append(rank(a=s, g=t))
        near = list(zip([own] + near, [rank(a=s) for s in range(wide)]))
        far = list(zip(far, far_rank))
        visit_rank = [rank(z=s) for s in range(1, length)]
        first = list(zip(first, visit_rank))
        last = list(zip(last, visit_rank[len(first) :]))
        best = best_of(near + far, near[:1] + first, table, True)
        if last:
            best = best + best_of(near + far, last, table, False)
        found = [best[0]] + [along(best[s], -s) for s in range(1, length)]
        return functools.reduce(jnp.maximum, found).reshape(rows)

    placed = (P(("clu", "grp"), None), P(("clu", "grp")), P())
    return jax.shard_map(
        shards, mesh=mesh, in_specs=placed, out_specs=P(("clu", "grp")), check_vma=False
    )
```

```python
import functools
import math

import jax
import jax.numpy as jnp
from jax import lax
from jax.experimental import pallas as pl
from jax.experimental.pallas import tpu as pltpu
from jax.sharding import PartitionSpec as P

AUX = 16
DIGIT = 256


def pack_kernel(groups, emb_ref, id_ref, group_ref, out_ref, table_ref):
    rows, width = emb_ref.shape
    values = emb_ref[...].astype(jnp.float32)
    scale = lax.rsqrt(jnp.sum(values * values, axis=-1, keepdims=True) + 1e-06)
    out_ref[:rows, :] = (values * scale).astype(jnp.bfloat16)
    ids = jnp.broadcast_to(id_ref[...], (AUX, rows))
    row = lax.broadcasted_iota(jnp.int32, (AUX, rows), 0)
    digits = jnp.where(row == 0, ids % DIGIT, ids // DIGIT)
    if width > rows:
        digits = jnp.concatenate([digits, jnp.zeros((AUX, width - rows), jnp.int32)], axis=1)
    out_ref[rows:, :] = digits.astype(jnp.float32).astype(jnp.bfloat16)
    clusters = group_ref.shape[1]
    index = lax.broadcasted_iota(jnp.int32, (groups, clusters), 0)
    member = jnp.where(index == group_ref[...], 1.0, 0.0).astype(jnp.bfloat16)
    same = lax.dot_general(member, member, (((0,), (0,)), ((), ())), preferred_element_type=jnp.float32)
    one = lax.broadcasted_iota(jnp.int32, (clusters, clusters), 0)
    other = lax.broadcasted_iota(jnp.int32, (clusters, clusters), 1)
    table_ref[...] = jnp.where(one == other, 1.0, 0.5 * same).astype(jnp.bfloat16)


def pack(embeddings, cluster_id, cluster_group, groups):
    rows, width = embeddings.shape
    clusters = cluster_group.shape[0]
    return pl.pallas_call(
        functools.partial(pack_kernel, groups),
        out_shape=[pltpu.VMEM((rows + AUX, width), jnp.bfloat16), pltpu.VMEM((clusters, clusters), jnp.bfloat16)],
    )(embeddings, cluster_id.reshape(1, rows), cluster_group.reshape(1, clusters))


def one_hot(digits, clusters):
    number = digits[0:1].astype(jnp.int32) + DIGIT * digits[1:2].astype(jnp.int32)
    index = lax.broadcasted_iota(jnp.int32, (clusters, digits.shape[1]), 0)
    return jnp.where(index == number, 1.0, 0.0).astype(jnp.bfloat16)


def best_kernel(n_keys, own, ranks, table_ref, *refs):
    n_queries = (len(refs) - n_keys) // 2
    keys, queries, outs = refs[:n_keys], refs[n_keys : n_keys + n_queries], refs[n_keys + n_queries :]
    rows = keys[0].shape[0] - AUX
    clusters = table_ref.shape[0]
    clu, grp = lax.axis_index("clu"), lax.axis_index("grp")
    ranks = [rank(clu, grp) for rank in ranks]

    def hot(block):
        return one_hot(block[rows:, :rows].astype(jnp.float32), clusters)

    key_hot = jnp.concatenate([hot(b) for b in keys], axis=1)
    key_rows = jnp.concatenate([b[:rows, :] for b in keys], axis=0)
    for j in range(n_queries):
        mixed = jnp.dot(table_ref[...], hot(queries[j]), preferred_element_type=jnp.float32).astype(jnp.bfloat16)
        weight = lax.dot_general(key_hot, mixed, (((0,), (0,)), ((), ())), preferred_element_type=jnp.float32)
        sims = lax.dot_general(
            key_rows, queries[j][:rows, :], (((1,), (1,)), ((), ())), preferred_element_type=jnp.float32
        )
        score = jnp.where(weight > 0, weight * sims, -1.0)
        best = jnp.full((1, rows), -1.0, jnp.float32)
        for i in range(n_keys):
            part = score[i * rows : (i + 1) * rows, :]
            if own and i + j == 0:
                k = lax.broadcasted_iota(jnp.int32, (rows, rows), 0)
                q = lax.broadcasted_iota(jnp.int32, (rows, rows), 1)
                found = jnp.max(jnp.where(k < q, part, -1.0), axis=0, keepdims=True)
            else:
                found = jnp.max(part, axis=0, keepdims=True)
                found = jnp.where(ranks[i] < ranks[n_keys + j], found, -1.0)
            best = jnp.maximum(best, found)
        outs[j][...] = best


def best_of(keys, queries, table, own):
    rows, width = keys[0][0].shape[0] - AUX, keys[0][0].shape[1]
    vmem = pl.BlockSpec(memory_space=pltpu.VMEM)
    ranks = [r for _, r in keys + queries]
    pairs = len(keys) * len(queries) * rows * rows
    return pl.pallas_call(
        functools.partial(best_kernel, len(keys), own, ranks),
        out_shape=[jax.ShapeDtypeStruct((1, rows), jnp.float32)] * len(queries),
        in_specs=[vmem] * (1 + len(keys) + len(queries)),
        out_specs=[vmem] * len(queries),
        compiler_params=pltpu.CompilerParams(vmem_limit_bytes=40 * 2**20),
        cost_estimate=pl.CostEstimate(
            flops=2 * pairs * width, bytes_accessed=2 * (len(keys) + len(queries)) * rows * width, transcendentals=0
        ),
    )(table, *[b for b, _ in keys + queries])


def solution(mesh):
    n_clu, n_grp = mesh.shape["clu"], mesh.shape["grp"]
    target = math.sqrt(n_clu * n_grp)
    wide = min(a for a in range(1, n_clu + 1) if n_clu % a == 0 and (a * n_grp >= target or a == n_clu))
    length = n_clu // wide

    def permute(x, move):
        pairs = []
        for z in range(length):
            for a in range(wide):
                for g in range(n_grp):
                    at = move(z, a, g)
                    pairs.append(((at[0] * wide + at[1]) * n_grp + at[2], (z * wide + a) * n_grp + g))
        return lax.ppermute(x, ("clu", "grp"), pairs)

    def turned(a, s, n):
        return a ^ abs(s) if n & (n - 1) == 0 else (a + s) % n

    def shards(embeddings, cluster_id, cluster_group):
        rows = embeddings.shape[0]
        own, table = pack(embeddings, cluster_id, cluster_group, n_clu)

        def rank(z=0, a=0, g=0):
            def of(clu, grp):
                line, place = turned(clu // wide, z, length), turned(clu % wide, a, wide)
                return turned(grp, g, n_grp) * n_clu + line * wide + place

            return of

        def along(x, s):
            return permute(x, lambda z, a, g: (turned(z, s, length), a, g))

        half = length // 2 if length & (length - 1) == 0 else length
        near = [permute(own, lambda z, a, g: (z, turned(a, s, wide), g)) for s in range(1, wide)]
        first = [along(own, s) for s in range(1, min(half + 1, length))]
        last = [along(first[half - 1], s) for s in range(1, length - half)]
        far, far_rank = [], []
        for t in range(1, n_grp):
            for s in range(wide):
                block = near[s - 1] if s else own
                far.append(permute(block, lambda z, a, g: (z, a, turned(g, t, n_grp))))
                far_rank.append(rank(a=s, g=t))
        near = list(zip([own] + near, [rank(a=s) for s in range(wide)]))
        far = list(zip(far, far_rank))
        visit_rank = [rank(z=s) for s in range(1, length)]
        first = list(zip(first, visit_rank))
        last = list(zip(last, visit_rank[len(first) :]))
        best = best_of(near + far, near[:1] + first + last, table, True)
        found = [best[0]] + [along(best[s], -s) for s in range(1, length)]
        return functools.reduce(jnp.maximum, found).reshape(rows)

    placed = (P(("clu", "grp"), None), P(("clu", "grp")), P())
    return jax.shard_map(
        shards, mesh=mesh, in_specs=placed, out_specs=P(("clu", "grp")), check_vma=False
    )
```

```python
import functools
import math

import jax
import jax.numpy as jnp
from jax import lax
from jax.experimental import pallas as pl
from jax.experimental.pallas import tpu as pltpu
from jax.sharding import PartitionSpec as P

AUX = 16
DIGIT = 256


def pack_kernel(groups, emb_ref, id_ref, group_ref, out_ref, table_ref):
    rows, width = emb_ref.shape
    values = emb_ref[...].astype(jnp.float32)
    scale = lax.rsqrt(jnp.sum(values * values, axis=-1, keepdims=True) + 1e-06)
    out_ref[:rows, :] = (values * scale).astype(jnp.bfloat16)
    ids = jnp.broadcast_to(id_ref[...], (AUX, rows))
    row = lax.broadcasted_iota(jnp.int32, (AUX, rows), 0)
    digits = jnp.where(row == 0, ids % DIGIT, ids // DIGIT)
    if width > rows:
        digits = jnp.concatenate([digits, jnp.zeros((AUX, width - rows), jnp.int32)], axis=1)
    out_ref[rows:, :] = digits.astype(jnp.float32).astype(jnp.bfloat16)
    clusters = group_ref.shape[1]
    index = lax.broadcasted_iota(jnp.int32, (groups, clusters), 0)
    member = jnp.where(index == group_ref[...], 1.0, 0.0).astype(jnp.bfloat16)
    same = lax.dot_general(member, member, (((0,), (0,)), ((), ())), preferred_element_type=jnp.float32)
    one = lax.broadcasted_iota(jnp.int32, (clusters, clusters), 0)
    other = lax.broadcasted_iota(jnp.int32, (clusters, clusters), 1)
    table_ref[...] = jnp.where(one == other, 1.0, 0.5 * same).astype(jnp.bfloat16)


def pack(embeddings, cluster_id, cluster_group, groups):
    rows, width = embeddings.shape
    clusters = cluster_group.shape[0]
    return pl.pallas_call(
        functools.partial(pack_kernel, groups),
        out_shape=[pltpu.VMEM((rows + AUX, width), jnp.bfloat16), pltpu.VMEM((clusters, clusters), jnp.bfloat16)],
    )(embeddings, cluster_id.reshape(1, rows), cluster_group.reshape(1, clusters))


def one_hot(digits, clusters):
    number = digits[0:1].astype(jnp.int32) + DIGIT * digits[1:2].astype(jnp.int32)
    index = lax.broadcasted_iota(jnp.int32, (clusters, digits.shape[1]), 0)
    return jnp.where(index == number, 1.0, 0.0).astype(jnp.bfloat16)


def best_kernel(n_keys, own, ranks, table_ref, *refs):
    n_queries = (len(refs) - n_keys) // 2
    keys, queries, outs = refs[:n_keys], refs[n_keys : n_keys + n_queries], refs[n_keys + n_queries :]
    rows = keys[0].shape[0] - AUX
    clusters = table_ref.shape[0]
    clu, grp = lax.axis_index("clu"), lax.axis_index("grp")
    ranks = [rank(clu, grp) for rank in ranks]

    def hot(block):
        return one_hot(block[rows:, :rows].astype(jnp.float32), clusters)

    key_hot = jnp.concatenate([hot(b) for b in keys], axis=1)
    key_rows = jnp.concatenate([b[:rows, :] for b in keys], axis=0)
    for j in range(n_queries):
        mixed = jnp.dot(table_ref[...], hot(queries[j]), preferred_element_type=jnp.float32).astype(jnp.bfloat16)
        weight = lax.dot_general(key_hot, mixed, (((0,), (0,)), ((), ())), preferred_element_type=jnp.float32)
        sims = lax.dot_general(
            key_rows, queries[j][:rows, :], (((1,), (1,)), ((), ())), preferred_element_type=jnp.float32
        )
        score = jnp.where(weight > 0, weight * sims, -1.0)
        best = jnp.full((1, rows), -1.0, jnp.float32)
        for i in range(n_keys):
            part = score[i * rows : (i + 1) * rows, :]
            if own and i + j == 0:
                k = lax.broadcasted_iota(jnp.int32, (rows, rows), 0)
                q = lax.broadcasted_iota(jnp.int32, (rows, rows), 1)
                found = jnp.max(jnp.where(k < q, part, -1.0), axis=0, keepdims=True)
            else:
                found = jnp.max(part, axis=0, keepdims=True)
                found = jnp.where(ranks[i] < ranks[n_keys + j], found, -1.0)
            best = jnp.maximum(best, found)
        outs[j][...] = best


def best_of(keys, queries, table, own):
    rows, width = keys[0][0].shape[0] - AUX, keys[0][0].shape[1]
    vmem = pl.BlockSpec(memory_space=pltpu.VMEM)
    ranks = [r for _, r in keys + queries]
    pairs = len(keys) * len(queries) * rows * rows
    return pl.pallas_call(
        functools.partial(best_kernel, len(keys), own, ranks),
        out_shape=[jax.ShapeDtypeStruct((1, rows), jnp.float32)] * len(queries),
        in_specs=[vmem] * (1 + len(keys) + len(queries)),
        out_specs=[vmem] * len(queries),
        compiler_params=pltpu.CompilerParams(vmem_limit_bytes=40 * 2**20),
        cost_estimate=pl.CostEstimate(
            flops=2 * pairs * width, bytes_accessed=2 * (len(keys) + len(queries)) * rows * width, transcendentals=0
        ),
    )(table, *[b for b, _ in keys + queries])


def solution(mesh):
    n_clu, n_grp = mesh.shape["clu"], mesh.shape["grp"]
    target = math.sqrt(n_clu * n_grp)
    wide = min(a for a in range(1, n_clu + 1) if n_clu % a == 0 and (a * n_grp >= target or a == n_clu))
    length = n_clu // wide

    def permute(x, move):
        pairs = []
        for z in range(length):
            for a in range(wide):
                for g in range(n_grp):
                    at = move(z, a, g)
                    pairs.append(((at[0] * wide + at[1]) * n_grp + at[2], (z * wide + a) * n_grp + g))
        return lax.ppermute(x, ("clu", "grp"), pairs)

    def turned(a, s, n):
        return a ^ abs(s) if n & (n - 1) == 0 else (a + s) % n

    def shards(embeddings, cluster_id, cluster_group):
        rows = embeddings.shape[0]
        own, table = pack(embeddings, cluster_id, cluster_group, n_clu)

        def rank(z=0, a=0, g=0):
            def of(clu, grp):
                line, place = turned(clu // wide, z, length), turned(clu % wide, a, wide)
                return turned(grp, g, n_grp) * n_clu + line * wide + place

            return of

        def along(x, s):
            return permute(x, lambda z, a, g: (turned(z, s, length), a, g))

        half = length // 2 if length & (length - 1) == 0 else length
        near = [permute(own, lambda z, a, g: (z, turned(a, s, wide), g)) for s in range(1, wide)]
        first = [along(own, s) for s in range(1, min(half + 1, length))]
        last = [along(first[half - 1], s) for s in range(1, length - half)]
        far, far_rank = [], []
        for t in range(1, n_grp):
            for s in range(wide):
                block = near[s - 1] if s else own
                far.append(permute(block, lambda z, a, g: (z, a, turned(g, t, n_grp))))
                far_rank.append(rank(a=s, g=t))
        near = list(zip([own] + near, [rank(a=s) for s in range(wide)]))
        far = list(zip(far, far_rank))
        visit_rank = [rank(z=s) for s in range(1, length)]
        first = list(zip(first, visit_rank))
        last = list(zip(last, visit_rank[len(first) :]))
        best = best_of(near + far, near[:1] + first + last, table, True)
        found = [along(best[s], -s) for s in reversed(range(1, length))] + [best[0]]
        return functools.reduce(jnp.maximum, found).reshape(rows)

    placed = (P(("clu", "grp"), None), P(("clu", "grp")), P())
    return jax.shard_map(
        shards, mesh=mesh, in_specs=placed, out_specs=P(("clu", "grp")), check_vma=False
    )
```

```python
import functools
import math

import jax
import jax.numpy as jnp
from jax import lax
from jax.experimental import pallas as pl
from jax.experimental.pallas import tpu as pltpu
from jax.sharding import PartitionSpec as P

AUX = 16
DIGIT = 256


def pack_kernel(groups, emb_ref, id_ref, group_ref, out_ref, table_ref):
    rows, width = emb_ref.shape
    values = emb_ref[...].astype(jnp.float32)
    scale = lax.rsqrt(jnp.sum(values * values, axis=-1, keepdims=True) + 1e-06)
    out_ref[:rows, :] = (values * scale).astype(jnp.bfloat16)
    ids = jnp.broadcast_to(id_ref[...], (AUX, rows))
    row = lax.broadcasted_iota(jnp.int32, (AUX, rows), 0)
    digits = jnp.where(row == 0, ids % DIGIT, ids // DIGIT)
    if width > rows:
        digits = jnp.concatenate([digits, jnp.zeros((AUX, width - rows), jnp.int32)], axis=1)
    out_ref[rows:, :] = digits.astype(jnp.float32).astype(jnp.bfloat16)
    clusters = group_ref.shape[1]
    index = lax.broadcasted_iota(jnp.int32, (groups, clusters), 0)
    member = jnp.where(index == group_ref[...], 1.0, 0.0).astype(jnp.bfloat16)
    same = lax.dot_general(member, member, (((0,), (0,)), ((), ())), preferred_element_type=jnp.float32)
    one = lax.broadcasted_iota(jnp.int32, (clusters, clusters), 0)
    other = lax.broadcasted_iota(jnp.int32, (clusters, clusters), 1)
    table_ref[...] = jnp.where(one == other, 1.0, 0.5 * same).astype(jnp.bfloat16)


def pack(embeddings, cluster_id, cluster_group, groups):
    rows, width = embeddings.shape
    clusters = cluster_group.shape[0]
    return pl.pallas_call(
        functools.partial(pack_kernel, groups),
        out_shape=[pltpu.VMEM((rows + AUX, width), jnp.bfloat16), pltpu.VMEM((clusters, clusters), jnp.bfloat16)],
    )(embeddings, cluster_id.reshape(1, rows), cluster_group.reshape(1, clusters))


def one_hot(digits, clusters):
    number = digits[0:1].astype(jnp.int32) + DIGIT * digits[1:2].astype(jnp.int32)
    index = lax.broadcasted_iota(jnp.int32, (clusters, digits.shape[1]), 0)
    return jnp.where(index == number, 1.0, 0.0).astype(jnp.bfloat16)


def best_kernel(n_keys, own, ranks, table_ref, *refs):
    n_queries = (len(refs) - n_keys) // 2
    keys, queries, outs = refs[:n_keys], refs[n_keys : n_keys + n_queries], refs[n_keys + n_queries :]
    rows = keys[0].shape[0] - AUX
    clusters = table_ref.shape[0]
    clu, grp = lax.axis_index("clu"), lax.axis_index("grp")
    ranks = [rank(clu, grp) for rank in ranks]

    def hot(block):
        return one_hot(block[rows:, :rows].astype(jnp.float32), clusters)

    key_hot = jnp.concatenate([hot(b) for b in keys], axis=1)
    key_rows = jnp.concatenate([b[:rows, :] for b in keys], axis=0)
    for j in range(n_queries):
        mixed = jnp.dot(table_ref[...], hot(queries[j]), preferred_element_type=jnp.float32).astype(jnp.bfloat16)
        weight = lax.dot_general(key_hot, mixed, (((0,), (0,)), ((), ())), preferred_element_type=jnp.float32)
        sims = lax.dot_general(
            key_rows, queries[j][:rows, :], (((1,), (1,)), ((), ())), preferred_element_type=jnp.float32
        )
        score = jnp.where(weight > 0, weight * sims, -1.0)
        best = jnp.full((1, rows), -1.0, jnp.float32)
        for i in range(n_keys):
            part = score[i * rows : (i + 1) * rows, :]
            if own and i + j == 0:
                k = lax.broadcasted_iota(jnp.int32, (rows, rows), 0)
                q = lax.broadcasted_iota(jnp.int32, (rows, rows), 1)
                found = jnp.max(jnp.where(k < q, part, -1.0), axis=0, keepdims=True)
            else:
                found = jnp.max(part, axis=0, keepdims=True)
                found = jnp.where(ranks[i] < ranks[n_keys + j], found, -1.0)
            best = jnp.maximum(best, found)
        outs[j][...] = best


def best_of(keys, queries, table, own):
    rows, width = keys[0][0].shape[0] - AUX, keys[0][0].shape[1]
    vmem = pl.BlockSpec(memory_space=pltpu.VMEM)
    ranks = [r for _, r in keys + queries]
    pairs = len(keys) * len(queries) * rows * rows
    return pl.pallas_call(
        functools.partial(best_kernel, len(keys), own, ranks),
        out_shape=[jax.ShapeDtypeStruct((1, rows), jnp.float32)] * len(queries),
        in_specs=[vmem] * (1 + len(keys) + len(queries)),
        out_specs=[vmem] * len(queries),
        compiler_params=pltpu.CompilerParams(vmem_limit_bytes=40 * 2**20),
        cost_estimate=pl.CostEstimate(
            flops=2 * pairs * width, bytes_accessed=2 * (len(keys) + len(queries)) * rows * width, transcendentals=0
        ),
    )(table, *[b for b, _ in keys + queries])


def solution(mesh):
    n_clu, n_grp = mesh.shape["clu"], mesh.shape["grp"]
    target = math.sqrt(n_clu * n_grp)
    wide = min(a for a in range(1, n_clu + 1) if n_clu % a == 0 and (a * n_grp >= target or a == n_clu))
    length = n_clu // wide

    def permute(x, move):
        pairs = []
        for z in range(length):
            for a in range(wide):
                for g in range(n_grp):
                    at = move(z, a, g)
                    pairs.append(((at[0] * wide + at[1]) * n_grp + at[2], (z * wide + a) * n_grp + g))
        return lax.ppermute(x, ("clu", "grp"), pairs)

    def turned(a, s, n):
        return a ^ abs(s) if n & (n - 1) == 0 else (a + s) % n

    def shards(embeddings, cluster_id, cluster_group):
        rows = embeddings.shape[0]
        own, table = pack(embeddings, cluster_id, cluster_group, n_clu)

        def rank(z=0, a=0, g=0):
            def of(clu, grp):
                line, place = turned(clu // wide, z, length), turned(clu % wide, a, wide)
                return turned(grp, g, n_grp) * n_clu + line * wide + place

            return of

        def along(x, s):
            return permute(x, lambda z, a, g: (turned(z, s, length), a, g))

        half = length // 2 if length & (length - 1) == 0 else length
        middle = along(own, length - 1) if half < length else None
        near = [permute(own, lambda z, a, g: (z, turned(a, s, wide), g)) for s in reversed(range(1, wide))]
        first = [along(own, s) for s in range(1, half)]
        middle, near, first = lax.optimization_barrier((middle, near, first))
        near = near[::-1]
        last = [along(middle, s) for s in range(1, half)] if half < length else []
        offsets = list(range(1, half))
        if half < length:
            first = first + [middle]
            offsets += [length - 1] + [(length - 1) ^ s for s in range(1, half)]
        far, far_rank = [], []
        for t in range(1, n_grp):
            for s in range(wide):
                block = near[s - 1] if s else own
                far.append(permute(block, lambda z, a, g: (z, a, turned(g, t, n_grp))))
                far_rank.append(rank(a=s, g=t))
        near = list(zip([own] + near, [rank(a=s) for s in range(wide)]))
        far = list(zip(far, far_rank))
        visit_rank = [rank(z=s) for s in offsets]
        first = list(zip(first, visit_rank))
        last = list(zip(last, visit_rank[len(first) :]))
        best = best_of(near + far, near[:1] + first, table, True)
        if last:
            best = best + best_of(near + far, last, table, False)
        found = [best[0]] + [along(b, -s) for b, s in zip(best[1:], offsets)]
        return functools.reduce(jnp.maximum, found).reshape(rows)

    placed = (P(("clu", "grp"), None), P(("clu", "grp")), P())
    return jax.shard_map(
        shards, mesh=mesh, in_specs=placed, out_specs=P(("clu", "grp")), check_vma=False
    )
```

```python
import functools
import math

import jax
import jax.numpy as jnp
from jax import lax
from jax.experimental import pallas as pl
from jax.experimental.pallas import tpu as pltpu
from jax.sharding import PartitionSpec as P

AUX = 8
DIGIT = 256


def pack_kernel(groups, emb_ref, id_ref, group_ref, out_ref, table_ref):
    rows, width = emb_ref.shape
    values = emb_ref[...].astype(jnp.float32)
    scale = lax.rsqrt(jnp.sum(values * values, axis=-1, keepdims=True) + 1e-06)
    out_ref[:rows, :] = (values * scale).astype(jnp.bfloat16)
    ids = jnp.broadcast_to(id_ref[...], (AUX, rows))
    row = lax.broadcasted_iota(jnp.int32, (AUX, rows), 0)
    digits = jnp.where(row == 0, ids % DIGIT, ids // DIGIT)
    if width > rows:
        digits = jnp.concatenate([digits, jnp.zeros((AUX, width - rows), jnp.int32)], axis=1)
    out_ref[rows:, :] = digits.astype(jnp.float32).astype(jnp.bfloat16)
    clusters = group_ref.shape[1]
    index = lax.broadcasted_iota(jnp.int32, (groups, clusters), 0)
    member = jnp.where(index == group_ref[...], 1.0, 0.0).astype(jnp.bfloat16)
    same = lax.dot_general(member, member, (((0,), (0,)), ((), ())), preferred_element_type=jnp.float32)
    one = lax.broadcasted_iota(jnp.int32, (clusters, clusters), 0)
    other = lax.broadcasted_iota(jnp.int32, (clusters, clusters), 1)
    table_ref[...] = jnp.where(one == other, 1.0, 0.5 * same).astype(jnp.bfloat16)


def pack(embeddings, cluster_id, cluster_group, groups):
    rows, width = embeddings.shape
    clusters = cluster_group.shape[0]
    return pl.pallas_call(
        functools.partial(pack_kernel, groups),
        out_shape=[pltpu.VMEM((rows + AUX, width), jnp.bfloat16), pltpu.VMEM((clusters, clusters), jnp.bfloat16)],
    )(embeddings, cluster_id.reshape(1, rows), cluster_group.reshape(1, clusters))


def one_hot(digits, clusters):
    number = digits[0:1].astype(jnp.int32) + DIGIT * digits[1:2].astype(jnp.int32)
    index = lax.broadcasted_iota(jnp.int32, (clusters, digits.shape[1]), 0)
    return jnp.where(index == number, 1.0, 0.0).astype(jnp.bfloat16)


def best_kernel(n_keys, own, ranks, table_ref, *refs):
    n_queries = (len(refs) - n_keys) // 2
    keys, queries, outs = refs[:n_keys], refs[n_keys : n_keys + n_queries], refs[n_keys + n_queries :]
    rows = keys[0].shape[0] - AUX
    clusters = table_ref.shape[0]
    clu, grp = lax.axis_index("clu"), lax.axis_index("grp")
    ranks = [rank(clu, grp) for rank in ranks]

    def hot(block):
        return one_hot(block[rows:, :rows].astype(jnp.float32), clusters)

    key_hot = jnp.concatenate([hot(b) for b in keys], axis=1)
    key_rows = jnp.concatenate([b[:rows, :] for b in keys], axis=0)
    for j in range(n_queries):
        mixed = jnp.dot(table_ref[...], hot(queries[j]), preferred_element_type=jnp.float32).astype(jnp.bfloat16)
        weight = lax.dot_general(key_hot, mixed, (((0,), (0,)), ((), ())), preferred_element_type=jnp.float32)
        sims = lax.dot_general(
            key_rows, queries[j][:rows, :], (((1,), (1,)), ((), ())), preferred_element_type=jnp.float32
        )
        score = jnp.where(weight > 0, weight * sims, -1.0)
        best = jnp.full((1, rows), -1.0, jnp.float32)
        for i in range(n_keys):
            part = score[i * rows : (i + 1) * rows, :]
            if own and i + j == 0:
                k = lax.broadcasted_iota(jnp.int32, (rows, rows), 0)
                q = lax.broadcasted_iota(jnp.int32, (rows, rows), 1)
                found = jnp.max(jnp.where(k < q, part, -1.0), axis=0, keepdims=True)
            else:
                found = jnp.max(part, axis=0, keepdims=True)
                found = jnp.where(ranks[i] < ranks[n_keys + j], found, -1.0)
            best = jnp.maximum(best, found)
        outs[j][...] = best


def best_of(keys, queries, table, own):
    rows, width = keys[0][0].shape[0] - AUX, keys[0][0].shape[1]
    vmem = pl.BlockSpec(memory_space=pltpu.VMEM)
    ranks = [r for _, r in keys + queries]
    pairs = len(keys) * len(queries) * rows * rows
    return pl.pallas_call(
        functools.partial(best_kernel, len(keys), own, ranks),
        out_shape=[jax.ShapeDtypeStruct((1, rows), jnp.float32)] * len(queries),
        in_specs=[vmem] * (1 + len(keys) + len(queries)),
        out_specs=[vmem] * len(queries),
        compiler_params=pltpu.CompilerParams(vmem_limit_bytes=40 * 2**20),
        cost_estimate=pl.CostEstimate(
            flops=2 * pairs * width, bytes_accessed=2 * (len(keys) + len(queries)) * rows * width, transcendentals=0
        ),
    )(table, *[b for b, _ in keys + queries])


def solution(mesh):
    n_clu, n_grp = mesh.shape["clu"], mesh.shape["grp"]
    target = math.sqrt(n_clu * n_grp)
    wide = min(a for a in range(1, n_clu + 1) if n_clu % a == 0 and (a * n_grp >= target or a == n_clu))
    length = n_clu // wide

    def permute(x, move):
        pairs = []
        for z in range(length):
            for a in range(wide):
                for g in range(n_grp):
                    at = move(z, a, g)
                    pairs.append(((at[0] * wide + at[1]) * n_grp + at[2], (z * wide + a) * n_grp + g))
        return lax.ppermute(x, ("clu", "grp"), pairs)

    def turned(a, s, n):
        return a ^ abs(s) if n & (n - 1) == 0 else (a + s) % n

    def shards(embeddings, cluster_id, cluster_group):
        rows = embeddings.shape[0]
        own, table = pack(embeddings, cluster_id, cluster_group, n_clu)

        def rank(z=0, a=0, g=0):
            def of(clu, grp):
                line, place = turned(clu // wide, z, length), turned(clu % wide, a, wide)
                return turned(grp, g, n_grp) * n_clu + line * wide + place

            return of

        def along(x, s):
            return permute(x, lambda z, a, g: (turned(z, s, length), a, g))

        half = length // 2 if length & (length - 1) == 0 else length
        middle = along(own, length - 1) if half < length else None
        near = [permute(own, lambda z, a, g: (z, turned(a, s, wide), g)) for s in reversed(range(1, wide))]
        first = [along(own, s) for s in range(1, half)]
        middle, near, first = lax.optimization_barrier((middle, near, first))
        near = near[::-1]
        last = [along(middle, s) for s in range(1, half)] if half < length else []
        offsets = list(range(1, half))
        if half < length:
            first = first + [middle]
            offsets += [length - 1] + [(length - 1) ^ s for s in range(1, half)]
        far, far_rank = [], []
        for t in range(1, n_grp):
            for s in range(wide):
                block = near[s - 1] if s else own
                far.append(permute(block, lambda z, a, g: (z, a, turned(g, t, n_grp))))
                far_rank.append(rank(a=s, g=t))
        near = list(zip([own] + near, [rank(a=s) for s in range(wide)]))
        far = list(zip(far, far_rank))
        visit_rank = [rank(z=s) for s in offsets]
        first = list(zip(first, visit_rank))
        last = list(zip(last, visit_rank[len(first) :]))
        best = best_of(near + far, near[:1] + first, table, True)
        if last:
            best = best + best_of(near + far, last, table, False)
        found = [best[0]] + [along(b, -s) for b, s in zip(best[1:], offsets)]
        return functools.reduce(jnp.maximum, found).reshape(rows)

    placed = (P(("clu", "grp"), None), P(("clu", "grp")), P())
    return jax.shard_map(
        shards, mesh=mesh, in_specs=placed, out_specs=P(("clu", "grp")), check_vma=False
    )
```

```python
import functools
import math

import jax
import jax.numpy as jnp
from jax import lax
from jax.experimental import pallas as pl
from jax.experimental.pallas import tpu as pltpu
from jax.sharding import PartitionSpec as P

AUX = 8
DIGIT = 256


def pack_kernel(groups, emb_ref, id_ref, group_ref, out_ref, table_ref):
    rows, width = emb_ref.shape
    values = emb_ref[...].astype(jnp.float32)
    scale = lax.rsqrt(jnp.sum(values * values, axis=-1, keepdims=True) + 1e-06)
    out_ref[:rows, :] = (values * scale).astype(jnp.bfloat16)
    ids = jnp.broadcast_to(id_ref[...], (AUX, rows))
    row = lax.broadcasted_iota(jnp.int32, (AUX, rows), 0)
    digits = jnp.where(row == 0, ids % DIGIT, ids // DIGIT)
    if width > rows:
        digits = jnp.concatenate([digits, jnp.zeros((AUX, width - rows), jnp.int32)], axis=1)
    out_ref[rows:, :] = digits.astype(jnp.float32).astype(jnp.bfloat16)
    clusters = group_ref.shape[1]
    index = lax.broadcasted_iota(jnp.int32, (groups, clusters), 0)
    member = jnp.where(index == group_ref[...], 1.0, 0.0).astype(jnp.bfloat16)
    same = lax.dot_general(member, member, (((0,), (0,)), ((), ())), preferred_element_type=jnp.float32)
    one = lax.broadcasted_iota(jnp.int32, (clusters, clusters), 0)
    other = lax.broadcasted_iota(jnp.int32, (clusters, clusters), 1)
    table_ref[...] = jnp.where(one == other, 1.0, 0.5 * same).astype(jnp.bfloat16)


def pack(embeddings, cluster_id, cluster_group, groups):
    rows, width = embeddings.shape
    clusters = cluster_group.shape[0]
    return pl.pallas_call(
        functools.partial(pack_kernel, groups),
        out_shape=[pltpu.VMEM((rows + AUX, width), jnp.bfloat16), pltpu.VMEM((clusters, clusters), jnp.bfloat16)],
    )(embeddings, cluster_id.reshape(1, rows), cluster_group.reshape(1, clusters))


def one_hot(digits, clusters):
    number = digits[0:1].astype(jnp.int32) + DIGIT * digits[1:2].astype(jnp.int32)
    index = lax.broadcasted_iota(jnp.int32, (clusters, digits.shape[1]), 0)
    return jnp.where(index == number, 1.0, 0.0).astype(jnp.bfloat16)


def best_kernel(n_keys, own, ranks, table_ref, *refs):
    n_queries = (len(refs) - n_keys) // 2
    keys, queries, outs = refs[:n_keys], refs[n_keys : n_keys + n_queries], refs[n_keys + n_queries :]
    rows = keys[0].shape[0] - AUX
    clusters = table_ref.shape[0]
    clu, grp = lax.axis_index("clu"), lax.axis_index("grp")
    ranks = [rank(clu, grp) for rank in ranks]

    def hot(block):
        return one_hot(block[rows:, :rows].astype(jnp.float32), clusters)

    key_hot = jnp.concatenate([hot(b) for b in keys], axis=1)
    key_rows = jnp.concatenate([b[:rows, :] for b in keys], axis=0)
    for j in range(n_queries):
        mixed = jnp.dot(table_ref[...], hot(queries[j]), preferred_element_type=jnp.float32).astype(jnp.bfloat16)
        weight = lax.dot_general(key_hot, mixed, (((0,), (0,)), ((), ())), preferred_element_type=jnp.float32)
        sims = lax.dot_general(
            key_rows, queries[j][:rows, :], (((1,), (1,)), ((), ())), preferred_element_type=jnp.float32
        )
        score = jnp.where(weight > 0, weight * sims, -1.0)
        best = jnp.full((1, rows), -1.0, jnp.float32)
        for i in range(n_keys):
            part = score[i * rows : (i + 1) * rows, :]
            if own and i + j == 0:
                k = lax.broadcasted_iota(jnp.int32, (rows, rows), 0)
                q = lax.broadcasted_iota(jnp.int32, (rows, rows), 1)
                found = jnp.max(jnp.where(k < q, part, -1.0), axis=0, keepdims=True)
            else:
                found = jnp.max(part, axis=0, keepdims=True)
                found = jnp.where(ranks[i] < ranks[n_keys + j], found, -1.0)
            best = jnp.maximum(best, found)
        outs[j][...] = best


def best_of(keys, queries, table, own):
    rows, width = keys[0][0].shape[0] - AUX, keys[0][0].shape[1]
    vmem = pl.BlockSpec(memory_space=pltpu.VMEM)
    ranks = [r for _, r in keys + queries]
    pairs = len(keys) * len(queries) * rows * rows
    return pl.pallas_call(
        functools.partial(best_kernel, len(keys), own, ranks),
        out_shape=[jax.ShapeDtypeStruct((1, rows), jnp.float32)] * len(queries),
        in_specs=[vmem] * (1 + len(keys) + len(queries)),
        out_specs=[vmem] * len(queries),
        compiler_params=pltpu.CompilerParams(vmem_limit_bytes=40 * 2**20),
        cost_estimate=pl.CostEstimate(
            flops=2 * pairs * width, bytes_accessed=2 * (len(keys) + len(queries)) * rows * width, transcendentals=0
        ),
    )(table, *[b for b, _ in keys + queries])


def solution(mesh):
    n_clu, n_grp = mesh.shape["clu"], mesh.shape["grp"]
    target = math.sqrt(n_clu * n_grp)
    wide = min(a for a in range(1, n_clu + 1) if n_clu % a == 0 and (a * n_grp >= target or a == n_clu))
    length = n_clu // wide

    def permute(x, move):
        pairs = []
        for z in range(length):
            for a in range(wide):
                for g in range(n_grp):
                    at = move(z, a, g)
                    pairs.append(((at[0] * wide + at[1]) * n_grp + at[2], (z * wide + a) * n_grp + g))
        return lax.ppermute(x, ("clu", "grp"), pairs)

    def turned(a, s, n):
        return a ^ abs(s) if n & (n - 1) == 0 else (a + s) % n

    def shards(embeddings, cluster_id, cluster_group):
        rows = embeddings.shape[0]
        own, table = pack(embeddings, cluster_id, cluster_group, n_clu)

        def rank(z=0, a=0, g=0):
            def of(clu, grp):
                line, place = turned(clu // wide, z, length), turned(clu % wide, a, wide)
                return turned(grp, g, n_grp) * n_clu + line * wide + place

            return of

        def along(x, s):
            return permute(x, lambda z, a, g: (turned(z, s, length), a, g))

        half = length // 2 if length & (length - 1) == 0 else length
        direct = list(range(1, half)) + ([length - 1] if half < length else [])
        onward = [s for s in range(1, half) if half < length]
        offsets = direct + [(length - 1) ^ s for s in onward]
        near = [permute(own, lambda z, a, g: (z, turned(a, s, wide), g)) for s in range(1, wide)]
        first = [along(own, s) for s in direct]
        last = [along(first[-1], s) for s in onward]
        far, far_rank = [], []
        for t in range(1, n_grp):
            for s in range(wide):
                block = near[s - 1] if s else own
                far.append(permute(block, lambda z, a, g: (z, a, turned(g, t, n_grp))))
                far_rank.append(rank(a=s, g=t))
        near = list(zip([own] + near, [rank(a=s) for s in range(wide)]))
        far = list(zip(far, far_rank))
        visit_rank = [rank(z=s) for s in offsets]
        first = list(zip(first, visit_rank))
        last = list(zip(last, visit_rank[len(first) :]))
        best = best_of(near + far, near[:1] + first + last, table, True)
        back = sorted(zip(offsets, best[1:]), key=lambda pair: -pair[0])
        found = [along(b, -s) for s, b in back] + [best[0]]
        return functools.reduce(jnp.maximum, found).reshape(rows)

    placed = (P(("clu", "grp"), None), P(("clu", "grp")), P())
    return jax.shard_map(
        shards, mesh=mesh, in_specs=placed, out_specs=P(("clu", "grp")), check_vma=False
    )
```

```python
import functools
import math

import jax
import jax.numpy as jnp
from jax import lax
from jax.experimental import pallas as pl
from jax.experimental.pallas import tpu as pltpu
from jax.sharding import PartitionSpec as P

AUX = 8
DIGIT = 256


def pack_kernel(groups, emb_ref, id_ref, group_ref, out_ref, table_ref):
    rows, width = emb_ref.shape
    values = emb_ref[...].astype(jnp.float32)
    scale = lax.rsqrt(jnp.sum(values * values, axis=-1, keepdims=True) + 1e-06)
    out_ref[:rows, :] = (values * scale).astype(jnp.bfloat16)
    ids = jnp.broadcast_to(id_ref[...], (AUX, rows))
    row = lax.broadcasted_iota(jnp.int32, (AUX, rows), 0)
    digits = jnp.where(row == 0, ids % DIGIT, ids // DIGIT)
    if width > rows:
        digits = jnp.concatenate([digits, jnp.zeros((AUX, width - rows), jnp.int32)], axis=1)
    out_ref[rows:, :] = digits.astype(jnp.float32).astype(jnp.bfloat16)
    clusters = group_ref.shape[1]
    index = lax.broadcasted_iota(jnp.int32, (groups, clusters), 0)
    member = jnp.where(index == group_ref[...], 1.0, 0.0).astype(jnp.bfloat16)
    same = lax.dot_general(member, member, (((0,), (0,)), ((), ())), preferred_element_type=jnp.float32)
    one = lax.broadcasted_iota(jnp.int32, (clusters, clusters), 0)
    other = lax.broadcasted_iota(jnp.int32, (clusters, clusters), 1)
    table_ref[...] = jnp.where(one == other, 1.0, 0.5 * same).astype(jnp.bfloat16)


def pack(embeddings, cluster_id, cluster_group, groups):
    rows, width = embeddings.shape
    clusters = cluster_group.shape[0]
    return pl.pallas_call(
        functools.partial(pack_kernel, groups),
        out_shape=[pltpu.VMEM((rows + AUX, width), jnp.bfloat16), pltpu.VMEM((clusters, clusters), jnp.bfloat16)],
    )(embeddings, cluster_id.reshape(1, rows), cluster_group.reshape(1, clusters))


def one_hot(digits, clusters):
    number = digits[0:1].astype(jnp.int32) + DIGIT * digits[1:2].astype(jnp.int32)
    index = lax.broadcasted_iota(jnp.int32, (clusters, digits.shape[1]), 0)
    return jnp.where(index == number, 1.0, 0.0).astype(jnp.bfloat16)


def best_kernel(n_keys, own, ranks, table_ref, *refs):
    n_queries = (len(refs) - n_keys) // 2
    keys, queries, outs = refs[:n_keys], refs[n_keys : n_keys + n_queries], refs[n_keys + n_queries :]
    rows = keys[0].shape[0] - AUX
    clusters = table_ref.shape[0]
    clu, grp = lax.axis_index("clu"), lax.axis_index("grp")
    ranks = [rank(clu, grp) for rank in ranks]

    def hot(block):
        return one_hot(block[rows:, :rows].astype(jnp.float32), clusters)

    key_hot = jnp.concatenate([hot(b) for b in keys], axis=1)
    key_rows = jnp.concatenate([b[:rows, :] for b in keys], axis=0)
    for j in range(n_queries):
        mixed = jnp.dot(table_ref[...], hot(queries[j]), preferred_element_type=jnp.float32).astype(jnp.bfloat16)
        weight = lax.dot_general(key_hot, mixed, (((0,), (0,)), ((), ())), preferred_element_type=jnp.float32)
        sims = lax.dot_general(
            key_rows, queries[j][:rows, :], (((1,), (1,)), ((), ())), preferred_element_type=jnp.float32
        )
        score = jnp.where(weight > 0, weight * sims, -1.0)
        best = jnp.full((1, rows), -1.0, jnp.float32)
        for i in range(n_keys):
            part = score[i * rows : (i + 1) * rows, :]
            if own and i + j == 0:
                k = lax.broadcasted_iota(jnp.int32, (rows, rows), 0)
                q = lax.broadcasted_iota(jnp.int32, (rows, rows), 1)
                found = jnp.max(jnp.where(k < q, part, -1.0), axis=0, keepdims=True)
            else:
                found = jnp.max(part, axis=0, keepdims=True)
                found = jnp.where(ranks[i] < ranks[n_keys + j], found, -1.0)
            best = jnp.maximum(best, found)
        outs[j][...] = best


def best_of(keys, queries, table, own):
    rows, width = keys[0][0].shape[0] - AUX, keys[0][0].shape[1]
    vmem = pl.BlockSpec(memory_space=pltpu.VMEM)
    ranks = [r for _, r in keys + queries]
    pairs = len(keys) * len(queries) * rows * rows
    return pl.pallas_call(
        functools.partial(best_kernel, len(keys), own, ranks),
        out_shape=[jax.ShapeDtypeStruct((1, rows), jnp.float32)] * len(queries),
        in_specs=[vmem] * (1 + len(keys) + len(queries)),
        out_specs=[vmem] * len(queries),
        compiler_params=pltpu.CompilerParams(vmem_limit_bytes=40 * 2**20),
        cost_estimate=pl.CostEstimate(
            flops=2 * pairs * width, bytes_accessed=2 * (len(keys) + len(queries)) * rows * width, transcendentals=0
        ),
    )(table, *[b for b, _ in keys + queries])


def solution(mesh):
    n_clu, n_grp = mesh.shape["clu"], mesh.shape["grp"]
    target = math.sqrt(n_clu * n_grp)
    wide = min(a for a in range(1, n_clu + 1) if n_clu % a == 0 and (a * n_grp >= target or a == n_clu))
    length = n_clu // wide

    def permute(x, move):
        pairs = []
        for z in range(length):
            for a in range(wide):
                for g in range(n_grp):
                    at = move(z, a, g)
                    pairs.append(((at[0] * wide + at[1]) * n_grp + at[2], (z * wide + a) * n_grp + g))
        return lax.ppermute(x, ("clu", "grp"), pairs)

    def turned(a, s, n):
        return a ^ abs(s) if n & (n - 1) == 0 else (a + s) % n

    def shards(embeddings, cluster_id, cluster_group):
        rows = embeddings.shape[0]
        own, table = pack(embeddings, cluster_id, cluster_group, n_clu)

        def rank(z=0, a=0, g=0):
            def of(clu, grp):
                line, place = turned(clu // wide, z, length), turned(clu % wide, a, wide)
                return turned(grp, g, n_grp) * n_clu + line * wide + place

            return of

        def along(x, s):
            return permute(x, lambda z, a, g: (turned(z, s, length), a, g))

        half = length // 2 if length & (length - 1) == 0 else length
        direct = list(range(1, half)) + ([length - 1] if half < length else [])
        onward = [s for s in range(1, half) if half < length]
        offsets = direct + [(length - 1) ^ s for s in onward]
        near = [permute(own, lambda z, a, g: (z, turned(a, s, wide), g)) for s in range(1, wide)]
        first = [along(own, s) for s in direct]
        last = [along(first[-1], s) for s in onward]
        near[0], mine = lax.optimization_barrier((near[0], own))
        far, far_rank = [], []
        for t in range(1, n_grp):
            for s in range(wide):
                block = near[s - 1] if s else mine
                far.append(permute(block, lambda z, a, g: (z, a, turned(g, t, n_grp))))
                far_rank.append(rank(a=s, g=t))
        near = list(zip([own] + near, [rank(a=s) for s in range(wide)]))
        far = list(zip(far, far_rank))
        visit_rank = [rank(z=s) for s in offsets]
        first = list(zip(first, visit_rank))
        last = list(zip(last, visit_rank[len(first) :]))
        best = best_of(near + far, near[:1] + first + last, table, True)
        back = sorted(zip(offsets, best[1:]), key=lambda pair: -pair[0])
        found = [along(b, -s) for s, b in back] + [best[0]]
        return functools.reduce(jnp.maximum, found).reshape(rows)

    placed = (P(("clu", "grp"), None), P(("clu", "grp")), P())
    return jax.shard_map(
        shards, mesh=mesh, in_specs=placed, out_specs=P(("clu", "grp")), check_vma=False
    )
```

```python
import functools
import math

import jax
import jax.numpy as jnp
from jax import lax
from jax.experimental import pallas as pl
from jax.experimental.pallas import tpu as pltpu
from jax.sharding import PartitionSpec as P

AUX = 8
DIGIT = 256


def pack_kernel(groups, emb_ref, id_ref, group_ref, out_ref, table_ref):
    rows, width = emb_ref.shape
    values = emb_ref[...].astype(jnp.float32)
    scale = lax.rsqrt(jnp.sum(values * values, axis=-1, keepdims=True) + 1e-06)
    out_ref[:rows, :] = (values * scale).astype(jnp.bfloat16)
    ids = jnp.broadcast_to(id_ref[...], (AUX, rows))
    row = lax.broadcasted_iota(jnp.int32, (AUX, rows), 0)
    digits = jnp.where(row == 0, ids % DIGIT, ids // DIGIT)
    if width > rows:
        digits = jnp.concatenate([digits, jnp.zeros((AUX, width - rows), jnp.int32)], axis=1)
    out_ref[rows:, :] = digits.astype(jnp.float32).astype(jnp.bfloat16)
    clusters = group_ref.shape[1]
    index = lax.broadcasted_iota(jnp.int32, (groups, clusters), 0)
    member = jnp.where(index == group_ref[...], 1.0, 0.0).astype(jnp.bfloat16)
    same = lax.dot_general(member, member, (((0,), (0,)), ((), ())), preferred_element_type=jnp.float32)
    one = lax.broadcasted_iota(jnp.int32, (clusters, clusters), 0)
    other = lax.broadcasted_iota(jnp.int32, (clusters, clusters), 1)
    table_ref[...] = jnp.where(one == other, 1.0, 0.5 * same).astype(jnp.bfloat16)


def pack(embeddings, cluster_id, cluster_group, groups):
    rows, width = embeddings.shape
    clusters = cluster_group.shape[0]
    return pl.pallas_call(
        functools.partial(pack_kernel, groups),
        out_shape=[pltpu.VMEM((rows + AUX, width), jnp.bfloat16), pltpu.VMEM((clusters, clusters), jnp.bfloat16)],
    )(embeddings, cluster_id.reshape(1, rows), cluster_group.reshape(1, clusters))


def one_hot(digits, clusters):
    number = digits[0:1].astype(jnp.int32) + DIGIT * digits[1:2].astype(jnp.int32)
    index = lax.broadcasted_iota(jnp.int32, (clusters, digits.shape[1]), 0)
    return jnp.where(index == number, 1.0, 0.0).astype(jnp.bfloat16)


def best_kernel(n_keys, own, ranks, table_ref, *refs):
    n_queries = (len(refs) - n_keys) // 2
    keys, queries, outs = refs[:n_keys], refs[n_keys : n_keys + n_queries], refs[n_keys + n_queries :]
    rows = keys[0].shape[0] - AUX
    clusters = table_ref.shape[0]
    clu, grp = lax.axis_index("clu"), lax.axis_index("grp")
    ranks = [rank(clu, grp) for rank in ranks]

    def hot(block):
        return one_hot(block[rows:, :rows].astype(jnp.float32), clusters)

    key_hot = jnp.concatenate([hot(b) for b in keys], axis=1)
    key_rows = jnp.concatenate([b[:rows, :] for b in keys], axis=0)
    for j in range(n_queries):
        mixed = jnp.dot(table_ref[...], hot(queries[j]), preferred_element_type=jnp.float32).astype(jnp.bfloat16)
        weight = lax.dot_general(key_hot, mixed, (((0,), (0,)), ((), ())), preferred_element_type=jnp.float32)
        sims = lax.dot_general(
            key_rows, queries[j][:rows, :], (((1,), (1,)), ((), ())), preferred_element_type=jnp.float32
        )
        score = jnp.where(weight > 0, weight * sims, -1.0)
        best = jnp.full((1, rows), -1.0, jnp.float32)
        for i in range(n_keys):
            part = score[i * rows : (i + 1) * rows, :]
            if own and i + j == 0:
                k = lax.broadcasted_iota(jnp.int32, (rows, rows), 0)
                q = lax.broadcasted_iota(jnp.int32, (rows, rows), 1)
                found = jnp.max(jnp.where(k < q, part, -1.0), axis=0, keepdims=True)
            else:
                found = jnp.max(part, axis=0, keepdims=True)
                found = jnp.where(ranks[i] < ranks[n_keys + j], found, -1.0)
            best = jnp.maximum(best, found)
        outs[j][...] = best


def best_of(keys, queries, table, own):
    rows, width = keys[0][0].shape[0] - AUX, keys[0][0].shape[1]
    vmem = pl.BlockSpec(memory_space=pltpu.VMEM)
    ranks = [r for _, r in keys + queries]
    pairs = len(keys) * len(queries) * rows * rows
    return pl.pallas_call(
        functools.partial(best_kernel, len(keys), own, ranks),
        out_shape=[jax.ShapeDtypeStruct((1, rows), jnp.float32)] * len(queries),
        in_specs=[vmem] * (1 + len(keys) + len(queries)),
        out_specs=[vmem] * len(queries),
        compiler_params=pltpu.CompilerParams(vmem_limit_bytes=40 * 2**20),
        cost_estimate=pl.CostEstimate(
            flops=2 * pairs * width, bytes_accessed=2 * (len(keys) + len(queries)) * rows * width, transcendentals=0
        ),
    )(table, *[b for b, _ in keys + queries])


def solution(mesh):
    n_clu, n_grp = mesh.shape["clu"], mesh.shape["grp"]
    target = math.sqrt(n_clu * n_grp)
    wide = min(a for a in range(1, n_clu + 1) if n_clu % a == 0 and (a * n_grp >= target or a == n_clu))
    length = n_clu // wide

    def permute(x, move):
        pairs = []
        for z in range(length):
            for a in range(wide):
                for g in range(n_grp):
                    at = move(z, a, g)
                    pairs.append(((at[0] * wide + at[1]) * n_grp + at[2], (z * wide + a) * n_grp + g))
        return lax.ppermute(x, ("clu", "grp"), pairs)

    def turned(a, s, n):
        return a ^ abs(s) if n & (n - 1) == 0 else (a + s) % n

    def shards(embeddings, cluster_id, cluster_group):
        rows = embeddings.shape[0]
        own, table = pack(embeddings, cluster_id, cluster_group, n_clu)

        def rank(z=0, a=0, g=0):
            def of(clu, grp):
                line, place = turned(clu // wide, z, length), turned(clu % wide, a, wide)
                return turned(grp, g, n_grp) * n_clu + line * wide + place

            return of

        def along(x, s):
            return permute(x, lambda z, a, g: (turned(z, s, length), a, g))

        half = length // 2 if length & (length - 1) == 0 else length
        direct = list(range(1, half)) + ([length - 1] if half < length else [])
        onward = [s for s in range(1, half) if half < length]
        offsets = direct + [(length - 1) ^ s for s in onward]
        near = [permute(own, lambda z, a, g: (z, turned(a, s, wide), g)) for s in range(1, wide)]
        first = [along(own, s) for s in direct]
        last = [
            permute(first[-1], lambda z, a, g: (turned(z, s, length) if g or z < half else z, a, g)) for s in onward
        ]
        near[0], mine = lax.optimization_barrier((near[0], own))
        far, far_rank = [], []
        for t in range(1, n_grp):
            for s in range(wide):
                block = near[s - 1] if s else mine
                far.append(permute(block, lambda z, a, g: (z, a, turned(g, t, n_grp))))
                far_rank.append(rank(a=s, g=t))
        near = list(zip([own] + near, [rank(a=s) for s in range(wide)]))
        far = list(zip(far, far_rank))
        visit_rank = [rank(z=s) for s in offsets]
        first = list(zip(first, visit_rank))
        last = list(zip(last, visit_rank[len(first) :]))
        best = best_of(near + far, near[:1] + first + last, table, True)
        back = sorted(zip(offsets, best[1:]), key=lambda pair: -pair[0])
        found = [along(b, -s) for s, b in back] + [best[0]]
        return functools.reduce(jnp.maximum, found).reshape(rows)

    placed = (P(("clu", "grp"), None), P(("clu", "grp")), P())
    return jax.shard_map(
        shards, mesh=mesh, in_specs=placed, out_specs=P(("clu", "grp")), check_vma=False
    )
```

```python
import functools
import math

import jax
import jax.numpy as jnp
from jax import lax
from jax.experimental import pallas as pl
from jax.experimental.pallas import tpu as pltpu
from jax.sharding import PartitionSpec as P

AUX = 8
DIGIT = 256


def pack_kernel(groups, emb_ref, id_ref, group_ref, out_ref, table_ref):
    rows, width = emb_ref.shape
    values = emb_ref[...].astype(jnp.float32)
    scale = lax.rsqrt(jnp.sum(values * values, axis=-1, keepdims=True) + 1e-06)
    out_ref[:rows, :] = (values * scale).astype(jnp.bfloat16)
    ids = jnp.broadcast_to(id_ref[...], (AUX, rows))
    row = lax.broadcasted_iota(jnp.int32, (AUX, rows), 0)
    digits = jnp.where(row == 0, ids % DIGIT, ids // DIGIT)
    if width > rows:
        digits = jnp.concatenate([digits, jnp.zeros((AUX, width - rows), jnp.int32)], axis=1)
    out_ref[rows:, :] = digits.astype(jnp.float32).astype(jnp.bfloat16)
    clusters = group_ref.shape[1]
    index = lax.broadcasted_iota(jnp.int32, (groups, clusters), 0)
    member = jnp.where(index == group_ref[...], 1.0, 0.0).astype(jnp.bfloat16)
    same = lax.dot_general(member, member, (((0,), (0,)), ((), ())), preferred_element_type=jnp.float32)
    one = lax.broadcasted_iota(jnp.int32, (clusters, clusters), 0)
    other = lax.broadcasted_iota(jnp.int32, (clusters, clusters), 1)
    table_ref[...] = jnp.where(one == other, 1.0, 0.5 * same).astype(jnp.bfloat16)


def pack(embeddings, cluster_id, cluster_group, groups):
    rows, width = embeddings.shape
    clusters = cluster_group.shape[0]
    return pl.pallas_call(
        functools.partial(pack_kernel, groups),
        out_shape=[pltpu.VMEM((rows + AUX, width), jnp.bfloat16), pltpu.VMEM((clusters, clusters), jnp.bfloat16)],
    )(embeddings, cluster_id.reshape(1, rows), cluster_group.reshape(1, clusters))


def one_hot(digits, clusters):
    number = digits[0:1].astype(jnp.int32) + DIGIT * digits[1:2].astype(jnp.int32)
    index = lax.broadcasted_iota(jnp.int32, (clusters, digits.shape[1]), 0)
    return jnp.where(index == number, 1.0, 0.0).astype(jnp.bfloat16)


def best_kernel(n_keys, own, ranks, table_ref, *refs):
    n_queries = (len(refs) - n_keys) // 2
    keys, queries, outs = refs[:n_keys], refs[n_keys : n_keys + n_queries], refs[n_keys + n_queries :]
    rows = keys[0].shape[0] - AUX
    clusters = table_ref.shape[0]
    clu, grp = lax.axis_index("clu"), lax.axis_index("grp")
    ranks = [rank(clu, grp) for rank in ranks]

    def hot(block):
        return one_hot(block[rows:, :rows].astype(jnp.float32), clusters)

    key_hot = jnp.concatenate([hot(b) for b in keys], axis=1)
    key_rows = jnp.concatenate([b[:rows, :] for b in keys], axis=0)
    for j in range(n_queries):
        mixed = jnp.dot(table_ref[...], hot(queries[j]), preferred_element_type=jnp.float32).astype(jnp.bfloat16)
        weight = lax.dot_general(key_hot, mixed, (((0,), (0,)), ((), ())), preferred_element_type=jnp.float32)
        sims = lax.dot_general(
            key_rows, queries[j][:rows, :], (((1,), (1,)), ((), ())), preferred_element_type=jnp.float32
        )
        score = jnp.where(weight > 0, weight * sims, -1.0)
        best = jnp.full((1, rows), -1.0, jnp.float32)
        for i in range(n_keys):
            part = score[i * rows : (i + 1) * rows, :]
            if own and i + j == 0:
                k = lax.broadcasted_iota(jnp.int32, (rows, rows), 0)
                q = lax.broadcasted_iota(jnp.int32, (rows, rows), 1)
                found = jnp.max(jnp.where(k < q, part, -1.0), axis=0, keepdims=True)
            else:
                found = jnp.max(part, axis=0, keepdims=True)
                found = jnp.where(ranks[i] < ranks[n_keys + j], found, -1.0)
            best = jnp.maximum(best, found)
        outs[j][...] = best


def best_of(keys, queries, table, own):
    rows, width = keys[0][0].shape[0] - AUX, keys[0][0].shape[1]
    vmem = pl.BlockSpec(memory_space=pltpu.VMEM)
    ranks = [r for _, r in keys + queries]
    pairs = len(keys) * len(queries) * rows * rows
    return pl.pallas_call(
        functools.partial(best_kernel, len(keys), own, ranks),
        out_shape=[jax.ShapeDtypeStruct((1, rows), jnp.float32)] * len(queries),
        in_specs=[vmem] * (1 + len(keys) + len(queries)),
        out_specs=[vmem] * len(queries),
        compiler_params=pltpu.CompilerParams(vmem_limit_bytes=40 * 2**20),
        cost_estimate=pl.CostEstimate(
            flops=2 * pairs * width, bytes_accessed=2 * (len(keys) + len(queries)) * rows * width, transcendentals=0
        ),
    )(table, *[b for b, _ in keys + queries])


def solution(mesh):
    n_clu, n_grp = mesh.shape["clu"], mesh.shape["grp"]
    target = math.sqrt(n_clu * n_grp)
    wide = min(a for a in range(1, n_clu + 1) if n_clu % a == 0 and (a * n_grp >= target or a == n_clu))
    length = n_clu // wide

    def permute(x, move):
        pairs = []
        for z in range(length):
            for a in range(wide):
                for g in range(n_grp):
                    at = move(z, a, g)
                    pairs.append(((at[0] * wide + at[1]) * n_grp + at[2], (z * wide + a) * n_grp + g))
        return lax.ppermute(x, ("clu", "grp"), pairs)

    def turned(a, s, n):
        return a ^ abs(s) if n & (n - 1) == 0 else (a + s) % n

    def shards(embeddings, cluster_id, cluster_group):
        rows = embeddings.shape[0]
        own, table = pack(embeddings, cluster_id, cluster_group, n_clu)

        def rank(z=0, a=0, g=0):
            def of(clu, grp):
                line, place = turned(clu // wide, z, length), turned(clu % wide, a, wide)
                return turned(grp, g, n_grp) * n_clu + line * wide + place

            return of

        def along(x, s):
            return permute(x, lambda z, a, g: (turned(z, s, length), a, g))

        half = length // 2 if length & (length - 1) == 0 else length
        near = [permute(own, lambda z, a, g: (z, turned(a, s, wide), g)) for s in reversed(range(1, wide))]
        middle = along(own, length - 1) if half < length else None
        first = [along(own, s) for s in range(1, half)]
        near, middle, first = lax.optimization_barrier((near, middle, first))
        near = near[::-1]
        last = [along(middle, s) for s in range(1, half)] if half < length else []
        offsets = list(range(1, half))
        if half < length:
            first = first + [middle]
            offsets += [length - 1] + [(length - 1) ^ s for s in range(1, half)]
        far, far_rank = [], []
        for t in range(1, n_grp):
            for s in range(wide):
                block = near[s - 1] if s else own
                far.append(permute(block, lambda z, a, g: (z, a, turned(g, t, n_grp))))
                far_rank.append(rank(a=s, g=t))
        near = list(zip([own] + near, [rank(a=s) for s in range(wide)]))
        far = list(zip(far, far_rank))
        visit_rank = [rank(z=s) for s in offsets]
        first = list(zip(first, visit_rank))
        last = list(zip(last, visit_rank[len(first) :]))
        best = best_of(near + far, near[:1] + first, table, True)
        if last:
            best = best + best_of(near + far, last, table, False)
        found = [best[0]] + [along(b, -s) for b, s in zip(best[1:], offsets)]
        return functools.reduce(jnp.maximum, found).reshape(rows)

    placed = (P(("clu", "grp"), None), P(("clu", "grp")), P())
    return jax.shard_map(
        shards, mesh=mesh, in_specs=placed, out_specs=P(("clu", "grp")), check_vma=False
    )
```

```python
import functools
import math

import jax
import jax.numpy as jnp
from jax import lax
from jax.experimental import pallas as pl
from jax.experimental.pallas import tpu as pltpu
from jax.sharding import PartitionSpec as P

AUX = 8
DIGIT = 256


def pack_kernel(groups, emb_ref, id_ref, group_ref, out_ref, table_ref):
    rows, width = emb_ref.shape
    values = emb_ref[...].astype(jnp.float32)
    scale = lax.rsqrt(jnp.sum(values * values, axis=-1, keepdims=True) + 1e-06)
    out_ref[:rows, :] = (values * scale).astype(jnp.bfloat16)
    ids = jnp.broadcast_to(id_ref[...], (AUX, rows))
    row = lax.broadcasted_iota(jnp.int32, (AUX, rows), 0)
    digits = jnp.where(row == 0, ids % DIGIT, ids // DIGIT)
    if width > rows:
        digits = jnp.concatenate([digits, jnp.zeros((AUX, width - rows), jnp.int32)], axis=1)
    out_ref[rows:, :] = digits.astype(jnp.float32).astype(jnp.bfloat16)
    clusters = group_ref.shape[1]
    index = lax.broadcasted_iota(jnp.int32, (groups, clusters), 0)
    member = jnp.where(index == group_ref[...], 1.0, 0.0).astype(jnp.bfloat16)
    same = lax.dot_general(member, member, (((0,), (0,)), ((), ())), preferred_element_type=jnp.float32)
    one = lax.broadcasted_iota(jnp.int32, (clusters, clusters), 0)
    other = lax.broadcasted_iota(jnp.int32, (clusters, clusters), 1)
    table_ref[...] = jnp.where(one == other, 1.0, 0.5 * same).astype(jnp.bfloat16)


def pack(embeddings, cluster_id, cluster_group, groups):
    rows, width = embeddings.shape
    clusters = cluster_group.shape[0]
    return pl.pallas_call(
        functools.partial(pack_kernel, groups),
        out_shape=[pltpu.VMEM((rows + AUX, width), jnp.bfloat16), pltpu.VMEM((clusters, clusters), jnp.bfloat16)],
    )(embeddings, cluster_id.reshape(1, rows), cluster_group.reshape(1, clusters))


def one_hot(digits, clusters):
    number = digits[0:1].astype(jnp.int32) + DIGIT * digits[1:2].astype(jnp.int32)
    index = lax.broadcasted_iota(jnp.int32, (clusters, digits.shape[1]), 0)
    return jnp.where(index == number, 1.0, 0.0).astype(jnp.bfloat16)


def best_kernel(n_keys, own, ranks, table_ref, *refs):
    n_queries = (len(refs) - n_keys) // 2
    keys, queries, outs = refs[:n_keys], refs[n_keys : n_keys + n_queries], refs[n_keys + n_queries :]
    rows = keys[0].shape[0] - AUX
    clusters = table_ref.shape[0]
    clu, grp = lax.axis_index("clu"), lax.axis_index("grp")
    ranks = [rank(clu, grp) for rank in ranks]

    def hot(block):
        return one_hot(block[rows:, :rows].astype(jnp.float32), clusters)

    key_hot = jnp.concatenate([hot(b) for b in keys], axis=1)
    key_rows = jnp.concatenate([b[:rows, :] for b in keys], axis=0)
    for j in range(n_queries):
        mixed = jnp.dot(table_ref[...], hot(queries[j]), preferred_element_type=jnp.float32).astype(jnp.bfloat16)
        weight = lax.dot_general(key_hot, mixed, (((0,), (0,)), ((), ())), preferred_element_type=jnp.float32)
        sims = lax.dot_general(
            key_rows, queries[j][:rows, :], (((1,), (1,)), ((), ())), preferred_element_type=jnp.float32
        )
        score = jnp.where(weight > 0, weight * sims, -1.0)
        best = jnp.full((1, rows), -1.0, jnp.float32)
        for i in range(n_keys):
            part = score[i * rows : (i + 1) * rows, :]
            if own and i + j == 0:
                k = lax.broadcasted_iota(jnp.int32, (rows, rows), 0)
                q = lax.broadcasted_iota(jnp.int32, (rows, rows), 1)
                found = jnp.max(jnp.where(k < q, part, -1.0), axis=0, keepdims=True)
            else:
                found = jnp.max(part, axis=0, keepdims=True)
                found = jnp.where(ranks[i] < ranks[n_keys + j], found, -1.0)
            best = jnp.maximum(best, found)
        outs[j][...] = best


def best_of(keys, queries, table, own):
    rows, width = keys[0][0].shape[0] - AUX, keys[0][0].shape[1]
    vmem = pl.BlockSpec(memory_space=pltpu.VMEM)
    ranks = [r for _, r in keys + queries]
    pairs = len(keys) * len(queries) * rows * rows
    return pl.pallas_call(
        functools.partial(best_kernel, len(keys), own, ranks),
        out_shape=[jax.ShapeDtypeStruct((1, rows), jnp.float32)] * len(queries),
        in_specs=[vmem] * (1 + len(keys) + len(queries)),
        out_specs=[vmem] * len(queries),
        compiler_params=pltpu.CompilerParams(vmem_limit_bytes=40 * 2**20),
        cost_estimate=pl.CostEstimate(
            flops=2 * pairs * width, bytes_accessed=2 * (len(keys) + len(queries)) * rows * width, transcendentals=0
        ),
    )(table, *[b for b, _ in keys + queries])


def solution(mesh):
    n_clu, n_grp = mesh.shape["clu"], mesh.shape["grp"]
    target = math.sqrt(n_clu * n_grp)
    wide = min(a for a in range(1, n_clu + 1) if n_clu % a == 0 and (a * n_grp >= target or a == n_clu))
    length = n_clu // wide

    def permute(x, move):
        pairs = []
        for z in range(length):
            for a in range(wide):
                for g in range(n_grp):
                    at = move(z, a, g)
                    pairs.append(((at[0] * wide + at[1]) * n_grp + at[2], (z * wide + a) * n_grp + g))
        return lax.ppermute(x, ("clu", "grp"), pairs)

    def turned(a, s, n):
        return a ^ abs(s) if n & (n - 1) == 0 else (a + s) % n

    def shards(embeddings, cluster_id, cluster_group):
        rows = embeddings.shape[0]
        own, table = pack(embeddings, cluster_id, cluster_group, n_clu)

        def rank(z=0, a=0, g=0):
            def of(clu, grp):
                line, place = turned(clu // wide, z, length), turned(clu % wide, a, wide)
                return turned(grp, g, n_grp) * n_clu + line * wide + place

            return of

        def along(x, s):
            return permute(x, lambda z, a, g: (turned(z, s, length), a, g))

        half = length // 2 if length & (length - 1) == 0 else length
        near = [permute(own, lambda z, a, g: (z, turned(a, s, wide), g)) for s in reversed(range(1, wide))]
        first = [along(own, s) for s in range(1, half)]
        middle = along(own, length - 1) if half < length else None
        near, first = lax.optimization_barrier((near, first))
        near = near[::-1]
        last = [along(middle, s) for s in range(1, half)] if half < length else []
        offsets = list(range(1, half))
        if half < length:
            first = first + [middle]
            offsets += [length - 1] + [(length - 1) ^ s for s in range(1, half)]
        far, far_rank = [], []
        for t in range(1, n_grp):
            for s in range(wide):
                block = near[s - 1] if s else own
                far.append(permute(block, lambda z, a, g: (z, a, turned(g, t, n_grp))))
                far_rank.append(rank(a=s, g=t))
        near = list(zip([own] + near, [rank(a=s) for s in range(wide)]))
        far = list(zip(far, far_rank))
        visit_rank = [rank(z=s) for s in offsets]
        first = list(zip(first, visit_rank))
        last = list(zip(last, visit_rank[len(first) :]))
        best = best_of(near + far, near[:1] + first, table, True)
        if last:
            best = best + best_of(near + far, last, table, False)
        found = [best[0]] + [along(b, -s) for b, s in zip(best[1:], offsets)]
        return functools.reduce(jnp.maximum, found).reshape(rows)

    placed = (P(("clu", "grp"), None), P(("clu", "grp")), P())
    return jax.shard_map(
        shards, mesh=mesh, in_specs=placed, out_specs=P(("clu", "grp")), check_vma=False
    )
```

```python
import functools
import math

import jax
import jax.numpy as jnp
from jax import lax
from jax.experimental import pallas as pl
from jax.experimental.pallas import tpu as pltpu
from jax.sharding import PartitionSpec as P

AUX = 8
DIGIT = 256


def pack_kernel(groups, emb_ref, id_ref, group_ref, out_ref, table_ref):
    rows, width = emb_ref.shape
    values = emb_ref[...].astype(jnp.float32)
    scale = lax.rsqrt(jnp.sum(values * values, axis=-1, keepdims=True) + 1e-06)
    out_ref[:rows, :] = (values * scale).astype(jnp.bfloat16)
    ids = jnp.broadcast_to(id_ref[...], (AUX, rows))
    row = lax.broadcasted_iota(jnp.int32, (AUX, rows), 0)
    digits = jnp.where(row == 0, ids % DIGIT, ids // DIGIT)
    if width > rows:
        digits = jnp.concatenate([digits, jnp.zeros((AUX, width - rows), jnp.int32)], axis=1)
    out_ref[rows:, :] = digits.astype(jnp.float32).astype(jnp.bfloat16)
    clusters = group_ref.shape[1]
    index = lax.broadcasted_iota(jnp.int32, (groups, clusters), 0)
    member = jnp.where(index == group_ref[...], 1.0, 0.0).astype(jnp.bfloat16)
    same = lax.dot_general(member, member, (((0,), (0,)), ((), ())), preferred_element_type=jnp.float32)
    one = lax.broadcasted_iota(jnp.int32, (clusters, clusters), 0)
    other = lax.broadcasted_iota(jnp.int32, (clusters, clusters), 1)
    table_ref[...] = jnp.where(one == other, 1.0, 0.5 * same).astype(jnp.bfloat16)


def pack(embeddings, cluster_id, cluster_group, groups):
    rows, width = embeddings.shape
    clusters = cluster_group.shape[0]
    return pl.pallas_call(
        functools.partial(pack_kernel, groups),
        out_shape=[pltpu.VMEM((rows + AUX, width), jnp.bfloat16), pltpu.VMEM((clusters, clusters), jnp.bfloat16)],
    )(embeddings, cluster_id.reshape(1, rows), cluster_group.reshape(1, clusters))


def one_hot(digits, clusters):
    number = digits[0:1].astype(jnp.int32) + DIGIT * digits[1:2].astype(jnp.int32)
    index = lax.broadcasted_iota(jnp.int32, (clusters, digits.shape[1]), 0)
    return jnp.where(index == number, 1.0, 0.0).astype(jnp.bfloat16)


def best_kernel(n_keys, own, ranks, table_ref, *refs):
    n_queries = (len(refs) - n_keys) // 2
    keys, queries, outs = refs[:n_keys], refs[n_keys : n_keys + n_queries], refs[n_keys + n_queries :]
    rows = keys[0].shape[0] - AUX
    clusters = table_ref.shape[0]
    clu, grp = lax.axis_index("clu"), lax.axis_index("grp")
    ranks = [rank(clu, grp) for rank in ranks]

    def hot(block):
        return one_hot(block[rows:, :rows].astype(jnp.float32), clusters)

    key_hot = jnp.concatenate([hot(b) for b in keys], axis=1)
    key_rows = jnp.concatenate([b[:rows, :] for b in keys], axis=0)
    for j in range(n_queries):
        mixed = jnp.dot(table_ref[...], hot(queries[j]), preferred_element_type=jnp.float32).astype(jnp.bfloat16)
        weight = lax.dot_general(key_hot, mixed, (((0,), (0,)), ((), ())), preferred_element_type=jnp.float32)
        sims = lax.dot_general(
            key_rows, queries[j][:rows, :], (((1,), (1,)), ((), ())), preferred_element_type=jnp.float32
        )
        score = jnp.where(weight > 0, weight * sims, -1.0)
        best = jnp.full((1, rows), -1.0, jnp.float32)
        for i in range(n_keys):
            part = score[i * rows : (i + 1) * rows, :]
            if own and i + j == 0:
                k = lax.broadcasted_iota(jnp.int32, (rows, rows), 0)
                q = lax.broadcasted_iota(jnp.int32, (rows, rows), 1)
                found = jnp.max(jnp.where(k < q, part, -1.0), axis=0, keepdims=True)
            else:
                found = jnp.max(part, axis=0, keepdims=True)
                found = jnp.where(ranks[i] < ranks[n_keys + j], found, -1.0)
            best = jnp.maximum(best, found)
        outs[j][...] = best


def best_of(keys, queries, table, own):
    rows, width = keys[0][0].shape[0] - AUX, keys[0][0].shape[1]
    vmem = pl.BlockSpec(memory_space=pltpu.VMEM)
    ranks = [r for _, r in keys + queries]
    pairs = len(keys) * len(queries) * rows * rows
    return pl.pallas_call(
        functools.partial(best_kernel, len(keys), own, ranks),
        out_shape=[jax.ShapeDtypeStruct((1, rows), jnp.float32)] * len(queries),
        in_specs=[vmem] * (1 + len(keys) + len(queries)),
        out_specs=[vmem] * len(queries),
        compiler_params=pltpu.CompilerParams(vmem_limit_bytes=40 * 2**20),
        cost_estimate=pl.CostEstimate(
            flops=2 * pairs * width, bytes_accessed=2 * (len(keys) + len(queries)) * rows * width, transcendentals=0
        ),
    )(table, *[b for b, _ in keys + queries])


def solution(mesh):
    n_clu, n_grp = mesh.shape["clu"], mesh.shape["grp"]
    target = math.sqrt(n_clu * n_grp)
    wide = min(a for a in range(1, n_clu + 1) if n_clu % a == 0 and (a * n_grp >= target or a == n_clu))
    length = n_clu // wide

    def permute(x, move):
        pairs = []
        for z in range(length):
            for a in range(wide):
                for g in range(n_grp):
                    at = move(z, a, g)
                    pairs.append(((at[0] * wide + at[1]) * n_grp + at[2], (z * wide + a) * n_grp + g))
        return lax.ppermute(x, ("clu", "grp"), pairs)

    def turned(a, s, n):
        return a ^ abs(s) if n & (n - 1) == 0 else (a + s) % n

    def shards(embeddings, cluster_id, cluster_group):
        rows = embeddings.shape[0]
        own, table = pack(embeddings, cluster_id, cluster_group, n_clu)

        def rank(z=0, a=0, g=0):
            def of(clu, grp):
                line, place = turned(clu // wide, z, length), turned(clu % wide, a, wide)
                return turned(grp, g, n_grp) * n_clu + line * wide + place

            return of

        def along(x, s):
            return permute(x, lambda z, a, g: (turned(z, s, length), a, g))

        half = length // 2 if length & (length - 1) == 0 else length
        near = [permute(own, lambda z, a, g: (z, turned(a, s, wide), g)) for s in reversed(range(1, wide))]
        middle = along(own, length - 1) if half < length else None
        first = [along(own, s) for s in range(1, half)]
        near = lax.optimization_barrier(near)
        middle, first = lax.optimization_barrier((middle, first))
        near = near[::-1]
        last = [along(middle, s) for s in range(1, half)] if half < length else []
        offsets = list(range(1, half))
        if half < length:
            first = first + [middle]
            offsets += [length - 1] + [(length - 1) ^ s for s in range(1, half)]
        far, far_rank = [], []
        for t in range(1, n_grp):
            for s in range(wide):
                block = near[s - 1] if s else own
                far.append(permute(block, lambda z, a, g: (z, a, turned(g, t, n_grp))))
                far_rank.append(rank(a=s, g=t))
        near = list(zip([own] + near, [rank(a=s) for s in range(wide)]))
        far = list(zip(far, far_rank))
        visit_rank = [rank(z=s) for s in offsets]
        first = list(zip(first, visit_rank))
        last = list(zip(last, visit_rank[len(first) :]))
        best = best_of(near + far, near[:1] + first, table, True)
        if last:
            best = best + best_of(near + far, last, table, False)
        found = [best[0]] + [along(b, -s) for b, s in zip(best[1:], offsets)]
        return functools.reduce(jnp.maximum, found).reshape(rows)

    placed = (P(("clu", "grp"), None), P(("clu", "grp")), P())
    return jax.shard_map(
        shards, mesh=mesh, in_specs=placed, out_specs=P(("clu", "grp")), check_vma=False
    )
```

```python
import functools
import math

import jax
import jax.numpy as jnp
from jax import lax
from jax.experimental import pallas as pl
from jax.experimental.pallas import tpu as pltpu
from jax.sharding import PartitionSpec as P

AUX = 8
DIGIT = 256


def pack_kernel(groups, emb_ref, id_ref, group_ref, out_ref, table_ref):
    rows, width = emb_ref.shape
    values = emb_ref[...].astype(jnp.float32)
    scale = lax.rsqrt(jnp.sum(values * values, axis=-1, keepdims=True) + 1e-06)
    out_ref[:rows, :] = (values * scale).astype(jnp.bfloat16)
    ids = jnp.broadcast_to(id_ref[...], (AUX, rows))
    row = lax.broadcasted_iota(jnp.int32, (AUX, rows), 0)
    digits = jnp.where(row == 0, ids % DIGIT, ids // DIGIT)
    if width > rows:
        digits = jnp.concatenate([digits, jnp.zeros((AUX, width - rows), jnp.int32)], axis=1)
    out_ref[rows:, :] = digits.astype(jnp.float32).astype(jnp.bfloat16)
    clusters = group_ref.shape[1]
    index = lax.broadcasted_iota(jnp.int32, (groups, clusters), 0)
    member = jnp.where(index == group_ref[...], 1.0, 0.0).astype(jnp.bfloat16)
    same = lax.dot_general(member, member, (((0,), (0,)), ((), ())), preferred_element_type=jnp.float32)
    one = lax.broadcasted_iota(jnp.int32, (clusters, clusters), 0)
    other = lax.broadcasted_iota(jnp.int32, (clusters, clusters), 1)
    table_ref[...] = jnp.where(one == other, 1.0, 0.5 * same).astype(jnp.bfloat16)


def pack(embeddings, cluster_id, cluster_group, groups):
    rows, width = embeddings.shape
    clusters = cluster_group.shape[0]
    return pl.pallas_call(
        functools.partial(pack_kernel, groups),
        out_shape=[pltpu.VMEM((rows + AUX, width), jnp.bfloat16), pltpu.VMEM((clusters, clusters), jnp.bfloat16)],
    )(embeddings, cluster_id.reshape(1, rows), cluster_group.reshape(1, clusters))


def one_hot(digits, clusters):
    number = digits[0:1].astype(jnp.int32) + DIGIT * digits[1:2].astype(jnp.int32)
    index = lax.broadcasted_iota(jnp.int32, (clusters, digits.shape[1]), 0)
    return jnp.where(index == number, 1.0, 0.0).astype(jnp.bfloat16)


def best_kernel(n_keys, n_spans, own, ranks, table_ref, *refs):
    n_queries = (len(refs) - n_keys) // 2
    keys, queries, outs = refs[:n_keys], refs[n_keys : n_keys + n_queries], refs[n_keys + n_queries :]
    rows = keys[0].shape[0] - AUX
    clusters = table_ref.shape[0]
    clu, grp = lax.axis_index("clu"), lax.axis_index("grp")
    ranks = [rank(clu, grp) for rank in ranks]

    def hot(block):
        return one_hot(block[rows:, :rows].astype(jnp.float32), clusters)

    mixed = [
        jnp.dot(table_ref[...], hot(query), preferred_element_type=jnp.float32).astype(jnp.bfloat16)
        for query in queries
    ]

    def search(span, first):
        key_hot = jnp.concatenate([hot(keys[i]) for i in span], axis=1)
        key_rows = jnp.concatenate([keys[i][:rows, :] for i in span], axis=0)
        for j in range(n_queries):
            weight = lax.dot_general(
                key_hot, mixed[j], (((0,), (0,)), ((), ())), preferred_element_type=jnp.float32
            )
            sims = lax.dot_general(
                key_rows, queries[j][:rows, :], (((1,), (1,)), ((), ())), preferred_element_type=jnp.float32
            )
            score = jnp.where(weight > 0, weight * sims, -1.0)
            best = jnp.full((1, rows), -1.0, jnp.float32) if first else outs[j][...]
            for at, i in enumerate(span):
                part = score[at * rows : (at + 1) * rows, :]
                if own and i + j == 0:
                    k = lax.broadcasted_iota(jnp.int32, (rows, rows), 0)
                    q = lax.broadcasted_iota(jnp.int32, (rows, rows), 1)
                    found = jnp.max(jnp.where(k < q, part, -1.0), axis=0, keepdims=True)
                else:
                    found = jnp.max(part, axis=0, keepdims=True)
                    found = jnp.where(ranks[i] < ranks[n_keys + j], found, -1.0)
                best = jnp.maximum(best, found)
            outs[j][...] = best

    width = n_keys // n_spans
    search(range(width), True)
    for t in range(1, n_spans):
        @pl.when(ranks[t * width] < ranks[0])
        def _():
            search(range(t * width, (t + 1) * width), False)


def best_of(keys, n_spans, queries, table, own):
    rows, width = keys[0][0].shape[0] - AUX, keys[0][0].shape[1]
    vmem = pl.BlockSpec(memory_space=pltpu.VMEM)
    ranks = [r for _, r in keys + queries]
    pairs = len(keys) * len(queries) * rows * rows
    return pl.pallas_call(
        functools.partial(best_kernel, len(keys), n_spans, own, ranks),
        out_shape=[jax.ShapeDtypeStruct((1, rows), jnp.float32)] * len(queries),
        in_specs=[vmem] * (1 + len(keys) + len(queries)),
        out_specs=[vmem] * len(queries),
        compiler_params=pltpu.CompilerParams(vmem_limit_bytes=40 * 2**20),
        cost_estimate=pl.CostEstimate(
            flops=2 * pairs * width, bytes_accessed=2 * (len(keys) + len(queries)) * rows * width, transcendentals=0
        ),
    )(table, *[b for b, _ in keys + queries])


def solution(mesh):
    n_clu, n_grp = mesh.shape["clu"], mesh.shape["grp"]
    target = math.sqrt(n_clu * n_grp)
    wide = min(a for a in range(1, n_clu + 1) if n_clu % a == 0 and (a * n_grp >= target or a == n_clu))
    length = n_clu // wide

    def permute(x, move):
        pairs = []
        for z in range(length):
            for a in range(wide):
                for g in range(n_grp):
                    at = move(z, a, g)
                    pairs.append(((at[0] * wide + at[1]) * n_grp + at[2], (z * wide + a) * n_grp + g))
        return lax.ppermute(x, ("clu", "grp"), pairs)

    def turned(a, s, n):
        return a ^ abs(s) if n & (n - 1) == 0 else (a + s) % n

    def shards(embeddings, cluster_id, cluster_group):
        rows = embeddings.shape[0]
        own, table = pack(embeddings, cluster_id, cluster_group, n_clu)

        def rank(z=0, a=0, g=0):
            def of(clu, grp):
                line, place = turned(clu // wide, z, length), turned(clu % wide, a, wide)
                return turned(grp, g, n_grp) * n_clu + line * wide + place

            return of

        def along(x, s):
            return permute(x, lambda z, a, g: (turned(z, s, length), a, g))

        half = length // 2 if length & (length - 1) == 0 else length
        near = [permute(own, lambda z, a, g: (z, turned(a, s, wide), g)) for s in reversed(range(1, wide))]
        middle = along(own, length - 1) if half < length else None
        first = [along(own, s) for s in range(1, half)]
        near = lax.optimization_barrier(near)
        middle, first = lax.optimization_barrier((middle, first))
        near = near[::-1]
        last = [along(middle, s) for s in range(1, half)] if half < length else []
        offsets = list(range(1, half))
        if half < length:
            first = first + [middle]
            offsets += [length - 1] + [(length - 1) ^ s for s in range(1, half)]
        far, far_rank = [], []
        for t in range(1, n_grp):
            for s in range(wide):
                block = near[s - 1] if s else own
                far.append(permute(block, lambda z, a, g: (z, a, turned(g, t, n_grp))))
                far_rank.append(rank(a=s, g=t))
        near = list(zip([own] + near, [rank(a=s) for s in range(wide)]))
        far = list(zip(far, far_rank))
        visit_rank = [rank(z=s) for s in offsets]
        first = list(zip(first, visit_rank))
        last = list(zip(last, visit_rank[len(first) :]))
        best = best_of(near + far, n_grp, near[:1] + first, table, True)
        if last:
            best = best + best_of(near + far, n_grp, last, table, False)
        found = [best[0]] + [along(b, -s) for b, s in zip(best[1:], offsets)]
        return functools.reduce(jnp.maximum, found).reshape(rows)

    placed = (P(("clu", "grp"), None), P(("clu", "grp")), P())
    return jax.shard_map(
        shards, mesh=mesh, in_specs=placed, out_specs=P(("clu", "grp")), check_vma=False
    )
```

```python
import functools
import math

import jax
import jax.numpy as jnp
from jax import lax
from jax.experimental import pallas as pl
from jax.experimental.pallas import tpu as pltpu
from jax.sharding import PartitionSpec as P

AUX = 8
DIGIT = 256


def pack_kernel(groups, emb_ref, id_ref, group_ref, out_ref, table_ref):
    rows, width = emb_ref.shape
    values = emb_ref[...].astype(jnp.float32)
    scale = lax.rsqrt(jnp.sum(values * values, axis=-1, keepdims=True) + 1e-06)
    out_ref[:rows, :] = (values * scale).astype(jnp.bfloat16)
    ids = jnp.broadcast_to(id_ref[...], (AUX, rows))
    row = lax.broadcasted_iota(jnp.int32, (AUX, rows), 0)
    digits = jnp.where(row == 0, ids % DIGIT, ids // DIGIT)
    if width > rows:
        digits = jnp.concatenate([digits, jnp.zeros((AUX, width - rows), jnp.int32)], axis=1)
    out_ref[rows:, :] = digits.astype(jnp.float32).astype(jnp.bfloat16)
    clusters = group_ref.shape[1]
    index = lax.broadcasted_iota(jnp.int32, (groups, clusters), 0)
    member = jnp.where(index == group_ref[...], 1.0, 0.0).astype(jnp.bfloat16)
    same = lax.dot_general(member, member, (((0,), (0,)), ((), ())), preferred_element_type=jnp.float32)
    one = lax.broadcasted_iota(jnp.int32, (clusters, clusters), 0)
    other = lax.broadcasted_iota(jnp.int32, (clusters, clusters), 1)
    table_ref[...] = jnp.where(one == other, 1.0, 0.5 * same).astype(jnp.bfloat16)


def pack(embeddings, cluster_id, cluster_group, groups):
    rows, width = embeddings.shape
    clusters = cluster_group.shape[0]
    return pl.pallas_call(
        functools.partial(pack_kernel, groups),
        out_shape=[pltpu.VMEM((rows + AUX, width), jnp.bfloat16), pltpu.VMEM((clusters, clusters), jnp.bfloat16)],
    )(embeddings, cluster_id.reshape(1, rows), cluster_group.reshape(1, clusters))


def one_hot(digits, clusters):
    number = digits[0:1].astype(jnp.int32) + DIGIT * digits[1:2].astype(jnp.int32)
    index = lax.broadcasted_iota(jnp.int32, (clusters, digits.shape[1]), 0)
    return jnp.where(index == number, 1.0, 0.0).astype(jnp.bfloat16)


def best_kernel(n_keys, n_spans, own, ranks, table_ref, *refs):
    n_queries = (len(refs) - n_keys) // 2
    keys, queries, outs = refs[:n_keys], refs[n_keys : n_keys + n_queries], refs[n_keys + n_queries :]
    rows = keys[0].shape[0] - AUX
    clusters = table_ref.shape[0]
    clu, grp = lax.axis_index("clu"), lax.axis_index("grp")
    ranks = [rank(clu, grp) for rank in ranks]

    def hot(block):
        return one_hot(block[rows:, :rows].astype(jnp.float32), clusters)

    mixed = [
        jnp.dot(table_ref[...], hot(query), preferred_element_type=jnp.float32).astype(jnp.bfloat16)
        for query in queries
    ]

    def search(span, first):
        key_hot = jnp.concatenate([hot(keys[i]) for i in span], axis=1)
        key_rows = jnp.concatenate([keys[i][:rows, :] for i in span], axis=0)
        for j in range(n_queries):
            weight = lax.dot_general(
                key_hot, mixed[j], (((0,), (0,)), ((), ())), preferred_element_type=jnp.float32
            )
            sims = lax.dot_general(
                key_rows, queries[j][:rows, :], (((1,), (1,)), ((), ())), preferred_element_type=jnp.float32
            )
            score = jnp.where(weight > 0, weight * sims, -1.0)
            best = jnp.full((1, rows), -1.0, jnp.float32) if first else outs[j][...]
            for at, i in enumerate(span):
                part = score[at * rows : (at + 1) * rows, :]
                if own and i + j == 0:
                    k = lax.broadcasted_iota(jnp.int32, (rows, rows), 0)
                    q = lax.broadcasted_iota(jnp.int32, (rows, rows), 1)
                    found = jnp.max(jnp.where(k < q, part, -1.0), axis=0, keepdims=True)
                else:
                    found = jnp.max(part, axis=0, keepdims=True)
                    found = jnp.where(ranks[i] < ranks[n_keys + j], found, -1.0)
                best = jnp.maximum(best, found)
            outs[j][...] = best

    width = n_keys // n_spans
    search(range(width), True)
    for t in range(1, n_spans):
        @pl.when(ranks[t * width] < ranks[0])
        def _():
            search(range(t * width, (t + 1) * width), False)


def best_of(keys, n_spans, queries, table, own):
    rows, width = keys[0][0].shape[0] - AUX, keys[0][0].shape[1]
    vmem = pl.BlockSpec(memory_space=pltpu.VMEM)
    ranks = [r for _, r in keys + queries]
    pairs = len(keys) * len(queries) * rows * rows
    return pl.pallas_call(
        functools.partial(best_kernel, len(keys), n_spans, own, ranks),
        out_shape=[jax.ShapeDtypeStruct((1, rows), jnp.float32)] * len(queries),
        in_specs=[vmem] * (1 + len(keys) + len(queries)),
        out_specs=[vmem] * len(queries),
        compiler_params=pltpu.CompilerParams(vmem_limit_bytes=40 * 2**20),
        cost_estimate=pl.CostEstimate(
            flops=2 * pairs * width, bytes_accessed=2 * (len(keys) + len(queries)) * rows * width, transcendentals=0
        ),
    )(table, *[b for b, _ in keys + queries])


def solution(mesh):
    n_clu, n_grp = mesh.shape["clu"], mesh.shape["grp"]
    target = math.sqrt(n_clu * n_grp)
    wide = min(a for a in range(1, n_clu + 1) if n_clu % a == 0 and (a * n_grp >= target or a == n_clu))
    length = n_clu // wide

    def permute(x, move):
        pairs = []
        for z in range(length):
            for a in range(wide):
                for g in range(n_grp):
                    at = move(z, a, g)
                    pairs.append(((at[0] * wide + at[1]) * n_grp + at[2], (z * wide + a) * n_grp + g))
        return lax.ppermute(x, ("clu", "grp"), pairs)

    def turned(a, s, n):
        return a ^ abs(s) if n & (n - 1) == 0 else (a + s) % n

    def shards(embeddings, cluster_id, cluster_group):
        rows = embeddings.shape[0]
        own, table = pack(embeddings, cluster_id, cluster_group, n_clu)

        def rank(z=0, a=0, g=0):
            def of(clu, grp):
                line, place = turned(clu // wide, z, length), turned(clu % wide, a, wide)
                return turned(grp, g, n_grp) * n_clu + line * wide + place

            return of

        def along(x, s):
            return permute(x, lambda z, a, g: (turned(z, s, length), a, g))

        half = length // 2 if length & (length - 1) == 0 else length
        near = [permute(own, lambda z, a, g: (z, turned(a, s, wide), g)) for s in reversed(range(1, wide))]
        middle = along(own, length - 1) if half < length else None
        first = [along(own, s) for s in range(1, half)]
        early, middle = lax.optimization_barrier((near[:-1], middle))
        late, first = lax.optimization_barrier((near[-1:], first))
        near = early + late
        near = near[::-1]
        last = [along(middle, s) for s in range(1, half)] if half < length else []
        offsets = list(range(1, half))
        if half < length:
            first = first + [middle]
            offsets += [length - 1] + [(length - 1) ^ s for s in range(1, half)]
        far, far_rank = [], []
        for t in range(1, n_grp):
            for s in range(wide):
                block = near[s - 1] if s else own
                far.append(permute(block, lambda z, a, g: (z, a, turned(g, t, n_grp))))
                far_rank.append(rank(a=s, g=t))
        near = list(zip([own] + near, [rank(a=s) for s in range(wide)]))
        far = list(zip(far, far_rank))
        visit_rank = [rank(z=s) for s in offsets]
        first = list(zip(first, visit_rank))
        last = list(zip(last, visit_rank[len(first) :]))
        best = best_of(near + far, n_grp, near[:1] + first, table, True)
        if last:
            best = best + best_of(near + far, n_grp, last, table, False)
        found = [best[0]] + [along(b, -s) for b, s in zip(best[1:], offsets)]
        return functools.reduce(jnp.maximum, found).reshape(rows)

    placed = (P(("clu", "grp"), None), P(("clu", "grp")), P())
    return jax.shard_map(
        shards, mesh=mesh, in_specs=placed, out_specs=P(("clu", "grp")), check_vma=False
    )
```

```python
import functools
import math

import jax
import jax.numpy as jnp
from jax import lax
from jax.experimental import pallas as pl
from jax.experimental.pallas import tpu as pltpu
from jax.sharding import PartitionSpec as P

AUX = 8
DIGIT = 256


def pack_kernel(groups, emb_ref, id_ref, group_ref, out_ref, table_ref):
    rows, width = emb_ref.shape
    values = emb_ref[...].astype(jnp.float32)
    scale = lax.rsqrt(jnp.sum(values * values, axis=-1, keepdims=True) + 1e-06)
    out_ref[:rows, :] = (values * scale).astype(jnp.bfloat16)
    ids = jnp.broadcast_to(id_ref[...], (AUX, rows))
    row = lax.broadcasted_iota(jnp.int32, (AUX, rows), 0)
    digits = jnp.where(row == 0, ids % DIGIT, ids // DIGIT)
    if width > rows:
        digits = jnp.concatenate([digits, jnp.zeros((AUX, width - rows), jnp.int32)], axis=1)
    out_ref[rows:, :] = digits.astype(jnp.float32).astype(jnp.bfloat16)
    clusters = group_ref.shape[1]
    index = lax.broadcasted_iota(jnp.int32, (groups, clusters), 0)
    member = jnp.where(index == group_ref[...], 1.0, 0.0).astype(jnp.bfloat16)
    same = lax.dot_general(member, member, (((0,), (0,)), ((), ())), preferred_element_type=jnp.float32)
    one = lax.broadcasted_iota(jnp.int32, (clusters, clusters), 0)
    other = lax.broadcasted_iota(jnp.int32, (clusters, clusters), 1)
    table_ref[...] = jnp.where(one == other, 1.0, 0.5 * same).astype(jnp.bfloat16)


def pack(embeddings, cluster_id, cluster_group, groups):
    rows, width = embeddings.shape
    clusters = cluster_group.shape[0]
    return pl.pallas_call(
        functools.partial(pack_kernel, groups),
        out_shape=[pltpu.VMEM((rows + AUX, width), jnp.bfloat16), pltpu.VMEM((clusters, clusters), jnp.bfloat16)],
    )(embeddings, cluster_id.reshape(1, rows), cluster_group.reshape(1, clusters))


def one_hot(digits, clusters):
    number = digits[0:1].astype(jnp.int32) + DIGIT * digits[1:2].astype(jnp.int32)
    index = lax.broadcasted_iota(jnp.int32, (clusters, digits.shape[1]), 0)
    return jnp.where(index == number, 1.0, 0.0).astype(jnp.bfloat16)


def best_kernel(n_keys, n_spans, own, ranks, table_ref, *refs):
    n_queries = (len(refs) - n_keys) // 2
    keys, queries, outs = refs[:n_keys], refs[n_keys : n_keys + n_queries], refs[n_keys + n_queries :]
    rows = keys[0].shape[0] - AUX
    clusters = table_ref.shape[0]
    clu, grp = lax.axis_index("clu"), lax.axis_index("grp")
    ranks = [rank(clu, grp) for rank in ranks]

    def hot(block):
        return one_hot(block[rows:, :rows].astype(jnp.float32), clusters)

    mixed = [
        jnp.dot(table_ref[...], hot(query), preferred_element_type=jnp.float32).astype(jnp.bfloat16)
        for query in queries
    ]

    def search(span, first):
        key_hot = jnp.concatenate([hot(keys[i]) for i in span], axis=1)
        key_rows = jnp.concatenate([keys[i][:rows, :] for i in span], axis=0)
        for j in range(n_queries):
            weight = lax.dot_general(
                key_hot, mixed[j], (((0,), (0,)), ((), ())), preferred_element_type=jnp.float32
            )
            sims = lax.dot_general(
                key_rows, queries[j][:rows, :], (((1,), (1,)), ((), ())), preferred_element_type=jnp.float32
            )
            score = jnp.where(weight > 0, weight * sims, -1.0)
            best = jnp.full((1, rows), -1.0, jnp.float32) if first else outs[j][...]
            for at, i in enumerate(span):
                part = score[at * rows : (at + 1) * rows, :]
                if own and i + j == 0:
                    k = lax.broadcasted_iota(jnp.int32, (rows, rows), 0)
                    q = lax.broadcasted_iota(jnp.int32, (rows, rows), 1)
                    found = jnp.max(jnp.where(k < q, part, -1.0), axis=0, keepdims=True)
                else:
                    found = jnp.max(part, axis=0, keepdims=True)
                    found = jnp.where(ranks[i] < ranks[n_keys + j], found, -1.0)
                best = jnp.maximum(best, found)
            outs[j][...] = best

    width = n_keys // n_spans
    search(range(width), True)
    for t in range(1, n_spans):
        @pl.when(ranks[t * width] < ranks[0])
        def _():
            search(range(t * width, (t + 1) * width), False)


def best_of(keys, n_spans, queries, table, own):
    rows, width = keys[0][0].shape[0] - AUX, keys[0][0].shape[1]
    vmem = pl.BlockSpec(memory_space=pltpu.VMEM)
    ranks = [r for _, r in keys + queries]
    pairs = len(keys) * len(queries) * rows * rows
    return pl.pallas_call(
        functools.partial(best_kernel, len(keys), n_spans, own, ranks),
        out_shape=[jax.ShapeDtypeStruct((1, rows), jnp.float32)] * len(queries),
        in_specs=[vmem] * (1 + len(keys) + len(queries)),
        out_specs=[vmem] * len(queries),
        compiler_params=pltpu.CompilerParams(vmem_limit_bytes=40 * 2**20),
        cost_estimate=pl.CostEstimate(
            flops=2 * pairs * width, bytes_accessed=2 * (len(keys) + len(queries)) * rows * width, transcendentals=0
        ),
    )(table, *[b for b, _ in keys + queries])


def solution(mesh):
    n_clu, n_grp = mesh.shape["clu"], mesh.shape["grp"]
    target = math.sqrt(n_clu * n_grp)
    wide = min(a for a in range(1, n_clu + 1) if n_clu % a == 0 and (a * n_grp >= target or a == n_clu))
    length = n_clu // wide

    def permute(x, move):
        pairs = []
        for z in range(length):
            for a in range(wide):
                for g in range(n_grp):
                    at = move(z, a, g)
                    pairs.append(((at[0] * wide + at[1]) * n_grp + at[2], (z * wide + a) * n_grp + g))
        return lax.ppermute(x, ("clu", "grp"), pairs)

    def turned(a, s, n):
        return a ^ abs(s) if n & (n - 1) == 0 else (a + s) % n

    def shards(embeddings, cluster_id, cluster_group):
        rows = embeddings.shape[0]
        own, table = pack(embeddings, cluster_id, cluster_group, n_clu)

        def rank(z=0, a=0, g=0):
            def of(clu, grp):
                line, place = turned(clu // wide, z, length), turned(clu % wide, a, wide)
                return turned(grp, g, n_grp) * n_clu + line * wide + place

            return of

        def along(x, s):
            return permute(x, lambda z, a, g: (turned(z, s, length), a, g))

        half = length // 2 if length & (length - 1) == 0 else length
        near = [permute(own, lambda z, a, g: (z, turned(a, s, wide), g)) for s in reversed(range(1, wide))]
        middle = along(own, length - 1) if half < length else None
        first = [along(own, s) for s in range(1, half)]
        middle, first = lax.optimization_barrier((middle, first))
        near = near[::-1]
        last = [along(middle, s) for s in range(1, half)] if half < length else []
        offsets = list(range(1, half))
        if half < length:
            first = first + [middle]
            offsets += [length - 1] + [(length - 1) ^ s for s in range(1, half)]
        far, far_rank = [], []
        for t in range(1, n_grp):
            for s in range(wide):
                block = near[s - 1] if s else own
                far.append(permute(block, lambda z, a, g: (z, a, turned(g, t, n_grp))))
                far_rank.append(rank(a=s, g=t))
        near = list(zip([own] + near, [rank(a=s) for s in range(wide)]))
        far = list(zip(far, far_rank))
        visit_rank = [rank(z=s) for s in offsets]
        first = list(zip(first, visit_rank))
        last = list(zip(last, visit_rank[len(first) :]))
        best = best_of(near + far, n_grp, near[:1] + first, table, True)
        if last:
            best = best + best_of(near + far, n_grp, last, table, False)
        found = [best[0]] + [along(b, -s) for b, s in zip(best[1:], offsets)]
        return functools.reduce(jnp.maximum, found).reshape(rows)

    placed = (P(("clu", "grp"), None), P(("clu", "grp")), P())
    return jax.shard_map(
        shards, mesh=mesh, in_specs=placed, out_specs=P(("clu", "grp")), check_vma=False
    )
```

```python
import functools
import math

import jax
import jax.numpy as jnp
from jax import lax
from jax.experimental import pallas as pl
from jax.experimental.pallas import tpu as pltpu
from jax.sharding import PartitionSpec as P

LANES = 128
AUX = 8
DIGIT = 256


def pack_kernel(groups, emb_ref, id_ref, group_ref, out_ref, table_ref):
    rows, width = emb_ref.shape
    values = emb_ref[...].astype(jnp.float32)
    scale = lax.rsqrt(jnp.sum(values * values, axis=-1, keepdims=True) + 1e-06)
    unit = (values * scale).astype(jnp.bfloat16)
    for panel in range(width // LANES):
        out_ref[panel * rows : (panel + 1) * rows, :] = unit[:, panel * LANES : (panel + 1) * LANES]
    ids = jnp.broadcast_to(id_ref[...], (AUX, rows))
    row = lax.broadcasted_iota(jnp.int32, (AUX, rows), 0)
    digits = jnp.where(row == 0, ids % DIGIT, ids // DIGIT)
    if LANES > rows:
        digits = jnp.concatenate([digits, jnp.zeros((AUX, LANES - rows), jnp.int32)], axis=1)
    out_ref[width // LANES * rows :, :] = digits.astype(jnp.float32).astype(jnp.bfloat16)
    clusters = group_ref.shape[1]
    index = lax.broadcasted_iota(jnp.int32, (groups, clusters), 0)
    member = jnp.where(index == group_ref[...], 1.0, 0.0).astype(jnp.bfloat16)
    same = lax.dot_general(member, member, (((0,), (0,)), ((), ())), preferred_element_type=jnp.float32)
    one = lax.broadcasted_iota(jnp.int32, (clusters, clusters), 0)
    other = lax.broadcasted_iota(jnp.int32, (clusters, clusters), 1)
    table_ref[...] = jnp.where(one == other, 1.0, 0.5 * same).astype(jnp.bfloat16)


def pack(embeddings, cluster_id, cluster_group, groups):
    rows, width = embeddings.shape
    assert rows <= LANES and width % LANES == 0
    clusters = cluster_group.shape[0]
    return pl.pallas_call(
        functools.partial(pack_kernel, groups),
        out_shape=[pltpu.VMEM((width // LANES * rows + AUX, LANES), jnp.bfloat16), pltpu.VMEM((clusters, clusters), jnp.bfloat16)],
    )(embeddings, cluster_id.reshape(1, rows), cluster_group.reshape(1, clusters))


def one_hot(digits, clusters):
    number = digits[0:1].astype(jnp.int32) + DIGIT * digits[1:2].astype(jnp.int32)
    index = lax.broadcasted_iota(jnp.int32, (clusters, digits.shape[1]), 0)
    return jnp.where(index == number, 1.0, 0.0).astype(jnp.bfloat16)


def best_kernel(rows, n_keys, n_spans, own, ranks, table_ref, *refs):
    n_queries = (len(refs) - n_keys) // 2
    keys, queries, outs = refs[:n_keys], refs[n_keys : n_keys + n_queries], refs[n_keys + n_queries :]
    panels = (keys[0].shape[0] - AUX) // rows
    clusters = table_ref.shape[0]
    clu, grp = lax.axis_index("clu"), lax.axis_index("grp")
    ranks = [rank(clu, grp) for rank in ranks]

    def hot(block):
        return one_hot(block[panels * rows :, :rows].astype(jnp.float32), clusters)

    def unit(block):
        return jnp.concatenate([block[p * rows : (p + 1) * rows, :] for p in range(panels)], axis=1)

    mixed = [
        jnp.dot(table_ref[...], hot(query), preferred_element_type=jnp.float32).astype(jnp.bfloat16)
        for query in queries
    ]

    def search(span, first):
        key_hot = jnp.concatenate([hot(keys[i]) for i in span], axis=1)
        key_rows = jnp.concatenate([unit(keys[i]) for i in span], axis=0)
        for j in range(n_queries):
            weight = lax.dot_general(
                key_hot, mixed[j], (((0,), (0,)), ((), ())), preferred_element_type=jnp.float32
            )
            sims = lax.dot_general(
                key_rows, unit(queries[j]), (((1,), (1,)), ((), ())), preferred_element_type=jnp.float32
            )
            score = jnp.where(weight > 0, weight * sims, -1.0)
            best = jnp.full((1, rows), -1.0, jnp.float32) if first else outs[j][...]
            for at, i in enumerate(span):
                part = score[at * rows : (at + 1) * rows, :]
                if own and i + j == 0:
                    k = lax.broadcasted_iota(jnp.int32, (rows, rows), 0)
                    q = lax.broadcasted_iota(jnp.int32, (rows, rows), 1)
                    found = jnp.max(jnp.where(k < q, part, -1.0), axis=0, keepdims=True)
                else:
                    found = jnp.max(part, axis=0, keepdims=True)
                    found = jnp.where(ranks[i] < ranks[n_keys + j], found, -1.0)
                best = jnp.maximum(best, found)
            outs[j][...] = best

    width = n_keys // n_spans
    search(range(width), True)
    for t in range(1, n_spans):
        @pl.when(ranks[t * width] < ranks[0])
        def _():
            search(range(t * width, (t + 1) * width), False)


def best_of(rows, keys, n_spans, queries, table, own):
    width = (keys[0][0].shape[0] - AUX) // rows * LANES
    vmem = pl.BlockSpec(memory_space=pltpu.VMEM)
    ranks = [r for _, r in keys + queries]
    pairs = len(keys) * len(queries) * rows * rows
    return pl.pallas_call(
        functools.partial(best_kernel, rows, len(keys), n_spans, own, ranks),
        out_shape=[jax.ShapeDtypeStruct((1, rows), jnp.float32)] * len(queries),
        in_specs=[vmem] * (1 + len(keys) + len(queries)),
        out_specs=[vmem] * len(queries),
        compiler_params=pltpu.CompilerParams(vmem_limit_bytes=40 * 2**20),
        cost_estimate=pl.CostEstimate(
            flops=2 * pairs * width, bytes_accessed=2 * (len(keys) + len(queries)) * rows * width, transcendentals=0
        ),
    )(table, *[b for b, _ in keys + queries])


def solution(mesh):
    n_clu, n_grp = mesh.shape["clu"], mesh.shape["grp"]
    target = math.sqrt(n_clu * n_grp)
    wide = min(a for a in range(1, n_clu + 1) if n_clu % a == 0 and (a * n_grp >= target or a == n_clu))
    length = n_clu // wide

    def permute(x, move):
        pairs = []
        for z in range(length):
            for a in range(wide):
                for g in range(n_grp):
                    at = move(z, a, g)
                    pairs.append(((at[0] * wide + at[1]) * n_grp + at[2], (z * wide + a) * n_grp + g))
        return lax.ppermute(x, ("clu", "grp"), pairs)

    def turned(a, s, n):
        return a ^ abs(s) if n & (n - 1) == 0 else (a + s) % n

    def shards(embeddings, cluster_id, cluster_group):
        rows = embeddings.shape[0]
        own, table = pack(embeddings, cluster_id, cluster_group, n_clu)

        def rank(z=0, a=0, g=0):
            def of(clu, grp):
                line, place = turned(clu // wide, z, length), turned(clu % wide, a, wide)
                return turned(grp, g, n_grp) * n_clu + line * wide + place

            return of

        def along(x, s):
            return permute(x, lambda z, a, g: (turned(z, s, length), a, g))

        half = length // 2 if length & (length - 1) == 0 else length
        near = [permute(own, lambda z, a, g: (z, turned(a, s, wide), g)) for s in reversed(range(1, wide))]
        middle = along(own, length - 1) if half < length else None
        first = [along(own, s) for s in range(1, half)]
        near = lax.optimization_barrier(near)
        middle, first = lax.optimization_barrier((middle, first))
        near = near[::-1]
        last = [along(middle, s) for s in range(1, half)] if half < length else []
        offsets = list(range(1, half))
        if half < length:
            first = first + [middle]
            offsets += [length - 1] + [(length - 1) ^ s for s in range(1, half)]
        far, far_rank = [], []
        for t in range(1, n_grp):
            for s in range(wide):
                block = near[s - 1] if s else own
                far.append(permute(block, lambda z, a, g: (z, a, turned(g, t, n_grp))))
                far_rank.append(rank(a=s, g=t))
        near = list(zip([own] + near, [rank(a=s) for s in range(wide)]))
        far = list(zip(far, far_rank))
        visit_rank = [rank(z=s) for s in offsets]
        first = list(zip(first, visit_rank))
        last = list(zip(last, visit_rank[len(first) :]))
        best = best_of(rows, near + far, n_grp, near[:1] + first, table, True)
        if last:
            best = best + best_of(rows, near + far, n_grp, last, table, False)
        found = [best[0]] + [along(b, -s) for b, s in zip(best[1:], offsets)]
        return functools.reduce(jnp.maximum, found).reshape(rows)

    placed = (P(("clu", "grp"), None), P(("clu", "grp")), P())
    return jax.shard_map(
        shards, mesh=mesh, in_specs=placed, out_specs=P(("clu", "grp")), check_vma=False
    )
```

```python
import functools
import math

import jax
import jax.numpy as jnp
from jax import lax
from jax.experimental import pallas as pl
from jax.experimental.pallas import tpu as pltpu
from jax.sharding import PartitionSpec as P

LANES = 128
AUX = 8
DIGIT = 256


def pack_kernel(groups, emb_ref, id_ref, group_ref, out_ref, table_ref):
    rows, width = emb_ref.shape
    values = emb_ref[...].astype(jnp.float32)
    scale = lax.rsqrt(jnp.sum(values * values, axis=-1, keepdims=True) + 1e-06)
    unit = (values * scale).astype(jnp.bfloat16)
    for panel in range(width // LANES):
        out_ref[panel * rows : (panel + 1) * rows, :] = unit[:, panel * LANES : (panel + 1) * LANES]
    ids = jnp.broadcast_to(id_ref[...], (AUX, rows))
    row = lax.broadcasted_iota(jnp.int32, (AUX, rows), 0)
    digits = jnp.where(row == 0, ids % DIGIT, ids // DIGIT)
    if LANES > rows:
        digits = jnp.concatenate([digits, jnp.zeros((AUX, LANES - rows), jnp.int32)], axis=1)
    out_ref[width // LANES * rows :, :] = digits.astype(jnp.float32).astype(jnp.bfloat16)
    clusters = group_ref.shape[1]
    index = lax.broadcasted_iota(jnp.int32, (groups, clusters), 0)
    member = jnp.where(index == group_ref[...], 1.0, 0.0).astype(jnp.bfloat16)
    same = lax.dot_general(member, member, (((0,), (0,)), ((), ())), preferred_element_type=jnp.float32)
    one = lax.broadcasted_iota(jnp.int32, (clusters, clusters), 0)
    other = lax.broadcasted_iota(jnp.int32, (clusters, clusters), 1)
    table_ref[...] = jnp.where(one == other, 1.0, 0.5 * same).astype(jnp.bfloat16)


def pack(embeddings, cluster_id, cluster_group, groups):
    rows, width = embeddings.shape
    assert rows <= LANES and width % LANES == 0
    clusters = cluster_group.shape[0]
    return pl.pallas_call(
        functools.partial(pack_kernel, groups),
        out_shape=[pltpu.VMEM((width // LANES * rows + AUX, LANES), jnp.bfloat16), pltpu.VMEM((clusters, clusters), jnp.bfloat16)],
    )(embeddings, cluster_id.reshape(1, rows), cluster_group.reshape(1, clusters))


def one_hot(digits, clusters):
    number = digits[0:1].astype(jnp.int32) + DIGIT * digits[1:2].astype(jnp.int32)
    index = lax.broadcasted_iota(jnp.int32, (clusters, digits.shape[1]), 0)
    return jnp.where(index == number, 1.0, 0.0).astype(jnp.bfloat16)


def best_kernel(rows, n_keys, n_spans, own, ranks, table_ref, *refs):
    n_queries = (len(refs) - n_keys) // 2
    keys, queries, outs = refs[:n_keys], refs[n_keys : n_keys + n_queries], refs[n_keys + n_queries :]
    panels = (keys[0].shape[0] - AUX) // rows
    clusters = table_ref.shape[0]
    clu, grp = lax.axis_index("clu"), lax.axis_index("grp")
    ranks = [rank(clu, grp) for rank in ranks]

    def hot(block):
        return one_hot(block[panels * rows :, :rows].astype(jnp.float32), clusters)

    def unit(block):
        return jnp.concatenate([block[p * rows : (p + 1) * rows, :] for p in range(panels)], axis=1)

    mixed = [
        jnp.dot(table_ref[...], hot(query), preferred_element_type=jnp.float32).astype(jnp.bfloat16)
        for query in queries
    ]

    def search(span, first):
        key_hot = jnp.concatenate([hot(keys[i]) for i in span], axis=1)
        key_rows = jnp.concatenate([unit(keys[i]) for i in span], axis=0)
        for j in range(n_queries):
            weight = lax.dot_general(
                key_hot, mixed[j], (((0,), (0,)), ((), ())), preferred_element_type=jnp.float32
            )
            sims = lax.dot_general(
                key_rows, unit(queries[j]), (((1,), (1,)), ((), ())), preferred_element_type=jnp.float32
            )
            score = jnp.where(weight > 0, weight * sims, -1.0)
            best = jnp.full((1, rows), -1.0, jnp.float32) if first else outs[j][...]
            for at, i in enumerate(span):
                part = score[at * rows : (at + 1) * rows, :]
                if own and i + j == 0:
                    k = lax.broadcasted_iota(jnp.int32, (rows, rows), 0)
                    q = lax.broadcasted_iota(jnp.int32, (rows, rows), 1)
                    found = jnp.max(jnp.where(k < q, part, -1.0), axis=0, keepdims=True)
                else:
                    found = jnp.max(part, axis=0, keepdims=True)
                    found = jnp.where(ranks[i] < ranks[n_keys + j], found, -1.0)
                best = jnp.maximum(best, found)
            outs[j][...] = best

    width = n_keys // n_spans
    search(range(width), True)
    for t in range(1, n_spans):
        @pl.when(ranks[t * width] < ranks[0])
        def _():
            search(range(t * width, (t + 1) * width), False)


def best_of(rows, keys, n_spans, queries, table, own):
    width = (keys[0][0].shape[0] - AUX) // rows * LANES
    vmem = pl.BlockSpec(memory_space=pltpu.VMEM)
    ranks = [r for _, r in keys + queries]
    pairs = len(keys) * len(queries) * rows * rows
    return pl.pallas_call(
        functools.partial(best_kernel, rows, len(keys), n_spans, own, ranks),
        out_shape=[jax.ShapeDtypeStruct((1, rows), jnp.float32)] * len(queries),
        in_specs=[vmem] * (1 + len(keys) + len(queries)),
        out_specs=[vmem] * len(queries),
        compiler_params=pltpu.CompilerParams(vmem_limit_bytes=40 * 2**20),
        cost_estimate=pl.CostEstimate(
            flops=2 * pairs * width, bytes_accessed=2 * (len(keys) + len(queries)) * rows * width, transcendentals=0
        ),
    )(table, *[b for b, _ in keys + queries])


def solution(mesh):
    n_clu, n_grp = mesh.shape["clu"], mesh.shape["grp"]
    target = math.sqrt(n_clu * n_grp)
    wide = min(a for a in range(1, n_clu + 1) if n_clu % a == 0 and (a * n_grp >= target or a == n_clu))
    length = n_clu // wide

    def permute(x, move):
        pairs = []
        for z in range(length):
            for a in range(wide):
                for g in range(n_grp):
                    at = move(z, a, g)
                    pairs.append(((at[0] * wide + at[1]) * n_grp + at[2], (z * wide + a) * n_grp + g))
        return lax.ppermute(x, ("clu", "grp"), pairs)

    def turned(a, s, n):
        return a ^ abs(s) if n & (n - 1) == 0 else (a + s) % n

    def shards(embeddings, cluster_id, cluster_group):
        rows = embeddings.shape[0]
        own, table = pack(embeddings, cluster_id, cluster_group, n_clu)

        def rank(z=0, a=0, g=0):
            def of(clu, grp):
                line, place = turned(clu // wide, z, length), turned(clu % wide, a, wide)
                return turned(grp, g, n_grp) * n_clu + line * wide + place

            return of

        def along(x, s):
            return permute(x, lambda z, a, g: (turned(z, s, length), a, g))

        half = length // 2 if length & (length - 1) == 0 else length
        near = [permute(own, lambda z, a, g: (z, turned(a, s, wide), g)) for s in reversed(range(1, wide))]
        middle = along(own, length - 1) if half < length else None
        first = [along(own, s) for s in range(1, half)]
        near[0], middle = lax.optimization_barrier((near[0], middle))
        near = lax.optimization_barrier(near)
        middle, first = lax.optimization_barrier((middle, first))
        near = near[::-1]
        last = [along(middle, s) for s in range(1, half)] if half < length else []
        offsets = list(range(1, half))
        if half < length:
            first = first + [middle]
            offsets += [length - 1] + [(length - 1) ^ s for s in range(1, half)]
        far, far_rank = [], []
        for t in range(1, n_grp):
            for s in range(wide):
                block = near[s - 1] if s else own
                far.append(permute(block, lambda z, a, g: (z, a, turned(g, t, n_grp))))
                far_rank.append(rank(a=s, g=t))
        near = list(zip([own] + near, [rank(a=s) for s in range(wide)]))
        far = list(zip(far, far_rank))
        visit_rank = [rank(z=s) for s in offsets]
        first = list(zip(first, visit_rank))
        last = list(zip(last, visit_rank[len(first) :]))
        best = best_of(rows, near + far, n_grp, near[:1] + first, table, True)
        if last:
            best = best + best_of(rows, near + far, n_grp, last, table, False)
        found = [best[0]] + [along(b, -s) for b, s in zip(best[1:], offsets)]
        return functools.reduce(jnp.maximum, found).reshape(rows)

    placed = (P(("clu", "grp"), None), P(("clu", "grp")), P())
    return jax.shard_map(
        shards, mesh=mesh, in_specs=placed, out_specs=P(("clu", "grp")), check_vma=False
    )
```

```python
import functools
import math

import jax
import jax.numpy as jnp
from jax import lax
from jax.experimental import pallas as pl
from jax.experimental.pallas import tpu as pltpu
from jax.sharding import PartitionSpec as P

LANES = 128
AUX = 8
DIGIT = 256


def pack_kernel(groups, emb_ref, id_ref, group_ref, out_ref, table_ref):
    rows, width = emb_ref.shape
    values = emb_ref[...].astype(jnp.float32)
    scale = lax.rsqrt(jnp.sum(values * values, axis=-1, keepdims=True) + 1e-06)
    unit = (values * scale).astype(jnp.bfloat16)
    for panel in range(width // LANES):
        out_ref[panel * rows : (panel + 1) * rows, :] = unit[:, panel * LANES : (panel + 1) * LANES]
    ids = jnp.broadcast_to(id_ref[...], (AUX, rows))
    row = lax.broadcasted_iota(jnp.int32, (AUX, rows), 0)
    digits = jnp.where(row == 0, ids % DIGIT, ids // DIGIT)
    if LANES > rows:
        digits = jnp.concatenate([digits, jnp.zeros((AUX, LANES - rows), jnp.int32)], axis=1)
    out_ref[width // LANES * rows :, :] = digits.astype(jnp.float32).astype(jnp.bfloat16)
    clusters = group_ref.shape[1]
    index = lax.broadcasted_iota(jnp.int32, (groups, clusters), 0)
    member = jnp.where(index == group_ref[...], 1.0, 0.0).astype(jnp.bfloat16)
    same = lax.dot_general(member, member, (((0,), (0,)), ((), ())), preferred_element_type=jnp.float32)
    one = lax.broadcasted_iota(jnp.int32, (clusters, clusters), 0)
    other = lax.broadcasted_iota(jnp.int32, (clusters, clusters), 1)
    table_ref[...] = jnp.where(one == other, 1.0, 0.5 * same).astype(jnp.bfloat16)


def pack(embeddings, cluster_id, cluster_group, groups):
    rows, width = embeddings.shape
    assert rows <= LANES and width % LANES == 0
    clusters = cluster_group.shape[0]
    return pl.pallas_call(
        functools.partial(pack_kernel, groups),
        out_shape=[pltpu.VMEM((width // LANES * rows + AUX, LANES), jnp.bfloat16), pltpu.VMEM((clusters, clusters), jnp.bfloat16)],
    )(embeddings, cluster_id.reshape(1, rows), cluster_group.reshape(1, clusters))


def one_hot(digits, clusters):
    number = digits[0:1].astype(jnp.int32) + DIGIT * digits[1:2].astype(jnp.int32)
    index = lax.broadcasted_iota(jnp.int32, (clusters, digits.shape[1]), 0)
    return jnp.where(index == number, 1.0, 0.0).astype(jnp.bfloat16)


def best_kernel(rows, n_keys, n_spans, own, ranks, table_ref, *refs):
    n_queries = (len(refs) - n_keys) // 2
    keys, queries, outs = refs[:n_keys], refs[n_keys : n_keys + n_queries], refs[n_keys + n_queries :]
    panels = (keys[0].shape[0] - AUX) // rows
    clusters = table_ref.shape[0]
    clu, grp = lax.axis_index("clu"), lax.axis_index("grp")
    ranks = [rank(clu, grp) for rank in ranks]

    def hot(block):
        return one_hot(block[panels * rows :, :rows].astype(jnp.float32), clusters)

    def unit(block):
        return jnp.concatenate([block[p * rows : (p + 1) * rows, :] for p in range(panels)], axis=1)

    mixed = [
        jnp.dot(table_ref[...], hot(query), preferred_element_type=jnp.float32).astype(jnp.bfloat16)
        for query in queries
    ]

    def search(span, first):
        key_hot = jnp.concatenate([hot(keys[i]) for i in span], axis=1)
        key_rows = jnp.concatenate([unit(keys[i]) for i in span], axis=0)
        for j in range(n_queries):
            weight = lax.dot_general(
                key_hot, mixed[j], (((0,), (0,)), ((), ())), preferred_element_type=jnp.float32
            )
            sims = lax.dot_general(
                key_rows, unit(queries[j]), (((1,), (1,)), ((), ())), preferred_element_type=jnp.float32
            )
            score = jnp.where(weight > 0, weight * sims, -1.0)
            best = jnp.full((1, rows), -1.0, jnp.float32) if first else outs[j][...]
            for at, i in enumerate(span):
                part = score[at * rows : (at + 1) * rows, :]
                if own and i + j == 0:
                    k = lax.broadcasted_iota(jnp.int32, (rows, rows), 0)
                    q = lax.broadcasted_iota(jnp.int32, (rows, rows), 1)
                    found = jnp.max(jnp.where(k < q, part, -1.0), axis=0, keepdims=True)
                else:
                    found = jnp.max(part, axis=0, keepdims=True)
                    found = jnp.where(ranks[i] < ranks[n_keys + j], found, -1.0)
                best = jnp.maximum(best, found)
            outs[j][...] = best

    width = n_keys // n_spans
    search(range(width), True)
    for t in range(1, n_spans):
        @pl.when(ranks[t * width] < ranks[0])
        def _():
            search(range(t * width, (t + 1) * width), False)


def best_of(rows, keys, n_spans, queries, table, own):
    width = (keys[0][0].shape[0] - AUX) // rows * LANES
    vmem = pl.BlockSpec(memory_space=pltpu.VMEM)
    ranks = [r for _, r in keys + queries]
    pairs = len(keys) * len(queries) * rows * rows
    return pl.pallas_call(
        functools.partial(best_kernel, rows, len(keys), n_spans, own, ranks),
        out_shape=[jax.ShapeDtypeStruct((1, rows), jnp.float32)] * len(queries),
        in_specs=[vmem] * (1 + len(keys) + len(queries)),
        out_specs=[vmem] * len(queries),
        compiler_params=pltpu.CompilerParams(vmem_limit_bytes=40 * 2**20),
        cost_estimate=pl.CostEstimate(
            flops=2 * pairs * width, bytes_accessed=2 * (len(keys) + len(queries)) * rows * width, transcendentals=0
        ),
    )(table, *[b for b, _ in keys + queries])


def solution(mesh):
    n_clu, n_grp = mesh.shape["clu"], mesh.shape["grp"]
    target = math.sqrt(n_clu * n_grp)
    wide = min(a for a in range(1, n_clu + 1) if n_clu % a == 0 and (a * n_grp >= target or a == n_clu))
    length = n_clu // wide

    def permute(x, move):
        pairs = []
        for z in range(length):
            for a in range(wide):
                for g in range(n_grp):
                    at = move(z, a, g)
                    pairs.append(((at[0] * wide + at[1]) * n_grp + at[2], (z * wide + a) * n_grp + g))
        return lax.ppermute(x, ("clu", "grp"), pairs)

    def turned(a, s, n):
        return a ^ abs(s) if n & (n - 1) == 0 else (a + s) % n

    def shards(embeddings, cluster_id, cluster_group):
        rows = embeddings.shape[0]
        own, table = pack(embeddings, cluster_id, cluster_group, n_clu)

        def rank(z=0, a=0, g=0):
            def of(clu, grp):
                line, place = turned(clu // wide, z, length), turned(clu % wide, a, wide)
                return turned(grp, g, n_grp) * n_clu + line * wide + place

            return of

        def along(x, s):
            return permute(x, lambda z, a, g: (turned(z, s, length), a, g))

        half = length // 2 if length & (length - 1) == 0 else length
        near = [permute(own, lambda z, a, g: (z, turned(a, s, wide), g)) for s in reversed(range(1, wide))]
        middle = along(own, length - 1) if half < length else None
        first = [along(own, s) for s in range(1, half)]
        near = lax.optimization_barrier(near)
        middle, first = lax.optimization_barrier((middle, first))
        near = near[::-1]
        last = [along(middle, s) for s in range(1, half)] if half < length else []
        offsets = list(range(1, half))
        if half < length:
            first = first + [middle]
            offsets += [length - 1] + [(length - 1) ^ s for s in range(1, half)]
        far, far_rank = [], []
        for t in range(1, n_grp):
            swapped = []
            for s in range(wide):
                block = near[s - 1] if s else own
                if s and s == wide - 1:
                    swapped[0], block = lax.optimization_barrier((swapped[0], block))
                swapped.append(permute(block, lambda z, a, g: (z, a, turned(g, t, n_grp))))
                far_rank.append(rank(a=s, g=t))
            far += swapped
        near = list(zip([own] + near, [rank(a=s) for s in range(wide)]))
        far = list(zip(far, far_rank))
        visit_rank = [rank(z=s) for s in offsets]
        first = list(zip(first, visit_rank))
        last = list(zip(last, visit_rank[len(first) :]))
        best = best_of(rows, near + far, n_grp, near[:1] + first, table, True)
        if last:
            best = best + best_of(rows, near + far, n_grp, last, table, False)
        found = [best[0]] + [along(b, -s) for b, s in zip(best[1:], offsets)]
        return functools.reduce(jnp.maximum, found).reshape(rows)

    placed = (P(("clu", "grp"), None), P(("clu", "grp")), P())
    return jax.shard_map(
        shards, mesh=mesh, in_specs=placed, out_specs=P(("clu", "grp")), check_vma=False
    )
```

```python
import functools
import math

import jax
import jax.numpy as jnp
from jax import lax
from jax.experimental import pallas as pl
from jax.experimental.pallas import tpu as pltpu
from jax.sharding import PartitionSpec as P

LANES = 128
AUX = 8
DIGIT = 256


def pack_kernel(emb_ref, id_ref, out_ref):
    rows, width = emb_ref.shape
    values = emb_ref[...].astype(jnp.float32)
    scale = lax.rsqrt(jnp.sum(values * values, axis=-1, keepdims=True) + 1e-06)
    unit = (values * scale).astype(jnp.bfloat16)
    for panel in range(width // LANES):
        out_ref[panel * rows : (panel + 1) * rows, :] = unit[:, panel * LANES : (panel + 1) * LANES]
    ids = jnp.broadcast_to(id_ref[...], (AUX, rows))
    row = lax.broadcasted_iota(jnp.int32, (AUX, rows), 0)
    digits = jnp.where(row == 0, ids % DIGIT, ids // DIGIT)
    if LANES > rows:
        digits = jnp.concatenate([digits, jnp.zeros((AUX, LANES - rows), jnp.int32)], axis=1)
    out_ref[width // LANES * rows :, :] = digits.astype(jnp.float32).astype(jnp.bfloat16)


def pack(embeddings, cluster_id):
    rows, width = embeddings.shape
    assert rows <= LANES and width % LANES == 0
    return pl.pallas_call(
        pack_kernel,
        out_shape=pltpu.VMEM((width // LANES * rows + AUX, LANES), jnp.bfloat16),
    )(embeddings, cluster_id.reshape(1, rows))


def make_table(group_ref, groups):
    clusters = group_ref.shape[1]
    index = lax.broadcasted_iota(jnp.int32, (groups, clusters), 0)
    member = jnp.where(index == group_ref[...], 1.0, 0.0).astype(jnp.bfloat16)
    same = lax.dot_general(member, member, (((0,), (0,)), ((), ())), preferred_element_type=jnp.float32)
    one = lax.broadcasted_iota(jnp.int32, (clusters, clusters), 0)
    other = lax.broadcasted_iota(jnp.int32, (clusters, clusters), 1)
    return jnp.where(one == other, 1.0, 0.5 * same).astype(jnp.bfloat16)


def one_hot(digits, clusters):
    number = digits[0:1].astype(jnp.int32) + DIGIT * digits[1:2].astype(jnp.int32)
    index = lax.broadcasted_iota(jnp.int32, (clusters, digits.shape[1]), 0)
    return jnp.where(index == number, 1.0, 0.0).astype(jnp.bfloat16)


def best_kernel(rows, groups, n_keys, n_spans, own, ranks, first_ref, *refs):
    n_queries = (len(refs) - n_keys) // 2
    keys, queries, outs = refs[:n_keys], refs[n_keys : n_keys + n_queries], refs[n_keys + n_queries :]
    panels = (keys[0].shape[0] - AUX) // rows
    clusters = first_ref.shape[1]
    if own:
        table = make_table(first_ref, groups)
        outs[n_queries][...] = table
    else:
        table = first_ref[...]
    clu, grp = lax.axis_index("clu"), lax.axis_index("grp")
    ranks = [rank(clu, grp) for rank in ranks]

    def hot(block):
        return one_hot(block[panels * rows :, :rows].astype(jnp.float32), clusters)

    def unit(block):
        return jnp.concatenate([block[p * rows : (p + 1) * rows, :] for p in range(panels)], axis=1)

    mixed = [
        jnp.dot(table, hot(query), preferred_element_type=jnp.float32).astype(jnp.bfloat16)
        for query in queries
    ]

    def search(span, first):
        key_hot = jnp.concatenate([hot(keys[i]) for i in span], axis=1)
        key_rows = jnp.concatenate([unit(keys[i]) for i in span], axis=0)
        for j in range(n_queries):
            weight = lax.dot_general(
                key_hot, mixed[j], (((0,), (0,)), ((), ())), preferred_element_type=jnp.float32
            )
            sims = lax.dot_general(
                key_rows, unit(queries[j]), (((1,), (1,)), ((), ())), preferred_element_type=jnp.float32
            )
            score = jnp.where(weight > 0, weight * sims, -1.0)
            best = jnp.full((1, rows), -1.0, jnp.float32) if first else outs[j][...]
            for at, i in enumerate(span):
                part = score[at * rows : (at + 1) * rows, :]
                if own and i + j == 0:
                    k = lax.broadcasted_iota(jnp.int32, (rows, rows), 0)
                    q = lax.broadcasted_iota(jnp.int32, (rows, rows), 1)
                    found = jnp.max(jnp.where(k < q, part, -1.0), axis=0, keepdims=True)
                else:
                    found = jnp.max(part, axis=0, keepdims=True)
                    found = jnp.where(ranks[i] < ranks[n_keys + j], found, -1.0)
                best = jnp.maximum(best, found)
            outs[j][...] = best

    width = n_keys // n_spans
    search(range(width), True)
    for t in range(1, n_spans):
        @pl.when(ranks[t * width] < ranks[0])
        def _():
            search(range(t * width, (t + 1) * width), False)


def best_of(rows, groups, keys, n_spans, queries, first, own):
    width = (keys[0][0].shape[0] - AUX) // rows * LANES
    vmem = pl.BlockSpec(memory_space=pltpu.VMEM)
    ranks = [r for _, r in keys + queries]
    pairs = len(keys) * len(queries) * rows * rows
    clusters = first.shape[1]
    made = [jax.ShapeDtypeStruct((clusters, clusters), jnp.bfloat16)] if own else []
    return pl.pallas_call(
        functools.partial(best_kernel, rows, groups, len(keys), n_spans, own, ranks),
        out_shape=[jax.ShapeDtypeStruct((1, rows), jnp.float32)] * len(queries) + made,
        in_specs=[vmem] * (1 + len(keys) + len(queries)),
        out_specs=[vmem] * (len(queries) + len(made)),
        compiler_params=pltpu.CompilerParams(vmem_limit_bytes=40 * 2**20),
        cost_estimate=pl.CostEstimate(
            flops=2 * pairs * width, bytes_accessed=2 * (len(keys) + len(queries)) * rows * width, transcendentals=0
        ),
    )(first, *[b for b, _ in keys + queries])


def solution(mesh):
    n_clu, n_grp = mesh.shape["clu"], mesh.shape["grp"]
    target = math.sqrt(n_clu * n_grp)
    wide = min(a for a in range(1, n_clu + 1) if n_clu % a == 0 and (a * n_grp >= target or a == n_clu))
    length = n_clu // wide

    def permute(x, move):
        pairs = []
        for z in range(length):
            for a in range(wide):
                for g in range(n_grp):
                    at = move(z, a, g)
                    pairs.append(((at[0] * wide + at[1]) * n_grp + at[2], (z * wide + a) * n_grp + g))
        return lax.ppermute(x, ("clu", "grp"), pairs)

    def turned(a, s, n):
        return a ^ abs(s) if n & (n - 1) == 0 else (a + s) % n

    def shards(embeddings, cluster_id, cluster_group):
        rows = embeddings.shape[0]
        own = pack(embeddings, cluster_id)

        def rank(z=0, a=0, g=0):
            def of(clu, grp):
                line, place = turned(clu // wide, z, length), turned(clu % wide, a, wide)
                return turned(grp, g, n_grp) * n_clu + line * wide + place

            return of

        def along(x, s):
            return permute(x, lambda z, a, g: (turned(z, s, length), a, g))

        half = length // 2 if length & (length - 1) == 0 else length
        near = [permute(own, lambda z, a, g: (z, turned(a, s, wide), g)) for s in reversed(range(1, wide))]
        middle = along(own, length - 1) if half < length else None
        first = [along(own, s) for s in range(1, half)]
        near = lax.optimization_barrier(near)
        middle, first = lax.optimization_barrier((middle, first))
        near = near[::-1]
        last = [along(middle, s) for s in range(1, half)] if half < length else []
        offsets = list(range(1, half))
        if half < length:
            first = first + [middle]
            offsets += [length - 1] + [(length - 1) ^ s for s in range(1, half)]
        far, far_rank = [], []
        for t in range(1, n_grp):
            for s in range(wide):
                block = near[s - 1] if s else own
                far.append(permute(block, lambda z, a, g: (z, a, turned(g, t, n_grp))))
                far_rank.append(rank(a=s, g=t))
        near = list(zip([own] + near, [rank(a=s) for s in range(wide)]))
        far = list(zip(far, far_rank))
        visit_rank = [rank(z=s) for s in offsets]
        first = list(zip(first, visit_rank))
        last = list(zip(last, visit_rank[len(first) :]))
        *best, table = best_of(rows, n_clu, near + far, n_grp, near[:1] + first, cluster_group.reshape(1, -1), True)
        if last:
            best += best_of(rows, n_clu, near + far, n_grp, last, table, False)
        found = [best[0]] + [along(b, -s) for b, s in zip(best[1:], offsets)]
        return functools.reduce(jnp.maximum, found).reshape(rows)

    placed = (P(("clu", "grp"), None), P(("clu", "grp")), P())
    return jax.shard_map(
        shards, mesh=mesh, in_specs=placed, out_specs=P(("clu", "grp")), check_vma=False
    )
```

```python
import functools
import math

import jax
import jax.numpy as jnp
from jax import lax
from jax.experimental import pallas as pl
from jax.experimental.pallas import tpu as pltpu
from jax.sharding import PartitionSpec as P

LANES = 128
AUX = 8
DIGIT = 256


def pack_kernel(groups, emb_ref, id_ref, group_ref, out_ref, table_ref):
    rows, width = emb_ref.shape
    values = emb_ref[...].astype(jnp.float32)
    scale = lax.rsqrt(jnp.sum(values * values, axis=-1, keepdims=True) + 1e-06)
    unit = (values * scale).astype(jnp.bfloat16)
    for panel in range(width // LANES):
        out_ref[panel * rows : (panel + 1) * rows, :] = unit[:, panel * LANES : (panel + 1) * LANES]
    ids = jnp.broadcast_to(id_ref[...], (AUX, rows))
    row = lax.broadcasted_iota(jnp.int32, (AUX, rows), 0)
    digits = jnp.where(row == 0, ids % DIGIT, ids // DIGIT)
    if LANES > rows:
        digits = jnp.concatenate([digits, jnp.zeros((AUX, LANES - rows), jnp.int32)], axis=1)
    out_ref[width // LANES * rows :, :] = digits.astype(jnp.float32).astype(jnp.bfloat16)
    clusters = group_ref.shape[1]
    index = lax.broadcasted_iota(jnp.int32, (groups, clusters), 0)
    member = jnp.where(index == group_ref[...], 1.0, 0.0).astype(jnp.bfloat16)
    same = lax.dot_general(member, member, (((0,), (0,)), ((), ())), preferred_element_type=jnp.float32)
    one = lax.broadcasted_iota(jnp.int32, (clusters, clusters), 0)
    other = lax.broadcasted_iota(jnp.int32, (clusters, clusters), 1)
    table_ref[...] = jnp.where(one == other, 1.0, 0.5 * same).astype(jnp.bfloat16)


def pack(embeddings, cluster_id, cluster_group, groups):
    rows, width = embeddings.shape
    assert rows <= LANES and width % LANES == 0
    clusters = cluster_group.shape[0]
    return pl.pallas_call(
        functools.partial(pack_kernel, groups),
        out_shape=[pltpu.VMEM((width // LANES * rows + AUX, LANES), jnp.bfloat16), pltpu.VMEM((clusters, clusters), jnp.bfloat16)],
    )(embeddings, cluster_id.reshape(1, rows), cluster_group.reshape(1, clusters))


def one_hot(digits, clusters):
    number = digits[0:1].astype(jnp.int32) + DIGIT * digits[1:2].astype(jnp.int32)
    index = lax.broadcasted_iota(jnp.int32, (clusters, digits.shape[1]), 0)
    return jnp.where(index == number, 1.0, 0.0).astype(jnp.bfloat16)


def best_kernel(rows, n_keys, n_spans, own, ranks, table_ref, *refs):
    n_queries = (len(refs) - n_keys) // 2
    keys, queries, outs = refs[:n_keys], refs[n_keys : n_keys + n_queries], refs[n_keys + n_queries :]
    panels = (keys[0].shape[0] - AUX) // rows
    clusters = table_ref.shape[0]
    clu, grp = lax.axis_index("clu"), lax.axis_index("grp")
    ranks = [rank(clu, grp) for rank in ranks]

    def hot(block):
        return one_hot(block[panels * rows :, :rows].astype(jnp.float32), clusters)

    def unit(block):
        return jnp.concatenate([block[p * rows : (p + 1) * rows, :] for p in range(panels)], axis=1)

    mixed = [
        jnp.dot(table_ref[...], hot(query), preferred_element_type=jnp.float32).astype(jnp.bfloat16)
        for query in queries
    ]

    def search(span, first):
        key_hot = jnp.concatenate([hot(keys[i]) for i in span], axis=1)
        key_rows = jnp.concatenate([unit(keys[i]) for i in span], axis=0)
        for j in range(n_queries):
            weight = lax.dot_general(
                key_hot, mixed[j], (((0,), (0,)), ((), ())), preferred_element_type=jnp.float32
            )
            sims = lax.dot_general(
                key_rows, unit(queries[j]), (((1,), (1,)), ((), ())), preferred_element_type=jnp.float32
            )
            score = jnp.where(weight > 0, weight * sims, -1.0)
            best = jnp.full((1, rows), -1.0, jnp.float32) if first else outs[j][...]
            for at, i in enumerate(span):
                part = score[at * rows : (at + 1) * rows, :]
                if own and i + j == 0:
                    k = lax.broadcasted_iota(jnp.int32, (rows, rows), 0)
                    q = lax.broadcasted_iota(jnp.int32, (rows, rows), 1)
                    found = jnp.max(jnp.where(k < q, part, -1.0), axis=0, keepdims=True)
                else:
                    found = jnp.max(part, axis=0, keepdims=True)
                    found = jnp.where(ranks[i] < ranks[n_keys + j], found, -1.0)
                best = jnp.maximum(best, found)
            outs[j][...] = best

    width = n_keys // n_spans
    search(range(width), True)
    for t in range(1, n_spans):
        @pl.when(ranks[t * width] < ranks[0])
        def _():
            search(range(t * width, (t + 1) * width), False)


def best_of(rows, keys, n_spans, queries, table, own):
    width = (keys[0][0].shape[0] - AUX) // rows * LANES
    vmem = pl.BlockSpec(memory_space=pltpu.VMEM)
    ranks = [r for _, r in keys + queries]
    pairs = len(keys) * len(queries) * rows * rows
    return pl.pallas_call(
        functools.partial(best_kernel, rows, len(keys), n_spans, own, ranks),
        out_shape=[jax.ShapeDtypeStruct((1, rows), jnp.float32)] * len(queries),
        in_specs=[vmem] * (1 + len(keys) + len(queries)),
        out_specs=[vmem] * len(queries),
        compiler_params=pltpu.CompilerParams(vmem_limit_bytes=40 * 2**20),
        cost_estimate=pl.CostEstimate(
            flops=2 * pairs * width, bytes_accessed=2 * (len(keys) + len(queries)) * rows * width, transcendentals=0
        ),
    )(table, *[b for b, _ in keys + queries])


def solution(mesh):
    n_clu, n_grp = mesh.shape["clu"], mesh.shape["grp"]
    target = math.sqrt(n_clu * n_grp)
    wide = min(a for a in range(1, n_clu + 1) if n_clu % a == 0 and (a * n_grp >= target or a == n_clu))
    length = n_clu // wide

    def permute(x, move):
        pairs = []
        for z in range(length):
            for a in range(wide):
                for g in range(n_grp):
                    at = move(z, a, g)
                    pairs.append(((at[0] * wide + at[1]) * n_grp + at[2], (z * wide + a) * n_grp + g))
        return lax.ppermute(x, ("clu", "grp"), pairs)

    def turned(a, s, n):
        return a ^ abs(s) if n & (n - 1) == 0 else (a + s) % n

    def shards(embeddings, cluster_id, cluster_group):
        rows = embeddings.shape[0]
        own, table = pack(embeddings, cluster_id, cluster_group, n_clu)

        def rank(z=0, a=0, g=0):
            def of(clu, grp):
                line, place = turned(clu // wide, z, length), turned(clu % wide, a, wide)
                return turned(grp, g, n_grp) * n_clu + line * wide + place

            return of

        def along(x, s):
            return permute(x, lambda z, a, g: (turned(z, s, length), a, g))

        half = length // 2 if length & (length - 1) == 0 else length
        near = [permute(own, lambda z, a, g: (z, turned(a, s, wide), g)) for s in range(1, wide)]
        middle = along(own, length - 1) if half < length else None
        first = [along(own, s) for s in range(1, half)]
        near = lax.optimization_barrier(near)
        middle, first = lax.optimization_barrier((middle, first))
        last = [along(middle, s) for s in range(1, half)] if half < length else []
        offsets = list(range(1, half))
        if half < length:
            first = first + [middle]
            offsets += [length - 1] + [(length - 1) ^ s for s in range(1, half)]
        far, far_rank = [], []
        for t in range(1, n_grp):
            for s in range(wide):
                block = near[s - 1] if s else own
                far.append(permute(block, lambda z, a, g: (z, a, turned(g, t, n_grp))))
                far_rank.append(rank(a=s, g=t))
        near = list(zip([own] + near, [rank(a=s) for s in range(wide)]))
        far = list(zip(far, far_rank))
        visit_rank = [rank(z=s) for s in offsets]
        first = list(zip(first, visit_rank))
        last = list(zip(last, visit_rank[len(first) :]))
        best = best_of(rows, near + far, n_grp, near[:1] + first, table, True)
        if last:
            best = best + best_of(rows, near + far, n_grp, last, table, False)
        found = [best[0]] + [along(b, -s) for b, s in zip(best[1:], offsets)]
        return functools.reduce(jnp.maximum, found).reshape(rows)

    placed = (P(("clu", "grp"), None), P(("clu", "grp")), P())
    return jax.shard_map(
        shards, mesh=mesh, in_specs=placed, out_specs=P(("clu", "grp")), check_vma=False
    )
```

```python
import functools
import math

import jax
import jax.numpy as jnp
from jax import lax
from jax.experimental import pallas as pl
from jax.experimental.pallas import tpu as pltpu
from jax.sharding import PartitionSpec as P

LANES = 128
AUX = 8
DIGIT = 256


def pack_kernel(groups, emb_ref, id_ref, group_ref, out_ref, table_ref):
    rows, width = emb_ref.shape
    values = emb_ref[...].astype(jnp.float32)
    scale = lax.rsqrt(jnp.sum(values * values, axis=-1, keepdims=True) + 1e-06)
    unit = (values * scale).astype(jnp.bfloat16)
    for panel in range(width // LANES):
        out_ref[panel * rows : (panel + 1) * rows, :] = unit[:, panel * LANES : (panel + 1) * LANES]
    ids = jnp.broadcast_to(id_ref[...], (AUX, rows))
    row = lax.broadcasted_iota(jnp.int32, (AUX, rows), 0)
    digits = jnp.where(row == 0, ids % DIGIT, ids // DIGIT)
    if LANES > rows:
        digits = jnp.concatenate([digits, jnp.zeros((AUX, LANES - rows), jnp.int32)], axis=1)
    out_ref[width // LANES * rows :, :] = digits.astype(jnp.float32).astype(jnp.bfloat16)
    clusters = group_ref.shape[1]
    index = lax.broadcasted_iota(jnp.int32, (groups, clusters), 0)
    member = jnp.where(index == group_ref[...], 1.0, 0.0).astype(jnp.bfloat16)
    same = lax.dot_general(member, member, (((0,), (0,)), ((), ())), preferred_element_type=jnp.float32)
    one = lax.broadcasted_iota(jnp.int32, (clusters, clusters), 0)
    other = lax.broadcasted_iota(jnp.int32, (clusters, clusters), 1)
    table_ref[...] = jnp.where(one == other, 1.0, 0.5 * same).astype(jnp.bfloat16)


def pack(embeddings, cluster_id, cluster_group, groups):
    rows, width = embeddings.shape
    assert rows <= LANES and width % LANES == 0
    clusters = cluster_group.shape[0]
    return pl.pallas_call(
        functools.partial(pack_kernel, groups),
        out_shape=[pltpu.VMEM((width // LANES * rows + AUX, LANES), jnp.bfloat16), pltpu.VMEM((clusters, clusters), jnp.bfloat16)],
    )(embeddings, cluster_id.reshape(1, rows), cluster_group.reshape(1, clusters))


def one_hot(digits, clusters):
    number = digits[0:1].astype(jnp.int32) + DIGIT * digits[1:2].astype(jnp.int32)
    index = lax.broadcasted_iota(jnp.int32, (clusters, digits.shape[1]), 0)
    return jnp.where(index == number, 1.0, 0.0).astype(jnp.bfloat16)


def best_kernel(rows, n_keys, n_spans, own, ranks, table_ref, *refs):
    n_queries = (len(refs) - n_keys) // 2
    keys, queries, outs = refs[:n_keys], refs[n_keys : n_keys + n_queries], refs[n_keys + n_queries :]
    panels = (keys[0].shape[0] - AUX) // rows
    clusters = table_ref.shape[0]
    clu, grp = lax.axis_index("clu"), lax.axis_index("grp")
    ranks = [rank(clu, grp) for rank in ranks]

    def hot(block):
        return one_hot(block[panels * rows :, :rows].astype(jnp.float32), clusters)

    def unit(block):
        return jnp.concatenate([block[p * rows : (p + 1) * rows, :] for p in range(panels)], axis=1)

    mixed = [
        jnp.dot(table_ref[...], hot(query), preferred_element_type=jnp.float32).astype(jnp.bfloat16)
        for query in queries
    ]

    def search(span, first):
        key_hot = jnp.concatenate([hot(keys[i]) for i in span], axis=1)
        key_rows = jnp.concatenate([unit(keys[i]) for i in span], axis=0)
        for j in range(n_queries):
            weight = lax.dot_general(
                key_hot, mixed[j], (((0,), (0,)), ((), ())), preferred_element_type=jnp.float32
            )
            sims = lax.dot_general(
                key_rows, unit(queries[j]), (((1,), (1,)), ((), ())), preferred_element_type=jnp.float32
            )
            score = jnp.where(weight > 0, weight * sims, -1.0)
            best = jnp.full((1, rows), -1.0, jnp.float32) if first else outs[j][...]
            for at, i in enumerate(span):
                part = score[at * rows : (at + 1) * rows, :]
                if own and i + j == 0:
                    k = lax.broadcasted_iota(jnp.int32, (rows, rows), 0)
                    q = lax.broadcasted_iota(jnp.int32, (rows, rows), 1)
                    found = jnp.max(jnp.where(k < q, part, -1.0), axis=0, keepdims=True)
                else:
                    found = jnp.max(part, axis=0, keepdims=True)
                    found = jnp.where(ranks[i] < ranks[n_keys + j], found, -1.0)
                best = jnp.maximum(best, found)
            outs[j][...] = best

    width = n_keys // n_spans
    search(range(width), True)
    for t in range(1, n_spans):
        @pl.when(ranks[t * width] < ranks[0])
        def _():
            search(range(t * width, (t + 1) * width), False)


def best_of(rows, keys, n_spans, queries, table, own):
    width = (keys[0][0].shape[0] - AUX) // rows * LANES
    vmem = pl.BlockSpec(memory_space=pltpu.VMEM)
    ranks = [r for _, r in keys + queries]
    pairs = len(keys) * len(queries) * rows * rows
    return pl.pallas_call(
        functools.partial(best_kernel, rows, len(keys), n_spans, own, ranks),
        out_shape=[jax.ShapeDtypeStruct((1, rows), jnp.float32)] * len(queries),
        in_specs=[vmem] * (1 + len(keys) + len(queries)),
        out_specs=[vmem] * len(queries),
        compiler_params=pltpu.CompilerParams(vmem_limit_bytes=40 * 2**20),
        cost_estimate=pl.CostEstimate(
            flops=2 * pairs * width, bytes_accessed=2 * (len(keys) + len(queries)) * rows * width, transcendentals=0
        ),
    )(table, *[b for b, _ in keys + queries])


def solution(mesh):
    n_clu, n_grp = mesh.shape["clu"], mesh.shape["grp"]
    target = math.sqrt(n_clu * n_grp)
    wide = min(a for a in range(1, n_clu + 1) if n_clu % a == 0 and (a * n_grp >= target or a == n_clu))
    length = n_clu // wide

    def permute(x, move):
        pairs = []
        for z in range(length):
            for a in range(wide):
                for g in range(n_grp):
                    at = move(z, a, g)
                    pairs.append(((at[0] * wide + at[1]) * n_grp + at[2], (z * wide + a) * n_grp + g))
        return lax.ppermute(x, ("clu", "grp"), pairs)

    def turned(a, s, n):
        return a ^ abs(s) if n & (n - 1) == 0 else (a + s) % n

    def shards(embeddings, cluster_id, cluster_group):
        rows = embeddings.shape[0]
        own, table = pack(embeddings, cluster_id, cluster_group, n_clu)

        def rank(z=0, a=0, g=0):
            def of(clu, grp):
                line, place = turned(clu // wide, z, length), turned(clu % wide, a, wide)
                return turned(grp, g, n_grp) * n_clu + line * wide + place

            return of

        def along(x, s):
            return permute(x, lambda z, a, g: (turned(z, s, length), a, g))

        half = length // 2 if length & (length - 1) == 0 else length
        near = [permute(own, lambda z, a, g: (z, turned(a, s, wide), g)) for s in range(1, wide)]
        middle = along(own, length - 1) if half < length else None
        first = [along(own, s) for s in range(1, half)]
        near[0], middle = lax.optimization_barrier((near[0], middle))
        near = lax.optimization_barrier(near)
        middle, first = lax.optimization_barrier((middle, first))
        last = [along(middle, s) for s in range(1, half)] if half < length else []
        offsets = list(range(1, half))
        if half < length:
            first = first + [middle]
            offsets += [length - 1] + [(length - 1) ^ s for s in range(1, half)]
        far, far_rank = [], []
        for t in range(1, n_grp):
            for s in range(wide):
                block = near[s - 1] if s else own
                far.append(permute(block, lambda z, a, g: (z, a, turned(g, t, n_grp))))
                far_rank.append(rank(a=s, g=t))
        near = list(zip([own] + near, [rank(a=s) for s in range(wide)]))
        far = list(zip(far, far_rank))
        visit_rank = [rank(z=s) for s in offsets]
        first = list(zip(first, visit_rank))
        last = list(zip(last, visit_rank[len(first) :]))
        best = best_of(rows, near + far, n_grp, near[:1] + first, table, True)
        if last:
            best = best + best_of(rows, near + far, n_grp, last, table, False)
        found = [best[0]] + [along(b, -s) for b, s in zip(best[1:], offsets)]
        return functools.reduce(jnp.maximum, found).reshape(rows)

    placed = (P(("clu", "grp"), None), P(("clu", "grp")), P())
    return jax.shard_map(
        shards, mesh=mesh, in_specs=placed, out_specs=P(("clu", "grp")), check_vma=False
    )
```

```python
import functools
import math

import jax
import jax.numpy as jnp
from jax import lax
from jax.experimental import pallas as pl
from jax.experimental.pallas import tpu as pltpu
from jax.sharding import PartitionSpec as P

LANES = 128
AUX = 8
DIGIT = 256


def pack_kernel(groups, emb_ref, id_ref, group_ref, out_ref, table_ref):
    rows, width = emb_ref.shape
    values = emb_ref[...].astype(jnp.float32)
    scale = lax.rsqrt(jnp.sum(values * values, axis=-1, keepdims=True) + 1e-06)
    unit = (values * scale).astype(jnp.bfloat16)
    for panel in range(width // LANES):
        out_ref[panel * rows : (panel + 1) * rows, :] = unit[:, panel * LANES : (panel + 1) * LANES]
    ids = jnp.broadcast_to(id_ref[...], (AUX, rows))
    row = lax.broadcasted_iota(jnp.int32, (AUX, rows), 0)
    digits = jnp.where(row == 0, ids % DIGIT, ids // DIGIT)
    if LANES > rows:
        digits = jnp.concatenate([digits, jnp.zeros((AUX, LANES - rows), jnp.int32)], axis=1)
    out_ref[width // LANES * rows :, :] = digits.astype(jnp.float32).astype(jnp.bfloat16)
    clusters = group_ref.shape[1]
    index = lax.broadcasted_iota(jnp.int32, (groups, clusters), 0)
    member = jnp.where(index == group_ref[...], 1.0, 0.0).astype(jnp.bfloat16)
    same = lax.dot_general(member, member, (((0,), (0,)), ((), ())), preferred_element_type=jnp.float32)
    one = lax.broadcasted_iota(jnp.int32, (clusters, clusters), 0)
    other = lax.broadcasted_iota(jnp.int32, (clusters, clusters), 1)
    table_ref[...] = jnp.where(one == other, 1.0, 0.5 * same).astype(jnp.bfloat16)


def pack(embeddings, cluster_id, cluster_group, groups):
    rows, width = embeddings.shape
    assert rows <= LANES and width % LANES == 0
    clusters = cluster_group.shape[0]
    return pl.pallas_call(
        functools.partial(pack_kernel, groups),
        out_shape=[pltpu.VMEM((width // LANES * rows + AUX, LANES), jnp.bfloat16), pltpu.VMEM((clusters, clusters), jnp.bfloat16)],
    )(embeddings, cluster_id.reshape(1, rows), cluster_group.reshape(1, clusters))


def one_hot(digits, clusters):
    number = digits[0:1].astype(jnp.int32) + DIGIT * digits[1:2].astype(jnp.int32)
    index = lax.broadcasted_iota(jnp.int32, (clusters, digits.shape[1]), 0)
    return jnp.where(index == number, 1.0, 0.0).astype(jnp.bfloat16)


def best_kernel(rows, n_keys, n_spans, own, ranks, table_ref, *refs):
    n_queries = (len(refs) - n_keys) // 2
    keys, queries, outs = refs[:n_keys], refs[n_keys : n_keys + n_queries], refs[n_keys + n_queries :]
    panels = (keys[0].shape[0] - AUX) // rows
    clusters = table_ref.shape[0]
    clu, grp = lax.axis_index("clu"), lax.axis_index("grp")
    ranks = [rank(clu, grp) for rank in ranks]

    def hot(block):
        return one_hot(block[panels * rows :, :rows].astype(jnp.float32), clusters)

    def unit(block):
        return jnp.concatenate([block[p * rows : (p + 1) * rows, :] for p in range(panels)], axis=1)

    mixed = [
        jnp.dot(table_ref[...], hot(query), preferred_element_type=jnp.float32).astype(jnp.bfloat16)
        for query in queries
    ]

    def search(span, first):
        key_hot = jnp.concatenate([hot(keys[i]) for i in span], axis=1)
        key_rows = jnp.concatenate([unit(keys[i]) for i in span], axis=0)
        for j in range(n_queries):
            weight = lax.dot_general(
                key_hot, mixed[j], (((0,), (0,)), ((), ())), preferred_element_type=jnp.float32
            )
            sims = lax.dot_general(
                key_rows, unit(queries[j]), (((1,), (1,)), ((), ())), preferred_element_type=jnp.float32
            )
            score = jnp.where(weight > 0, weight * sims, -1.0)
            best = jnp.full((1, rows), -1.0, jnp.float32) if first else outs[j][...]
            for at, i in enumerate(span):
                part = score[at * rows : (at + 1) * rows, :]
                if own and i + j == 0:
                    k = lax.broadcasted_iota(jnp.int32, (rows, rows), 0)
                    q = lax.broadcasted_iota(jnp.int32, (rows, rows), 1)
                    found = jnp.max(jnp.where(k < q, part, -1.0), axis=0, keepdims=True)
                else:
                    found = jnp.max(part, axis=0, keepdims=True)
                    found = jnp.where(ranks[i] < ranks[n_keys + j], found, -1.0)
                best = jnp.maximum(best, found)
            outs[j][...] = best

    width = n_keys // n_spans
    search(range(width), True)
    for t in range(1, n_spans):
        @pl.when(ranks[t * width] < ranks[0])
        def _():
            search(range(t * width, (t + 1) * width), False)


def best_of(rows, keys, n_spans, queries, table, own):
    width = (keys[0][0].shape[0] - AUX) // rows * LANES
    vmem = pl.BlockSpec(memory_space=pltpu.VMEM)
    ranks = [r for _, r in keys + queries]
    pairs = len(keys) * len(queries) * rows * rows
    return pl.pallas_call(
        functools.partial(best_kernel, rows, len(keys), n_spans, own, ranks),
        out_shape=[jax.ShapeDtypeStruct((1, rows), jnp.float32)] * len(queries),
        in_specs=[vmem] * (1 + len(keys) + len(queries)),
        out_specs=[vmem] * len(queries),
        compiler_params=pltpu.CompilerParams(vmem_limit_bytes=40 * 2**20),
        cost_estimate=pl.CostEstimate(
            flops=2 * pairs * width, bytes_accessed=2 * (len(keys) + len(queries)) * rows * width, transcendentals=0
        ),
    )(table, *[b for b, _ in keys + queries])


def solution(mesh):
    n_clu, n_grp = mesh.shape["clu"], mesh.shape["grp"]
    target = math.sqrt(n_clu * n_grp)
    wide = min(a for a in range(1, n_clu + 1) if n_clu % a == 0 and (a * n_grp >= target or a == n_clu))
    length = n_clu // wide

    def permute(x, move):
        pairs = []
        for z in range(length):
            for a in range(wide):
                for g in range(n_grp):
                    at = move(z, a, g)
                    pairs.append(((at[0] * wide + at[1]) * n_grp + at[2], (z * wide + a) * n_grp + g))
        return lax.ppermute(x, ("clu", "grp"), pairs)

    def turned(a, s, n):
        return a ^ abs(s) if n & (n - 1) == 0 else (a + s) % n

    def shards(embeddings, cluster_id, cluster_group):
        rows = embeddings.shape[0]
        own, table = pack(embeddings, cluster_id, cluster_group, n_clu)

        def rank(z=0, a=0, g=0):
            def of(clu, grp):
                line, place = turned(clu // wide, z, length), turned(clu % wide, a, wide)
                return turned(grp, g, n_grp) * n_clu + line * wide + place

            return of

        def along(x, s):
            return permute(x, lambda z, a, g: (turned(z, s, length), a, g))

        half = length // 2 if length & (length - 1) == 0 else length
        order = sorted(range(1, wide), key=lambda s: (s & (s - 1) != 0, -s))
        sent = {s: permute(own, lambda z, a, g: (z, turned(a, s, wide), g)) for s in order}
        near = [sent[s] for s in order]
        middle = along(own, length - 1) if half < length else None
        first = [along(own, s) for s in range(1, half)]
        near = lax.optimization_barrier(near)
        near = [near[order.index(s)] for s in range(1, wide)]
        middle, first = lax.optimization_barrier((middle, first))
        last = [along(middle, s) for s in range(1, half)] if half < length else []
        offsets = list(range(1, half))
        if half < length:
            first = first + [middle]
            offsets += [length - 1] + [(length - 1) ^ s for s in range(1, half)]
        far, far_rank = [], []
        for t in range(1, n_grp):
            for s in range(wide):
                block = near[s - 1] if s else own
                far.append(permute(block, lambda z, a, g: (z, a, turned(g, t, n_grp))))
                far_rank.append(rank(a=s, g=t))
        near = list(zip([own] + near, [rank(a=s) for s in range(wide)]))
        far = list(zip(far, far_rank))
        visit_rank = [rank(z=s) for s in offsets]
        first = list(zip(first, visit_rank))
        last = list(zip(last, visit_rank[len(first) :]))
        best = best_of(rows, near + far, n_grp, near[:1] + first, table, True)
        if last:
            best = best + best_of(rows, near + far, n_grp, last, table, False)
        found = [best[0]] + [along(b, -s) for b, s in zip(best[1:], offsets)]
        return functools.reduce(jnp.maximum, found).reshape(rows)

    placed = (P(("clu", "grp"), None), P(("clu", "grp")), P())
    return jax.shard_map(
        shards, mesh=mesh, in_specs=placed, out_specs=P(("clu", "grp")), check_vma=False
    )
```

```python
import functools
import math

import jax
import jax.numpy as jnp
from jax import lax
from jax.experimental import pallas as pl
from jax.experimental.pallas import tpu as pltpu
from jax.sharding import PartitionSpec as P

LANES = 128
AUX = 8
DIGIT = 256


def pack_kernel(groups, emb_ref, id_ref, group_ref, out_ref, table_ref):
    rows, width = emb_ref.shape
    values = emb_ref[...].astype(jnp.float32)
    scale = lax.rsqrt(jnp.sum(values * values, axis=-1, keepdims=True) + 1e-06)
    unit = (values * scale).astype(jnp.bfloat16)
    for panel in range(width // LANES):
        out_ref[panel * rows : (panel + 1) * rows, :] = unit[:, panel * LANES : (panel + 1) * LANES]
    ids = jnp.broadcast_to(id_ref[...], (AUX, rows))
    row = lax.broadcasted_iota(jnp.int32, (AUX, rows), 0)
    digits = jnp.where(row == 0, ids % DIGIT, ids // DIGIT)
    if LANES > rows:
        digits = jnp.concatenate([digits, jnp.zeros((AUX, LANES - rows), jnp.int32)], axis=1)
    out_ref[width // LANES * rows :, :] = digits.astype(jnp.float32).astype(jnp.bfloat16)
    clusters = group_ref.shape[1]
    index = lax.broadcasted_iota(jnp.int32, (groups, clusters), 0)
    member = jnp.where(index == group_ref[...], 1.0, 0.0).astype(jnp.bfloat16)
    same = lax.dot_general(member, member, (((0,), (0,)), ((), ())), preferred_element_type=jnp.float32)
    one = lax.broadcasted_iota(jnp.int32, (clusters, clusters), 0)
    other = lax.broadcasted_iota(jnp.int32, (clusters, clusters), 1)
    table_ref[...] = jnp.where(one == other, 1.0, 0.5 * same).astype(jnp.bfloat16)


def pack(embeddings, cluster_id, cluster_group, groups):
    rows, width = embeddings.shape
    assert rows <= LANES and width % LANES == 0
    clusters = cluster_group.shape[0]
    return pl.pallas_call(
        functools.partial(pack_kernel, groups),
        out_shape=[pltpu.VMEM((width // LANES * rows + AUX, LANES), jnp.bfloat16), pltpu.VMEM((clusters, clusters), jnp.bfloat16)],
    )(embeddings, cluster_id.reshape(1, rows), cluster_group.reshape(1, clusters))


def one_hot(digits, clusters):
    number = digits[0:1].astype(jnp.int32) + DIGIT * digits[1:2].astype(jnp.int32)
    index = lax.broadcasted_iota(jnp.int32, (clusters, digits.shape[1]), 0)
    return jnp.where(index == number, 1.0, 0.0).astype(jnp.bfloat16)


def best_kernel(rows, n_keys, n_spans, own, ranks, table_ref, *refs):
    n_queries = (len(refs) - n_keys) // 2
    keys, queries, outs = refs[:n_keys], refs[n_keys : n_keys + n_queries], refs[n_keys + n_queries :]
    panels = (keys[0].shape[0] - AUX) // rows
    clusters = table_ref.shape[0]
    clu, grp = lax.axis_index("clu"), lax.axis_index("grp")
    ranks = [rank(clu, grp) for rank in ranks]

    def hot(block):
        return one_hot(block[panels * rows :, :rows].astype(jnp.float32), clusters)

    def unit(block):
        return jnp.concatenate([block[p * rows : (p + 1) * rows, :] for p in range(panels)], axis=1)

    mixed = [
        jnp.dot(table_ref[...], hot(query), preferred_element_type=jnp.float32).astype(jnp.bfloat16)
        for query in queries
    ]

    def search(span, first):
        key_hot = jnp.concatenate([hot(keys[i]) for i in span], axis=1)
        key_rows = jnp.concatenate([unit(keys[i]) for i in span], axis=0)
        for j in range(n_queries):
            weight = lax.dot_general(
                key_hot, mixed[j], (((0,), (0,)), ((), ())), preferred_element_type=jnp.float32
            )
            sims = lax.dot_general(
                key_rows, unit(queries[j]), (((1,), (1,)), ((), ())), preferred_element_type=jnp.float32
            )
            score = jnp.where(weight > 0, weight * sims, -1.0)
            best = jnp.full((1, rows), -1.0, jnp.float32) if first else outs[j][...]
            for at, i in enumerate(span):
                part = score[at * rows : (at + 1) * rows, :]
                if own and i + j == 0:
                    k = lax.broadcasted_iota(jnp.int32, (rows, rows), 0)
                    q = lax.broadcasted_iota(jnp.int32, (rows, rows), 1)
                    found = jnp.max(jnp.where(k < q, part, -1.0), axis=0, keepdims=True)
                else:
                    found = jnp.max(part, axis=0, keepdims=True)
                    found = jnp.where(ranks[i] < ranks[n_keys + j], found, -1.0)
                best = jnp.maximum(best, found)
            outs[j][...] = best

    width = n_keys // n_spans
    if own:
        search(range(width), True)
    else:
        for out in outs:
            out[...] = jnp.full((1, rows), -1.0, jnp.float32)

        @pl.when(functools.reduce(jnp.maximum, ranks[n_keys:]) > ranks[0])
        def _():
            search(range(width), False)

    for t in range(1, n_spans):
        @pl.when(ranks[t * width] < ranks[0])
        def _():
            search(range(t * width, (t + 1) * width), False)


def best_of(rows, keys, n_spans, queries, table, own):
    width = (keys[0][0].shape[0] - AUX) // rows * LANES
    vmem = pl.BlockSpec(memory_space=pltpu.VMEM)
    ranks = [r for _, r in keys + queries]
    pairs = len(keys) * len(queries) * rows * rows
    return pl.pallas_call(
        functools.partial(best_kernel, rows, len(keys), n_spans, own, ranks),
        out_shape=[jax.ShapeDtypeStruct((1, rows), jnp.float32)] * len(queries),
        in_specs=[vmem] * (1 + len(keys) + len(queries)),
        out_specs=[vmem] * len(queries),
        compiler_params=pltpu.CompilerParams(vmem_limit_bytes=40 * 2**20),
        cost_estimate=pl.CostEstimate(
            flops=2 * pairs * width, bytes_accessed=2 * (len(keys) + len(queries)) * rows * width, transcendentals=0
        ),
    )(table, *[b for b, _ in keys + queries])


def solution(mesh):
    n_clu, n_grp = mesh.shape["clu"], mesh.shape["grp"]
    target = math.sqrt(n_clu * n_grp)
    wide = min(a for a in range(1, n_clu + 1) if n_clu % a == 0 and (a * n_grp >= target or a == n_clu))
    length = n_clu // wide

    def permute(x, move):
        pairs = []
        for z in range(length):
            for a in range(wide):
                for g in range(n_grp):
                    at = move(z, a, g)
                    pairs.append(((at[0] * wide + at[1]) * n_grp + at[2], (z * wide + a) * n_grp + g))
        return lax.ppermute(x, ("clu", "grp"), pairs)

    def turned(a, s, n):
        return a ^ abs(s) if n & (n - 1) == 0 else (a + s) % n

    def shards(embeddings, cluster_id, cluster_group):
        rows = embeddings.shape[0]
        own, table = pack(embeddings, cluster_id, cluster_group, n_clu)

        def rank(z=0, a=0, g=0):
            def of(clu, grp):
                line, place = turned(clu // wide, z, length), turned(clu % wide, a, wide)
                return turned(grp, g, n_grp) * n_clu + line * wide + place

            return of

        def along(x, s):
            return permute(x, lambda z, a, g: (turned(z, s, length), a, g))

        half = length // 2 if length & (length - 1) == 0 else length
        near = [permute(own, lambda z, a, g: (z, turned(a, s, wide), g)) for s in range(1, wide)]
        middle = along(own, length - 1) if half < length else None
        first = [along(own, s) for s in range(1, half)]
        near = lax.optimization_barrier(near)
        middle, first = lax.optimization_barrier((middle, first))
        last = [along(middle, s) for s in range(1, half)] if half < length else []
        offsets = list(range(1, half))
        if half < length:
            first = first + [middle]
            offsets += [length - 1] + [(length - 1) ^ s for s in range(1, half)]
        far, far_rank = [], []
        for t in range(1, n_grp):
            for s in range(wide):
                block = near[s - 1] if s else own
                far.append(permute(block, lambda z, a, g: (z, a, turned(g, t, n_grp))))
                far_rank.append(rank(a=s, g=t))
        near = list(zip([own] + near, [rank(a=s) for s in range(wide)]))
        far = list(zip(far, far_rank))
        visit_rank = [rank(z=s) for s in offsets]
        first = list(zip(first, visit_rank))
        last = list(zip(last, visit_rank[len(first) :]))
        best = best_of(rows, near + far, n_grp, near[:1] + first, table, True)
        if last:
            best = best + best_of(rows, near + far, n_grp, last, table, False)
        found = [best[0]] + [along(b, -s) for b, s in zip(best[1:], offsets)]
        return functools.reduce(jnp.maximum, found).reshape(rows)

    placed = (P(("clu", "grp"), None), P(("clu", "grp")), P())
    return jax.shard_map(
        shards, mesh=mesh, in_specs=placed, out_specs=P(("clu", "grp")), check_vma=False
    )
```
